128 devices in a mesh: shard: 8 (over y_lo, z), ctx: 4 (over x), tp: 4 (over y_hi, core).
Axes of the slice: x: 4, y: 4 (y_hi: 2, y_lo: 2; y = y_hi * 2 + y_lo), z: 4, core: 2. Of those that a mesh axis runs over, the one named last changes fastest.
Arguments:
- tokens: bfloat16 [20480, 768], P(('shard', 'ctx', 'tp')), may hold values from -6 to 6
- parents: int32 [8, 20], P('shard'), may hold values from -1 to 19, as said below
- query_weight: bfloat16 [768, 768], P('shard', 'tp'), may hold values from -0.21875 to 0.21875
- query_bias: float32 [768], P('tp'), may hold values from -3 to 3
- key_weight: bfloat16 [768, 768], P('shard', 'tp'), may hold values from -0.21875 to 0.21875
- value_weight: bfloat16 [768, 768], P('shard', 'tp'), may hold values from -0.21875 to 0.21875
- value_bias: float32 [768], P('tp'), may hold values from -3 to 3
- output_weight: bfloat16 [768, 768], P('tp', 'shard'), may hold values from -2 to 2
- output_bias: float32 [768], replicated, may hold values from -3 to 3
- first_gain: float32 [768], replicated, may hold values from 0.1 to 1.9
- first_shift: float32 [768], replicated, may hold values from -3 to 3
- inner_weight: bfloat16 [768, 3072], P('shard', 'tp'), may hold values from -0.21875 to 0.21875
- inner_bias: float32 [3072], P('tp'), may hold values from -3 to 3
- outer_weight: bfloat16 [3072, 768], P('tp', 'shard'), may hold values from -0.109375 to 0.109375
- outer_bias: float32 [768], replicated, may hold values from -3 to 3
- second_gain: float32 [768], replicated, may hold values from 0.1 to 1.9
- second_shift: float32 [768], replicated, may hold values from -3 to 3
- mask_logits: float32 [12, 512, 512], P('tp', 'shard'), may hold values from -6 to 6
- mask_noise: float32 [12, 512, 512], P('tp', 'shard'), may hold values from -5 to 5
- cotangent: bfloat16 [20480, 768], P(('shard', 'ctx', 'tp')), may hold values from -6 to 6
Outputs:
- result: bfloat16 [20480, 768], P(('shard', 'ctx', 'tp'))
- tokens_grad: float32 [20480, 768], P(('shard', 'ctx', 'tp'))
- query_weight_grad: float32 [768, 768], P('shard', 'tp')
- query_bias_grad: float32 [768], P('tp')
- key_weight_grad: float32 [768, 768], P('shard', 'tp')
- value_weight_grad: float32 [768, 768], P('shard', 'tp')
- value_bias_grad: float32 [768], P('tp')
- output_weight_grad: float32 [768, 768], P('tp', 'shard')
- output_bias_grad: float32 [768], replicated
- first_gain_grad: float32 [768], replicated
- first_shift_grad: float32 [768], replicated
- inner_weight_grad: float32 [768, 3072], P('shard', 'tp')
- inner_bias_grad: float32 [3072], P('tp')
- outer_weight_grad: float32 [3072, 768], P('tp', 'shard')
- outer_bias_grad: float32 [768], replicated
- second_gain_grad: float32 [768], replicated
- second_shift_grad: float32 [768], replicated
- mask_logits_grad: float32 [12, 512, 512], P('tp', 'shard')
The draws below stay inside these ranges and needn't reach their ends.
Inputs may be any that keep to these rules, and one draw needn't show every extreme that they name: `parents`: each group's 20 segments form 1 trees: a chain of 8 trunk segments, 4 branch segments whose parent is the trunk's last, and 2 leaf segments under each branch. Writing L = 20 // 4, tree t holds, for every c, the L segments c * 20 // 4 + t * L to c * 20 // 4 + (t + 1) * L - 1.
All inputs are finite; a program needn't handle non-finite values.
Results may differ from the reference program's by a relative error of at most 0.023.
Values may be sent and summed in bfloat16 or wider, within the bound.
A program may use at most 192 MiB of HBM per device.

```python
import jax
import jax.numpy as jnp
import numpy as np
from jax import lax

D = 768
HEADS = 12
HEAD_DIM = 64
FF = 3072
DEPTHS = 512
SEG_LEN = 128
TRUNK_SEGS = 8
BRANCHES = 4
LEAVES_PER = 2
TREES_DEV = 1
TREE_SEGS = 20
TREE_TOK = 2560
SEGS = 20
GROUP_TOK = 2560
GROUPS = 8
TOKENS = 20480
N_CTX = 4


def draw_parents(key, part):
    per_device = TREE_SEGS // N_CTX
    local_slots = SEGS // N_CTX
    role_parent = np.zeros(TREE_SEGS, dtype=np.int32)
    for role_index in range(TREE_SEGS):
        if role_index < TRUNK_SEGS:
            role_parent[role_index] = role_index - 1
        elif role_index < TRUNK_SEGS + BRANCHES:
            role_parent[role_index] = TRUNK_SEGS - 1
        else:
            role_parent[role_index] = TRUNK_SEGS + (role_index - TRUNK_SEGS - BRANCHES) // LEAVES_PER
    has_parent = jnp.asarray(role_parent >= 0)
    parent_role = jnp.asarray(np.maximum(role_parent, 0))
    rows_out = []
    for group_index in range(GROUPS):
        group_key = jax.random.fold_in(key, 11 + group_index)
        device_rows = []
        for device in range(N_CTX):
            tree_rows = []
            for tree_index in range(TREES_DEV):
                order = jax.random.permutation(jax.random.fold_in(group_key, 101 + device * 977 + tree_index), per_device).astype(jnp.int32)
                tree_rows.append(order + device * local_slots + tree_index * per_device)
            device_rows.append(jnp.stack(tree_rows))
        device_slots = jnp.stack(device_rows)
        tree_slots = device_slots.transpose(1, 0, 2).reshape(TREES_DEV, TREE_SEGS)
        role_orders = jnp.stack([jax.random.permutation(jax.random.fold_in(group_key, 9001 + tree_index), TREE_SEGS).astype(jnp.int32) for tree_index in range(TREES_DEV)])
        slot_of_role = jnp.take_along_axis(tree_slots, role_orders, axis=1)
        parent_slot = jnp.where(has_parent[None, :], slot_of_role[:, parent_role], -1).astype(jnp.int32)
        parent_row = jnp.zeros((SEGS,), jnp.int32).at[slot_of_role.reshape(-1)].set(parent_slot.reshape(-1))
        rows_out.append(parent_row)
    return jnp.stack(rows_out)


def shard_levels(own_key, extent, pieces, smallest, largest):
    factor_of, own = 1.0, jax.random.fold_in(own_key, 6)
    for axis_at, parts in pieces:
        steps = jnp.exp(jax.random.uniform(jax.random.fold_in(own, axis_at), (parts,), jnp.float32, smallest / len(pieces), largest / len(pieces)))
        factor_of = factor_of * jnp.repeat(steps, extent[axis_at] // parts).reshape([-1 if axis == axis_at else 1 for axis in range(len(extent))])
    return factor_of


def scatter_about(key, dims, scale, most, cuts=(), held_as=jnp.bfloat16):
    values = scale * jax.random.normal(key, dims, jnp.float32)
    if cuts:
        values = values * shard_levels(key, dims, cuts, -0.22, 0.18)
    return jnp.clip(values, -most, most).astype(held_as)


def setup_inputs(seed: int = 0) -> dict:
    seeds = jax.random.split(jax.random.key(seed), 21)
    return {
        "tokens": scatter_about(seeds[0], (TOKENS, D), 1.0, 6.0, ((0, 128),)),
        "parents": draw_parents(jax.random.fold_in(seeds[20], 71), 0),
        "query_weight": scatter_about(seeds[2], (D, D), D ** -0.5, 0.21875, ((0, 8), (1, 4))),
        "query_bias": scatter_about(seeds[3], (D,), 0.5, 3.0, ((0, 4),), jnp.float32),
        "key_weight": scatter_about(seeds[4], (D, D), D ** -0.5, 0.21875, ((0, 8), (1, 4))),
        "value_weight": scatter_about(seeds[5], (D, D), D ** -0.5, 0.21875, ((0, 8), (1, 4))),
        "value_bias": scatter_about(seeds[6], (D,), 0.5, 3.0, ((0, 4),), jnp.float32),
        "output_weight": scatter_about(seeds[7], (D, D), 8 ** -0.5, 2.0, ((0, 4), (1, 8))),
        "output_bias": scatter_about(seeds[8], (D,), 0.5, 3.0, (), jnp.float32),
        "first_gain": jnp.clip(1.0 + 0.18 * jax.random.normal(seeds[9], (D,), jnp.float32), 0.1, 1.9),
        "first_shift": scatter_about(seeds[10], (D,), 0.5, 3.0, (), jnp.float32),
        "inner_weight": scatter_about(seeds[11], (D, FF), D ** -0.5, 0.21875, ((0, 8), (1, 4))),
        "inner_bias": scatter_about(seeds[12], (FF,), 0.5, 3.0, ((0, 4),), jnp.float32),
        "outer_weight": scatter_about(seeds[13], (FF, D), FF ** -0.5, 0.109375, ((0, 4), (1, 8))),
        "outer_bias": scatter_about(seeds[14], (D,), 0.5, 3.0, (), jnp.float32),
        "second_gain": jnp.clip(1.0 + 0.18 * jax.random.normal(seeds[15], (D,), jnp.float32), 0.1, 1.9),
        "second_shift": scatter_about(seeds[16], (D,), 0.5, 3.0, (), jnp.float32),
        "mask_logits": scatter_about(seeds[17], (HEADS, DEPTHS, DEPTHS), 1.5, 6.0, ((0, 4), (1, 8)), jnp.float32),
        "mask_noise": scatter_about(seeds[18], (HEADS, DEPTHS, DEPTHS), 1.0, 5.0, ((0, 4), (1, 8)), jnp.float32),
        "cotangent": scatter_about(seeds[19], (TOKENS, D), 1.0, 6.0, ((0, 128),)),
    }


@jax.custom_vjp
def low(v):
    return lax.optimization_barrier(v.astype(jnp.bfloat16)).astype(jnp.float32)

@jax.custom_vjp
def low_back(v):
    return v

def low_keep(v):
    return (low(v), None)

def low_pass(kept, grad):
    return (grad,)

def back_keep(v):
    return (v, None)

def back_low(kept, grad):
    return (low(grad),)
low.defvjp(low_keep, low_pass)
low_back.defvjp(back_keep, back_low)

def mult(left, right):
    return jnp.dot(left, right, precision=lax.Precision.HIGHEST)

def layer_norm(values, gain_vector, shift_vector):
    centre = lax.optimization_barrier(jnp.mean(values, axis=-1, keepdims=True))
    spread = lax.optimization_barrier(jnp.mean(jnp.square(values - centre), axis=-1, keepdims=True))
    return (values - centre) * lax.rsqrt(spread + 1e-05) * gain_vector + shift_vector

def tree_tables(parent_row):
    segment_count = parent_row.shape[0]
    segment_ids = jnp.arange(segment_count, dtype=jnp.int32)
    current = segment_ids
    reachable = current[:, None] == segment_ids[None, :]
    strict = jnp.zeros((segment_count,), jnp.int32)
    for climb in range(segment_count):
        safe_index = jnp.maximum(current, 0).astype(jnp.int32)
        upper = jnp.where(current >= 0, jnp.take(parent_row, safe_index), -1).astype(jnp.int32)
        reachable = reachable | (upper[:, None] == segment_ids[None, :])
        strict = strict + (upper >= 0).astype(jnp.int32)
        current = upper
    positions = jnp.arange(segment_count * SEG_LEN, dtype=jnp.int32)
    token_depth = strict[positions // SEG_LEN] * SEG_LEN + positions % SEG_LEN
    return (reachable, (token_depth % DEPTHS).astype(jnp.int32))

def reference(tokens, parents, query_weight, query_bias, key_weight, value_weight, value_bias, output_weight, output_bias, first_gain, first_shift, inner_weight, inner_bias, outer_weight, outer_bias, second_gain, second_shift, mask_logits, mask_noise, cotangent):
    block_rows = TREE_TOK // N_CTX
    block_count = GROUP_TOK // block_rows
    score_scale = HEAD_DIM ** (-0.5)
    tables = [tree_tables(parents[group_index]) for group_index in range(GROUPS)]
    reach_all = jnp.stack([entry[0] for entry in tables])
    depth_all = jnp.stack([entry[1] for entry in tables])
    key_segment = jnp.arange(GROUP_TOK, dtype=jnp.int32) // SEG_LEN
    segment_blocks = key_segment.reshape(block_count, block_rows)
    tree_of_block = (jnp.arange(block_count, dtype=jnp.int32) % TREES_DEV).astype(jnp.int32)
    key_segment_trees = key_segment.reshape(N_CTX, TREES_DEV, block_rows)

    def forward(token_input, query_matrix, query_shift, key_matrix, value_matrix, value_shift, output_matrix, output_shift, first_scale, first_offset, inner_matrix, inner_shift, outer_matrix, outer_shift, second_scale, second_offset, mask_table):
        relaxed = low(jax.nn.log_sigmoid(mask_table + mask_noise)).reshape(HEADS, DEPTHS * DEPTHS)
        query_all = low_back(low(mult(token_input, query_matrix) + query_shift)).reshape(GROUPS, GROUP_TOK, HEADS, HEAD_DIM)
        key_all = low_back(low(mult(token_input, key_matrix))).reshape(GROUPS, GROUP_TOK, HEADS, HEAD_DIM)
        value_all = low_back(low(mult(token_input, value_matrix) + value_shift)).reshape(GROUPS, GROUP_TOK, HEADS, HEAD_DIM)

        def group_attention(inputs):
            query_group, key_group, value_group, reachable, token_depth = inputs
            key_trees = key_group.reshape(N_CTX, TREES_DEV, block_rows, HEADS, HEAD_DIM)
            value_trees = value_group.reshape(N_CTX, TREES_DEV, block_rows, HEADS, HEAD_DIM)
            depth_trees = token_depth.reshape(N_CTX, TREES_DEV, block_rows)

            def one_block(block_inputs):
                query_block, segment_block, depth_block, tree_index = block_inputs
                key_block = jnp.take(key_trees, tree_index, axis=1).reshape(N_CTX * block_rows, HEADS, HEAD_DIM)
                value_block = jnp.take(value_trees, tree_index, axis=1).reshape(N_CTX * block_rows, HEADS, HEAD_DIM)
                key_seg_block = jnp.take(key_segment_trees, tree_index, axis=1).reshape(N_CTX * block_rows).astype(jnp.int32)
                key_depth_block = jnp.take(depth_trees, tree_index, axis=1).reshape(N_CTX * block_rows).astype(jnp.int32)
                plain_scores = jnp.einsum('qhd,khd->hqk', query_block, key_block, precision=lax.Precision.HIGHEST) * score_scale
                table_index = depth_block[:, None] * DEPTHS + key_depth_block[None, :]
                mask_bias = jnp.take(relaxed, table_index, axis=1)
                scores = low_back(plain_scores + mask_bias)
                allowed = reachable[segment_block][:, key_seg_block]
                scores = jnp.where(allowed[None], scores, -1e+30)
                soft_low = low(jax.nn.softmax(scores, axis=-1))
                return jnp.einsum('hqk,khd->qhd', soft_low, value_block, precision=lax.Precision.HIGHEST)
            attended_blocks = lax.map(jax.checkpoint(one_block), (query_group.reshape(block_count, block_rows, HEADS, HEAD_DIM), segment_blocks, token_depth.reshape(block_count, block_rows), tree_of_block))
            return attended_blocks.reshape(GROUP_TOK, D)
        attended = lax.map(group_attention, (query_all, key_all, value_all, reach_all, depth_all)).reshape(TOKENS, D)
        attended = low_back(low(attended))
        attn_output = low_back(mult(attended, output_matrix) + output_shift)
        first_out = layer_norm(token_input + attn_output, first_scale, first_offset)
        inner_pre = low_back(mult(low(first_out), inner_matrix) + inner_shift)
        activated = low(jax.nn.gelu(inner_pre, approximate=False))
        outer_out = low_back(mult(activated, outer_matrix) + outer_shift)
        return layer_norm(first_out + outer_out, second_scale, second_offset)
    result_full, backward = jax.vjp(forward, tokens.astype(jnp.float32), query_weight.astype(jnp.float32), query_bias, key_weight.astype(jnp.float32), value_weight.astype(jnp.float32), value_bias, output_weight.astype(jnp.float32), output_bias, first_gain, first_shift, inner_weight.astype(jnp.float32), inner_bias, outer_weight.astype(jnp.float32), outer_bias, second_gain, second_shift, mask_logits)
    grads = backward(cotangent.astype(jnp.float32))
    return (result_full.astype(jnp.bfloat16), grads[0], grads[1], grads[2], grads[3], grads[4], grads[5], grads[6], grads[7], grads[8], grads[9], grads[10], grads[11], grads[12], grads[13], grads[14], grads[15], grads[16])
```

```python
import jax
import jax.numpy as jnp
from jax import lax
from jax.experimental import pallas as pl
from jax.experimental.pallas import tpu as pltpu
from jax.sharding import PartitionSpec as P

MESH = pl.DeviceIdType.MESH
BF = jnp.bfloat16
F32 = jnp.float32
HEADS_DEV = 3
HEAD_DIM = 64
WIDE = 128
SEG = 128
SEGS = 20
PATH = 10
KEYS = PATH * SEG
D = 768
QK = 192
QKW = 384
ROWS = 160
CTX_ROWS = 640
TREE = 2560
DEPTHS = 512
MIB = 2**20
VM = pl.BlockSpec(memory_space=pltpu.VMEM)
SM = pl.BlockSpec(memory_space=pltpu.SMEM)


def place():
    shard = lax.axis_index("shard")
    tp = lax.axis_index("tp")
    return {
        "x": lax.axis_index("ctx"),
        "yl": lax.div(shard, 4),
        "z": lax.rem(shard, 4),
        "yh": lax.div(tp, 2),
        "core": lax.rem(tp, 2),
    }


def ident(at, **moved):
    to = {**at, **moved}
    return {"shard": to["yl"] * 4 + to["z"], "ctx": to["x"], "tp": to["yh"] * 2 + to["core"]}


def around(value, step):
    return lax.rem(value + step, 4)


def greet(devices):
    barrier = pltpu.get_barrier_semaphore()
    for device in devices:
        pl.semaphore_signal(barrier, inc=1, device_id=device, device_id_type=MESH)
    pl.semaphore_wait(barrier, len(devices))


class Mail:
    def __init__(self, send, recv):
        self.send, self.recv, self.used, self.sent = send, recv, 0, []

    def post(self, src, dst, device):
        copy = pltpu.make_async_remote_copy(
            src_ref=src,
            dst_ref=dst,
            send_sem=self.send.at[self.used],
            recv_sem=self.recv.at[self.used],
            device_id=device,
            device_id_type=MESH,
        )
        self.used += 1
        copy.start()
        self.sent.append(copy)
        return copy

    def close(self):
        for copy in self.sent:
            copy.wait_send()


def nn(a, b):
    return jnp.dot(a, b, preferred_element_type=F32)


def nt(a, b):
    return lax.dot_general(a, b, (((1,), (1,)), ((), ())), preferred_element_type=F32)


def spread(kind=BF):
    rows = lax.broadcasted_iota(jnp.int32, (QK, QKW), 0)
    cols = lax.broadcasted_iota(jnp.int32, (QK, QKW), 1)
    head, lane = cols // WIDE, cols % WIDE
    return ((head * HEAD_DIM + lane == rows) & (lane < HEAD_DIM)).astype(kind)


def project_kernel(
    tok,
    wq,
    wk,
    wv,
    qb,
    vb,
    logits,
    noise,
    q_out,
    k_out,
    v_out,
    rows_out,
    tab,
    xs,
    ws,
    wide,
    send,
    recv,
):
    at = place()
    x, yl, z, yh, core = at["x"], at["yl"], at["z"], at["yh"], at["core"]
    shard, tp = yl * 4 + z, yh * 2 + core
    sib = ident(at, core=1 - core)
    far = ident(at, yh=1 - yh)
    low = ident(at, yl=1 - yl)
    zs = [ident(at, z=around(z, k)) for k in (1, 2, 3)]
    xp = [ident(at, x=around(x, k)) for k in (1, 2, 3)]
    xs[x, tp] = tok[...]
    for j, w in enumerate((wq, wk, wv)):
        ws[shard, j] = w[...]
    masks = logits[...] + noise[...]
    tab[:, shard] = jax.nn.log_sigmoid(masks).astype(BF)
    greet([sib, far, low, *zs, *xp])
    mail = Mail(send, recv)

    def block(kx, other):
        return xs.at[around(x, 4 - kx), (1 - yh if other else yh) * 2 + core]

    def pass_on(src, device):
        return mail.post(src, src, device)

    first_far = pass_on(block(0, False), far)
    own_low = [pass_on(ws.at[shard], low), pass_on(tab.at[0, shard], low)]
    own_x = [pass_on(block(0, False), d) for d in xp]
    own_z = [pass_on(ws.at[shard], d) for d in zs]
    own_z0 = [pass_on(tab.at[0, shard], d) for d in zs]
    own_z1 = [pass_on(tab.at[pl.ds(1, 2), shard], d) for d in zs]
    to_low = [pass_on(tab.at[pl.ds(1, 2), shard], low)]
    to_sib = [pass_on(block(0, False), sib)]
    first_far.wait_recv()
    far_x = [pass_on(block(0, True), d) for d in xp]
    to_sib.append(pass_on(block(0, True), sib))
    for copy in own_low:
        copy.wait_recv()
    mate = (1 - yl) * 4 + z
    low_z = [pass_on(ws.at[mate], d) for d in zs]
    low_z0 = [pass_on(tab.at[0, mate], d) for d in zs]
    for k in (1, 3, 2):
        own_x[k - 1].wait_recv()
        to_sib.append(pass_on(block(k, False), sib))
    for k in (1, 3, 2):
        own_z1[k - 1].wait_recv()
        to_low.append(pass_on(tab.at[pl.ds(1, 2), yl * 4 + around(z, 4 - k)], low))
    for k in (1, 3, 2):
        far_x[k - 1].wait_recv()
        to_sib.append(pass_on(block(k, True), sib))
    for copy in own_z + own_z0 + low_z + to_sib:
        copy.wait_recv()

    hots = spread()
    hots32 = spread(F32)
    for j in range(3):
        whole = ws[:, j].reshape(D, QK)
        wide[:, j * QKW : (j + 1) * QKW] = nn(whole, hots).astype(BF)
    q_add = jnp.dot(qb[...], hots32, precision=lax.Precision.HIGHEST)
    v_add = jnp.dot(vb[...], hots32, precision=lax.Precision.HIGHEST)

    @pl.loop(0, 16)
    def _(i):
        rows = xs[lax.div(i, 4), lax.rem(i, 4)]
        both = nn(rows, wide[:, QKW:])
        k_out[pl.ds(i * ROWS, ROWS), :] = both[:, :QKW].astype(BF)
        v_out[pl.ds(i * ROWS, ROWS), :] = (both[:, QKW:] + v_add).astype(BF)

    @pl.loop(0, 4)
    def _(i):
        rows = xs[x, i]
        rows_out[pl.ds(i * ROWS, ROWS), :] = rows
        q_out[pl.ds(i * ROWS, ROWS), :] = (nn(rows, wide[:, :QKW]) + q_add).astype(BF)

    for copy in low_z0 + to_low:
        copy.wait_recv()
    mail.close()


def project(tokens, wq, wk, wv, qb, vb, logits, noise):
    shape = jax.ShapeDtypeStruct
    posts = 2 + 1 + 3 + 9 + 1 + 8 + 3 + 6 + 3
    return pl.pallas_call(
        project_kernel,
        out_shape=(
            shape((CTX_ROWS, QKW), BF),
            shape((TREE, QKW), BF),
            shape((TREE, QKW), BF),
            shape((CTX_ROWS, D), BF),
            shape((HEADS_DEV, 8, 64, DEPTHS), BF),
        ),
        in_specs=[VM] * 8,
        out_specs=[VM] * 5,
        scratch_shapes=[
            pltpu.VMEM((4, 4, ROWS, D), BF),
            pltpu.VMEM((8, 3, 96, QK), BF),
            pltpu.VMEM((D, 3 * QKW), BF),
            pltpu.SemaphoreType.DMA((posts,)),
            pltpu.SemaphoreType.DMA((posts,)),
        ],
        compiler_params=pltpu.CompilerParams(
            collective_id=1, has_side_effects=True, vmem_limit_bytes=56 * MIB
        ),
        name="project",
    )(tokens, wq, wk, wv, qb.reshape(1, QK), vb.reshape(1, QK), logits, noise)


def climb(parents, seg, trail):
    trail[0] = seg
    depth = jnp.int32(0)
    here = seg
    for i in range(1, PATH):
        up = parents[0, here]
        found = up >= 0
        here = jnp.where(found, up, here)
        trail[i] = here
        depth = depth + found.astype(jnp.int32)
    return depth


def on_path(trail, depth, j):
    return trail[jnp.maximum(depth - j, 0)]


def attend_kernel(parents, q, k, v, tab, o_out, p_out, trail, kp, vp):
    a = pl.program_id(0)
    seg = lax.axis_index("ctx") * 5 + a
    depth = climb(parents, seg, trail)
    for j in range(PATH):
        rows = pl.ds(pl.multiple_of(on_path(trail, depth, j) * SEG, SEG), SEG)
        kp[pl.ds(j * SEG, SEG), :] = k[rows, :]
        vp[pl.ds(j * SEG, SEG), :] = v[rows, :]
    tile = pl.ds(pl.multiple_of(lax.rem(depth, 4) * SEG, SEG), SEG)
    outs = []
    for h in range(HEADS_DEV):
        head = slice(h * WIDE, (h + 1) * WIDE)
        mine = q[:, head] * jnp.asarray(HEAD_DIM**-0.5, BF)
        bias = tab[h, tile, :].astype(F32)
        scores = nt(mine, kp[:, head])
        parts = []
        for j in range(PATH):
            cols = slice((j % 4) * SEG, (j % 4 + 1) * SEG)
            part = scores[:, j * SEG : (j + 1) * SEG] + bias[:, cols]
            parts.append(jnp.where(j <= depth, part, -1e30))
        scores = jnp.concatenate(parts, axis=1)
        peak = jnp.max(scores, axis=1, keepdims=True)
        raised = jnp.exp(scores - peak)
        total = jnp.sum(raised, axis=1, keepdims=True)
        soft = (raised * (1.0 / total)).astype(BF)
        p_out[0, h] = soft
        outs.append(nn(soft, vp[:, head]).astype(BF))
    o_out[...] = nt(jnp.concatenate(outs, axis=1), spread()).astype(BF)


def whole(shape):
    return pl.BlockSpec(shape, lambda a: (0,) * len(shape))


def attend(parents, q, k, v, tab):
    shape = jax.ShapeDtypeStruct
    return pl.pallas_call(
        attend_kernel,
        grid=(5,),
        out_shape=(
            shape((CTX_ROWS, QK), BF),
            shape((5, HEADS_DEV, SEG, KEYS), BF),
        ),
        in_specs=[
            SM,
            pl.BlockSpec((SEG, QKW), lambda a: (a, 0)),
            whole((TREE, QKW)),
            whole((TREE, QKW)),
            whole((HEADS_DEV, DEPTHS, DEPTHS)),
        ],
        out_specs=(
            pl.BlockSpec((SEG, QK), lambda a: (a, 0)),
            pl.BlockSpec((1, HEADS_DEV, SEG, KEYS), lambda a: (a, 0, 0, 0)),
        ),
        scratch_shapes=[
            pltpu.SMEM((PATH,), jnp.int32),
            pltpu.VMEM((KEYS, QKW), BF),
            pltpu.VMEM((KEYS, QKW), BF),
        ],
        compiler_params=pltpu.CompilerParams(vmem_limit_bytes=56 * MIB),
        cost_estimate=pl.CostEstimate(
            flops=2 * 2 * 15 * SEG * KEYS * WIDE, bytes_accessed=12 * MIB, transcendentals=15 * SEG * KEYS
        ),
        name="attend",
    )(parents, q, k, v, tab)


def attend_back_kernel(
    parents, q, k, v, o, g, p, dq_out, dk_out, dv_out, tab_out, trail, kp, vp, dk, dv, dtab
):
    a = pl.program_id(0)
    seg = lax.axis_index("ctx") * 5 + a

    @pl.when(a == 0)
    def _():
        dk[...] = jnp.zeros_like(dk)
        dv[...] = jnp.zeros_like(dv)
        dtab[...] = jnp.zeros_like(dtab)

    depth = climb(parents, seg, trail)
    starts = [pl.multiple_of(on_path(trail, depth, j) * SEG, SEG) for j in range(PATH)]
    for j in range(PATH):
        kp[pl.ds(j * SEG, SEG), :] = k[pl.ds(starts[j], SEG), :]
        vp[pl.ds(j * SEG, SEG), :] = v[pl.ds(starts[j], SEG), :]
    tile = pl.ds(pl.multiple_of(lax.rem(depth, 4) * SEG, SEG), SEG)
    hots = spread()
    g_wide = nn(g[...], hots).astype(BF)
    o_wide = nn(o[...], hots)
    scale = HEAD_DIM**-0.5
    outs = []
    for h in range(HEADS_DEV):
        head = slice(h * WIDE, (h + 1) * WIDE)
        mine, grad = q[:, head], g_wide[:, head]
        soft = p[0, h]
        inner = jnp.sum(grad.astype(F32) * o_wide[:, head], axis=1, keepdims=True)
        ds = soft.astype(F32) * (nt(grad, vp[:, head]) - inner)
        low = ds.astype(BF)
        outs.append((nn(low, kp[:, head]) * scale).astype(BF))
        mine_t = (mine.astype(F32).T[:HEAD_DIM] * scale).astype(BF)
        grad_t = grad.astype(F32).T[:HEAD_DIM].astype(BF)
        dk_part = nn(mine_t, low)
        dv_part = nn(grad_t, soft)
        for j in range(PATH):
            cols = slice(j * SEG, (j + 1) * SEG)
            dk[h, :, pl.ds(starts[j], SEG)] += dk_part[:, cols]
            dv[h, :, pl.ds(starts[j], SEG)] += dv_part[:, cols]
        down = low.astype(F32)
        dtab[h, tile, 0:256] += down[:, 0:256] + down[:, 512:768] + down[:, 1024:1280]
        dtab[h, tile, 256:512] += down[:, 256:512] + down[:, 768:1024]
    dq_out[...] = nt(jnp.concatenate(outs, axis=1), hots).astype(BF)

    @pl.when(a == 4)
    def _():
        for h in range(HEADS_DEV):
            dk_out[pl.ds(h * HEAD_DIM, HEAD_DIM), :] = dk[h].astype(BF)
            dv_out[pl.ds(h * HEAD_DIM, HEAD_DIM), :] = dv[h].astype(BF)
            tab_out[h] = dtab[h].astype(BF)


def attend_back(parents, q, k, v, o, g, p):
    shape = jax.ShapeDtypeStruct
    return pl.pallas_call(
        attend_back_kernel,
        grid=(5,),
        out_shape=(
            shape((CTX_ROWS, QK), BF),
            shape((QK, TREE), BF),
            shape((QK, TREE), BF),
            shape((HEADS_DEV, DEPTHS, DEPTHS), BF),
        ),
        in_specs=[
            SM,
            pl.BlockSpec((SEG, QKW), lambda a: (a, 0)),
            whole((TREE, QKW)),
            whole((TREE, QKW)),
            pl.BlockSpec((SEG, QK), lambda a: (a, 0)),
            pl.BlockSpec((SEG, QK), lambda a: (a, 0)),
            pl.BlockSpec((1, HEADS_DEV, SEG, KEYS), lambda a: (a, 0, 0, 0)),
        ],
        out_specs=(
            pl.BlockSpec((SEG, QK), lambda a: (a, 0)),
            whole((QK, TREE)),
            whole((QK, TREE)),
            whole((HEADS_DEV, DEPTHS, DEPTHS)),
        ),
        scratch_shapes=[
            pltpu.SMEM((PATH,), jnp.int32),
            pltpu.VMEM((KEYS, QKW), BF),
            pltpu.VMEM((KEYS, QKW), BF),
            pltpu.VMEM((HEADS_DEV, HEAD_DIM, TREE), F32),
            pltpu.VMEM((HEADS_DEV, HEAD_DIM, TREE), F32),
            pltpu.VMEM((HEADS_DEV, DEPTHS, DEPTHS), F32),
        ],
        compiler_params=pltpu.CompilerParams(vmem_limit_bytes=56 * MIB),
        cost_estimate=pl.CostEstimate(
            flops=5 * 2 * 15 * SEG * KEYS * WIDE, bytes_accessed=20 * MIB, transcendentals=0
        ),
        name="attend_back",
    )(parents, q, k, v, o, g, p)


def layer_norm(values, gain_vector, shift_vector):
    centre = jnp.mean(values, axis=-1, keepdims=True)
    spread = jnp.mean(jnp.square(values - centre), axis=-1, keepdims=True)
    return (values - centre) * lax.rsqrt(spread + 1e-05) * gain_vector + shift_vector


def gelu_exact(values):
    return jax.nn.gelu(values, approximate=False)


def tree_tables(parent_row):
    segment_count = parent_row.shape[0]
    segment_ids = jnp.arange(segment_count, dtype=jnp.int32)
    current = segment_ids
    reachable = current[:, None] == segment_ids[None, :]
    strict = jnp.zeros((segment_count,), jnp.int32)
    for climb in range(segment_count):
        safe_index = jnp.maximum(current, 0)
        upper = jnp.where(current >= 0, jnp.take(parent_row, safe_index), -1)
        reachable = reachable | (upper[:, None] == segment_ids[None, :])
        strict = strict + (upper >= 0).astype(jnp.int32)
        current = upper
    segment_tile = strict * SEG_LEN % DEPTHS // SEG_LEN
    return (reachable, segment_tile)


def gather_rows(values):
    return lax.all_gather(values, "tp", axis=0, tiled=True)


def sum_rows(values):
    return lax.psum_scatter(values, "tp", scatter_dimension=0, tiled=True)


def block_scores(query_heads, key_heads, tiles, reach_pair, query_hot, key_hot):
    heads_local = tiles.shape[0]
    query_segs = query_hot.shape[0]
    key_segs = key_hot.shape[0]
    plain_scores = jnp.einsum(
        "qhd,khd->hqk", query_heads, key_heads, preferred_element_type=jnp.float32
    ) * HEAD_DIM ** (-0.5)
    partial_bias = jnp.einsum(
        "hxpyq,by->hxpbq", tiles, key_hot, preferred_element_type=jnp.float32
    ).astype(jnp.bfloat16)
    mask_bias = jnp.einsum(
        "ax,hxpbq->hapbq", query_hot, partial_bias, preferred_element_type=jnp.float32
    )
    scores = plain_scores.reshape(heads_local, query_segs, SEG_LEN, key_segs, SEG_LEN) + mask_bias
    scores = jnp.where(reach_pair[None, :, None, :, None], scores, -1e30)
    return scores.reshape(heads_local, query_segs * SEG_LEN, key_segs * SEG_LEN)


def attend_forward(
    queries, key_trees, value_trees, tiles, reach_blocks, query_hots, key_hots, block_rows
):
    heads_local = tiles.shape[0]
    row_count, width = queries.shape
    head_size = width // heads_local
    trees = reach_blocks.shape[0]

    def one_block(inputs):
        query_block, key_block, value_block, reach_pair, query_hot, key_hot = inputs
        query_heads = query_block.reshape(block_rows, heads_local, head_size)
        key_heads = key_block.reshape(key_block.shape[0], heads_local, head_size)
        value_heads = value_block.reshape(value_block.shape[0], heads_local, head_size)
        scores = block_scores(query_heads, key_heads, tiles, reach_pair, query_hot, key_hot)
        row_peak = jnp.max(scores, axis=-1, keepdims=True)
        exponent = jnp.exp(scores - row_peak)
        row_total = jnp.sum(exponent, axis=-1, keepdims=True)
        soft_low = (exponent / row_total).astype(jnp.bfloat16)
        attended_block = jnp.einsum(
            "hqk,khd->qhd", soft_low, value_heads, preferred_element_type=jnp.float32
        )
        return (
            attended_block.reshape(block_rows, width).astype(jnp.bfloat16),
            row_peak[:, :, 0] + jnp.log(row_total[:, :, 0]),
        )

    attended, log_totals = lax.map(
        one_block,
        (
            queries.reshape(trees, block_rows, width),
            key_trees,
            value_trees,
            reach_blocks,
            query_hots,
            key_hots,
        ),
    )
    return (attended.reshape(row_count, width), log_totals)


def attend_backward(
    queries,
    key_trees,
    value_trees,
    tiles,
    reach_blocks,
    query_hots,
    key_hots,
    block_rows,
    log_totals,
    mixed_grad,
):
    heads_local = tiles.shape[0]
    row_count, width = queries.shape
    head_size = width // heads_local
    trees = reach_blocks.shape[0]
    score_scale = HEAD_DIM ** (-0.5)

    def one_block(table_acc, inputs):
        (
            query_block,
            grad_block,
            key_block,
            value_block,
            reach_pair,
            query_hot,
            key_hot,
            total_block,
        ) = inputs
        key_count = key_block.shape[0]
        query_heads = query_block.reshape(block_rows, heads_local, head_size)
        grad_heads = grad_block.reshape(block_rows, heads_local, head_size)
        key_heads = key_block.reshape(key_count, heads_local, head_size)
        value_heads = value_block.reshape(key_count, heads_local, head_size)
        scores = block_scores(query_heads, key_heads, tiles, reach_pair, query_hot, key_hot)
        soft = jnp.exp(scores - total_block[:, :, None])
        soft_low = soft.astype(jnp.bfloat16)
        soft_grad = jnp.einsum(
            "qhd,khd->hqk", grad_heads, value_heads, preferred_element_type=jnp.float32
        )
        value_grad = jnp.einsum(
            "hqk,qhd->khd", soft_low, grad_heads, preferred_element_type=jnp.float32
        ).reshape(key_count, width)
        score_grad = soft * (soft_grad - jnp.sum(soft * soft_grad, axis=-1, keepdims=True))
        score_low = score_grad.astype(jnp.bfloat16)
        query_grad = (
            jnp.einsum("hqk,khd->qhd", score_low, key_heads, preferred_element_type=jnp.float32)
            * score_scale
        )
        key_grad = (
            jnp.einsum(
                "hqk,qhd->khd", score_low, query_heads, preferred_element_type=jnp.float32
            ).reshape(key_count, width)
            * score_scale
        )
        score_tiles = score_low.reshape(
            heads_local, query_hot.shape[0], SEG_LEN, key_hot.shape[0], SEG_LEN
        )
        by_query = jnp.einsum(
            "hapbq,ax->hxpbq", score_tiles, query_hot, preferred_element_type=jnp.float32
        )
        by_both = jnp.einsum(
            "hxpbq,by->hxpyq",
            by_query,
            key_hot.astype(jnp.float32),
            precision=lax.Precision.HIGHEST,
        )
        table_acc = table_acc + by_both.reshape(heads_local, DEPTHS, DEPTHS)
        return (table_acc, (query_grad.reshape(block_rows, width), key_grad, value_grad))

    start_table = jnp.zeros((heads_local, DEPTHS, DEPTHS), jnp.float32)
    table_acc, block_grads = lax.scan(
        one_block,
        start_table,
        (
            queries.reshape(trees, block_rows, width),
            mixed_grad.reshape(trees, block_rows, width),
            key_trees,
            value_trees,
            reach_blocks,
            query_hots,
            key_hots,
            log_totals,
        ),
    )
    return (block_grads[0].reshape(row_count, width), block_grads[1], block_grads[2], table_acc)


def shards(
    tokens,
    parents,
    query_weight,
    query_bias,
    key_weight,
    value_weight,
    value_bias,
    output_weight,
    output_bias,
    first_gain,
    first_shift,
    inner_weight,
    inner_bias,
    outer_weight,
    outer_bias,
    second_gain,
    second_shift,
    mask_logits,
    mask_noise,
    cotangent,
):
    relaxed_low = jax.nn.log_sigmoid(mask_logits + mask_noise).astype(jnp.bfloat16)
    queries, keys_all, values_all, full_rows, table = project(tokens, query_weight, key_weight, value_weight, query_bias, value_bias, mask_logits, mask_noise)
    table = table.reshape(HEADS_DEV, DEPTHS, DEPTHS)
    attended, soft = attend(parents, queries, keys_all, values_all, table)
    weight_set = (None,None,None,
        lax.all_gather(inner_weight, "shard", axis=0, tiled=True),
        lax.all_gather(output_weight, "shard", axis=1, tiled=True),
        lax.all_gather(outer_weight, "shard", axis=1, tiled=True))
    attn_sum = (
        sum_rows(jnp.dot(attended, weight_set[4], preferred_element_type=jnp.float32)) + output_bias
    )
    first_out, first_back = jax.vjp(
        layer_norm, tokens.astype(jnp.float32) + attn_sum, first_gain, first_shift
    )
    first_rows = gather_rows(first_out.astype(jnp.bfloat16))
    inner_pre = jnp.dot(first_rows, weight_set[3], preferred_element_type=jnp.float32) + inner_bias
    activated, gelu_back = jax.vjp(gelu_exact, inner_pre)
    act_low = activated.astype(jnp.bfloat16)
    outer_sum = (
        sum_rows(jnp.dot(act_low, weight_set[5], preferred_element_type=jnp.float32)) + outer_bias
    )
    second_out, second_back = jax.vjp(layer_norm, first_out + outer_sum, second_gain, second_shift)
    result = second_out.astype(jnp.bfloat16)
    weight_back = (
        lax.all_gather(query_weight, "shard", axis=0, tiled=True),
        lax.all_gather(key_weight, "shard", axis=0, tiled=True),
        lax.all_gather(value_weight, "shard", axis=0, tiled=True),
        lax.all_gather(inner_weight, "shard", axis=0, tiled=True),
        lax.all_gather(output_weight, "shard", axis=1, tiled=True),
        lax.all_gather(outer_weight, "shard", axis=1, tiled=True),
        lax.all_gather(relaxed_low, "shard", axis=1, tiled=True),
    )
    second_grad, second_gain_grad, second_shift_grad = second_back(cotangent.astype(jnp.float32))
    outer_low = second_grad.astype(jnp.bfloat16)
    outer_bias_grad = jnp.sum(outer_low.astype(jnp.float32), axis=0)
    outer_rows = gather_rows(outer_low)
    outer_weight_grad = jnp.einsum(
        "rf,rd->fd", act_low, outer_rows, preferred_element_type=jnp.float32
    )
    act_grad = jnp.einsum(
        "rd,fd->rf", outer_rows, weight_back[5], preferred_element_type=jnp.float32
    )
    inner_low = gelu_back(act_grad)[0].astype(jnp.bfloat16)
    inner_bias_grad = jnp.sum(inner_low.astype(jnp.float32), axis=0)
    inner_weight_grad = jnp.einsum(
        "rd,rf->df", first_rows, inner_low, preferred_element_type=jnp.float32
    )
    first_grad = (
        sum_rows(
            jnp.einsum("rf,df->rd", inner_low, weight_back[3], preferred_element_type=jnp.float32)
        )
        + second_grad
    )
    first_in_grad, first_gain_grad, first_shift_grad = first_back(first_grad)
    attn_low = first_in_grad.astype(jnp.bfloat16)
    output_bias_grad = jnp.sum(attn_low.astype(jnp.float32), axis=0)
    attn_rows = gather_rows(attn_low)
    output_weight_grad = jnp.einsum(
        "rh,rd->hd", attended, attn_rows, preferred_element_type=jnp.float32
    )
    mixed_grad = jnp.einsum(
        "rd,hd->rh", attn_rows, weight_back[4], preferred_element_type=jnp.float32
    ).astype(jnp.bfloat16)
    query_low, key_t, value_t, table_grad = attend_back(parents, queries, keys_all, values_all, attended, mixed_grad, soft)
    key_low = lax.psum_scatter(key_t.T, "ctx", scatter_dimension=0, tiled=True)
    value_low = lax.psum_scatter(value_t.T, "ctx", scatter_dimension=0, tiled=True)
    query_bias_grad = jnp.sum(query_low.astype(jnp.float32), axis=0)
    value_bias_grad = jnp.sum(value_low.astype(jnp.float32), axis=0)
    query_weight_grad = jnp.einsum(
        "rd,rh->dh", full_rows, query_low, preferred_element_type=jnp.float32
    )
    key_weight_grad = jnp.einsum(
        "rd,rh->dh", full_rows, key_low, preferred_element_type=jnp.float32
    )
    value_weight_grad = jnp.einsum(
        "rd,rh->dh", full_rows, value_low, preferred_element_type=jnp.float32
    )
    token_terms = jnp.einsum(
        "rh,dh->rd", query_low, weight_back[0], preferred_element_type=jnp.float32
    )
    token_terms = token_terms + jnp.einsum(
        "rh,dh->rd", key_low, weight_back[1], preferred_element_type=jnp.float32
    )
    token_terms = token_terms + jnp.einsum(
        "rh,dh->rd", value_low, weight_back[2], preferred_element_type=jnp.float32
    )
    tokens_grad = sum_rows(token_terms) + first_in_grad
    shard_part = (
        lax.psum_scatter(
            query_weight_grad.astype(jnp.bfloat16), "shard", scatter_dimension=0, tiled=True
        ).astype(jnp.float32),
        lax.psum_scatter(
            key_weight_grad.astype(jnp.bfloat16), "shard", scatter_dimension=0, tiled=True
        ).astype(jnp.float32),
        lax.psum_scatter(
            value_weight_grad.astype(jnp.bfloat16), "shard", scatter_dimension=0, tiled=True
        ).astype(jnp.float32),
        lax.psum_scatter(
            inner_weight_grad.astype(jnp.bfloat16), "shard", scatter_dimension=0, tiled=True
        ).astype(jnp.float32),
        lax.psum_scatter(
            output_weight_grad.astype(jnp.bfloat16), "shard", scatter_dimension=1, tiled=True
        ).astype(jnp.float32),
        lax.psum_scatter(
            outer_weight_grad.astype(jnp.bfloat16), "shard", scatter_dimension=1, tiled=True
        ).astype(jnp.float32),
        lax.psum_scatter(
            table_grad.astype(jnp.bfloat16), "shard", scatter_dimension=1, tiled=True
        ).astype(jnp.float32),
    )
    reduced = (
        lax.psum(shard_part[0].astype(jnp.bfloat16), "ctx").astype(jnp.float32),
        lax.psum(shard_part[1].astype(jnp.bfloat16), "ctx").astype(jnp.float32),
        lax.psum(shard_part[2].astype(jnp.bfloat16), "ctx").astype(jnp.float32),
        lax.psum(shard_part[3].astype(jnp.bfloat16), "ctx").astype(jnp.float32),
        lax.psum(shard_part[4].astype(jnp.bfloat16), "ctx").astype(jnp.float32),
        lax.psum(shard_part[5].astype(jnp.bfloat16), "ctx").astype(jnp.float32),
        lax.psum(shard_part[6].astype(jnp.bfloat16), "ctx").astype(jnp.float32),
    )
    mask_logits_grad = reduced[6] * jax.nn.sigmoid(-(mask_logits + mask_noise))
    head_totals = lax.psum((query_bias_grad, value_bias_grad, inner_bias_grad), ("shard", "ctx"))
    row_totals = lax.psum(
        (
            output_bias_grad,
            outer_bias_grad,
            first_gain_grad,
            first_shift_grad,
            second_gain_grad,
            second_shift_grad,
        ),
        ("shard", "ctx", "tp"),
    )
    return (
        result,
        tokens_grad,
        reduced[0],
        head_totals[0],
        reduced[1],
        reduced[2],
        head_totals[1],
        reduced[4],
        row_totals[0],
        row_totals[2],
        row_totals[3],
        reduced[3],
        head_totals[2],
        reduced[5],
        row_totals[1],
        row_totals[4],
        row_totals[5],
        mask_logits_grad,
    )


def solution(mesh):
    in_specs = (
        P(("shard", "ctx", "tp"), None),
        P("shard", None),
        P("shard", "tp"),
        P("tp"),
        P("shard", "tp"),
        P("shard", "tp"),
        P("tp"),
        P("tp", "shard"),
        P(),
        P(),
        P(),
        P("shard", "tp"),
        P("tp"),
        P("tp", "shard"),
        P(),
        P(),
        P(),
        P("tp", "shard", None),
        P("tp", "shard", None),
        P(("shard", "ctx", "tp"), None),
    )
    out_specs = (
        P(("shard", "ctx", "tp"), None),
        P(("shard", "ctx", "tp"), None),
        P("shard", "tp"),
        P("tp"),
        P("shard", "tp"),
        P("shard", "tp"),
        P("tp"),
        P("tp", "shard"),
        P(),
        P(),
        P(),
        P("shard", "tp"),
        P("tp"),
        P("tp", "shard"),
        P(),
        P(),
        P(),
        P("tp", "shard", None),
    )
    return jax.shard_map(shards, mesh=mesh, in_specs=in_specs, out_specs=out_specs, check_vma=False)
```

```python
import jax
import jax.numpy as jnp
from jax import lax
from jax.experimental import pallas as pl
from jax.experimental.pallas import tpu as pltpu
from jax.sharding import PartitionSpec as P

MESH = pl.DeviceIdType.MESH
BF = jnp.bfloat16
F32 = jnp.float32
HEADS_DEV = 3
HEAD_DIM = 64
WIDE = 128
SEG = 128
SEGS = 20
PATH = 10
KEYS = PATH * SEG
D = 768
QK = 192
QKW = 384
ROWS = 160
CTX_ROWS = 640
TREE = 2560
DEPTHS = 512
MIB = 2**20
VM = pl.BlockSpec(memory_space=pltpu.VMEM)
SM = pl.BlockSpec(memory_space=pltpu.SMEM)


def place():
    shard = lax.axis_index("shard")
    tp = lax.axis_index("tp")
    return {
        "x": lax.axis_index("ctx"),
        "yl": lax.div(shard, 4),
        "z": lax.rem(shard, 4),
        "yh": lax.div(tp, 2),
        "core": lax.rem(tp, 2),
    }


def ident(at, **moved):
    to = {**at, **moved}
    return {"shard": to["yl"] * 4 + to["z"], "ctx": to["x"], "tp": to["yh"] * 2 + to["core"]}


def around(value, step):
    return lax.rem(value + step, 4)


def greet(devices):
    barrier = pltpu.get_barrier_semaphore()
    for device in devices:
        pl.semaphore_signal(barrier, inc=1, device_id=device, device_id_type=MESH)
    pl.semaphore_wait(barrier, len(devices))


class Mail:
    def __init__(self, send, recv):
        self.send, self.recv, self.used, self.sent = send, recv, 0, []

    def post(self, src, dst, device):
        copy = pltpu.make_async_remote_copy(
            src_ref=src,
            dst_ref=dst,
            send_sem=self.send.at[self.used],
            recv_sem=self.recv.at[self.used],
            device_id=device,
            device_id_type=MESH,
        )
        self.used += 1
        copy.start()
        self.sent.append(copy)
        return copy

    def done(self, copy):
        copy.wait()
        self.sent = [kept for kept in self.sent if kept is not copy]

    def close(self):
        for copy in self.sent:
            copy.wait_send()


def nn(a, b):
    return jnp.dot(a, b, preferred_element_type=F32)


def nt(a, b):
    return lax.dot_general(a, b, (((1,), (1,)), ((), ())), preferred_element_type=F32)


def spread(kind=BF):
    rows = lax.broadcasted_iota(jnp.int32, (QK, QKW), 0)
    cols = lax.broadcasted_iota(jnp.int32, (QK, QKW), 1)
    head, lane = cols // WIDE, cols % WIDE
    return ((head * HEAD_DIM + lane == rows) & (lane < HEAD_DIM)).astype(kind)


def project_kernel(
    tok,
    wq,
    wk,
    wv,
    qb,
    vb,
    logits,
    noise,
    q_out,
    k_out,
    v_out,
    rows_out,
    tab,
    ws,
    xs,
    wide,
    send,
    recv,
):
    at = place()
    x, yl, z, yh, core = at["x"], at["yl"], at["z"], at["yh"], at["core"]
    shard, tp = yl * 4 + z, yh * 2 + core
    sib = ident(at, core=1 - core)
    far = ident(at, yh=1 - yh)
    low = ident(at, yl=1 - yl)
    zs = [ident(at, z=around(z, k)) for k in (1, 2, 3)]
    xp = [ident(at, x=around(x, k)) for k in (1, 2, 3)]
    xs[x, tp] = tok[...]
    for j, w in enumerate((wq, wk, wv)):
        ws[shard, j] = w[...]
    masks = logits[...] + noise[...]
    tab[:, shard] = jax.nn.log_sigmoid(masks).astype(BF)
    greet([sib, far, low, *zs, *xp])
    mail = Mail(send, recv)

    def block(kx, other):
        return xs.at[around(x, 4 - kx), (1 - yh if other else yh) * 2 + core]

    def pass_on(src, device):
        return mail.post(src, src, device)

    first_far = pass_on(block(0, False), far)
    own_low = [pass_on(ws.at[shard], low), pass_on(tab.at[0, shard], low)]
    own_x = [pass_on(block(0, False), d) for d in xp]
    own_z = [pass_on(ws.at[shard], d) for d in zs]
    own_z0 = [pass_on(tab.at[0, shard], d) for d in zs]
    own_z1 = [pass_on(tab.at[pl.ds(1, 2), shard], d) for d in zs]
    to_low = [pass_on(tab.at[pl.ds(1, 2), shard], low)]
    to_sib = [pass_on(block(0, False), sib)]
    first_far.wait_recv()
    far_x = [pass_on(block(0, True), d) for d in xp]
    to_sib.append(pass_on(block(0, True), sib))
    for copy in own_low:
        copy.wait_recv()
    mate = (1 - yl) * 4 + z
    low_z = [pass_on(ws.at[mate], d) for d in zs]
    low_z0 = [pass_on(tab.at[0, mate], d) for d in zs]
    for k in (1, 3, 2):
        own_x[k - 1].wait_recv()
        to_sib.append(pass_on(block(k, False), sib))
    for k in (1, 3, 2):
        own_z1[k - 1].wait_recv()
        to_low.append(pass_on(tab.at[pl.ds(1, 2), yl * 4 + around(z, 4 - k)], low))
    for k in (1, 3, 2):
        far_x[k - 1].wait_recv()
        to_sib.append(pass_on(block(k, True), sib))
    for copy in own_z + own_z0 + low_z + to_sib:
        copy.wait_recv()

    hots = spread()
    hots32 = spread(F32)
    for j in range(3):
        whole = ws[:, j].reshape(D, QK)
        wide[:, j * QKW : (j + 1) * QKW] = nn(whole, hots).astype(BF)
    q_add = jnp.dot(qb[...], hots32, precision=lax.Precision.HIGHEST)
    v_add = jnp.dot(vb[...], hots32, precision=lax.Precision.HIGHEST)

    @pl.loop(0, 16)
    def _(i):
        rows = xs[lax.div(i, 4), lax.rem(i, 4)]
        both = nn(rows, wide[:, QKW:])
        k_out[pl.ds(i * ROWS, ROWS), :] = both[:, :QKW].astype(BF)
        v_out[pl.ds(i * ROWS, ROWS), :] = (both[:, QKW:] + v_add).astype(BF)

    @pl.loop(0, 4)
    def _(i):
        rows = xs[x, i]
        rows_out[pl.ds(i * ROWS, ROWS), :] = rows
        q_out[pl.ds(i * ROWS, ROWS), :] = (nn(rows, wide[:, :QKW]) + q_add).astype(BF)

    for copy in low_z0 + to_low:
        copy.wait_recv()
    mail.close()


def project(tokens, wq, wk, wv, qb, vb, logits, noise):
    shape = jax.ShapeDtypeStruct
    posts = 2 + 1 + 3 + 9 + 1 + 8 + 3 + 6 + 3
    return pl.pallas_call(
        project_kernel,
        out_shape=(
            shape((CTX_ROWS, QKW), BF),
            shape((TREE, QKW), BF),
            shape((TREE, QKW), BF),
            shape((CTX_ROWS, D), BF),
            shape((HEADS_DEV, 8, 64, DEPTHS), BF),
            shape((8, 3, 96, QK), BF),
        ),
        in_specs=[VM] * 8,
        out_specs=[VM] * 6,
        scratch_shapes=[
            pltpu.VMEM((4, 4, ROWS, D), BF),
            pltpu.VMEM((D, 3 * QKW), BF),
            pltpu.SemaphoreType.DMA((posts,)),
            pltpu.SemaphoreType.DMA((posts,)),
        ],
        compiler_params=pltpu.CompilerParams(
            collective_id=1, has_side_effects=True, vmem_limit_bytes=56 * MIB
        ),
        name="project",
    )(tokens, wq, wk, wv, qb.reshape(1, QK), vb.reshape(1, QK), logits, noise)


def climb(parents, seg, trail):
    trail[0] = seg
    depth = jnp.int32(0)
    here = seg
    for i in range(1, PATH):
        up = parents[0, here]
        found = up >= 0
        here = jnp.where(found, up, here)
        trail[i] = here
        depth = depth + found.astype(jnp.int32)
    return depth


def on_path(trail, depth, j):
    return trail[jnp.maximum(depth - j, 0)]


def attend_kernel(parents, q, k, v, tab, o_out, p_out, trail, kp, vp):
    a = pl.program_id(0)
    seg = lax.axis_index("ctx") * 5 + a
    depth = climb(parents, seg, trail)
    for j in range(PATH):
        rows = pl.ds(pl.multiple_of(on_path(trail, depth, j) * SEG, SEG), SEG)
        kp[pl.ds(j * SEG, SEG), :] = k[rows, :]
        vp[pl.ds(j * SEG, SEG), :] = v[rows, :]
    tile = pl.ds(pl.multiple_of(lax.rem(depth, 4) * SEG, SEG), SEG)
    outs = []
    for h in range(HEADS_DEV):
        head = slice(h * WIDE, (h + 1) * WIDE)
        mine = q[:, head] * jnp.asarray(HEAD_DIM**-0.5, BF)
        bias = tab[h, tile, :].astype(F32)
        scores = nt(mine, kp[:, head])
        parts = []
        for j in range(PATH):
            cols = slice((j % 4) * SEG, (j % 4 + 1) * SEG)
            part = scores[:, j * SEG : (j + 1) * SEG] + bias[:, cols]
            parts.append(jnp.where(j <= depth, part, -1e30))
        scores = jnp.concatenate(parts, axis=1)
        peak = jnp.max(scores, axis=1, keepdims=True)
        raised = jnp.exp(scores - peak)
        total = jnp.sum(raised, axis=1, keepdims=True)
        soft = (raised * (1.0 / total)).astype(BF)
        p_out[0, h] = soft
        outs.append(nn(soft, vp[:, head]).astype(BF))
    o_out[...] = nt(jnp.concatenate(outs, axis=1), spread()).astype(BF)


def whole(shape):
    return pl.BlockSpec(shape, lambda a: (0,) * len(shape))


def attend(parents, q, k, v, tab):
    shape = jax.ShapeDtypeStruct
    return pl.pallas_call(
        attend_kernel,
        grid=(5,),
        out_shape=(
            shape((CTX_ROWS, QK), BF),
            shape((5, HEADS_DEV, SEG, KEYS), BF),
        ),
        in_specs=[
            SM,
            pl.BlockSpec((SEG, QKW), lambda a: (a, 0)),
            whole((TREE, QKW)),
            whole((TREE, QKW)),
            whole((HEADS_DEV, DEPTHS, DEPTHS)),
        ],
        out_specs=(
            pl.BlockSpec((SEG, QK), lambda a: (a, 0)),
            pl.BlockSpec((1, HEADS_DEV, SEG, KEYS), lambda a: (a, 0, 0, 0)),
        ),
        scratch_shapes=[
            pltpu.SMEM((PATH,), jnp.int32),
            pltpu.VMEM((KEYS, QKW), BF),
            pltpu.VMEM((KEYS, QKW), BF),
        ],
        compiler_params=pltpu.CompilerParams(vmem_limit_bytes=56 * MIB),
        cost_estimate=pl.CostEstimate(
            flops=2 * 2 * 15 * SEG * KEYS * WIDE, bytes_accessed=12 * MIB, transcendentals=15 * SEG * KEYS
        ),
        name="attend",
    )(parents, q, k, v, tab)


def attend_back_kernel(
    parents, q, k, v, o, g, p, dq_out, dk_out, dv_out, tab_out, trail, kp, vp, dk, dv, dtab
):
    a = pl.program_id(0)
    seg = lax.axis_index("ctx") * 5 + a

    @pl.when(a == 0)
    def _():
        dk[...] = jnp.zeros_like(dk)
        dv[...] = jnp.zeros_like(dv)
        dtab[...] = jnp.zeros_like(dtab)

    depth = climb(parents, seg, trail)
    starts = [pl.multiple_of(on_path(trail, depth, j) * SEG, SEG) for j in range(PATH)]
    for j in range(PATH):
        kp[pl.ds(j * SEG, SEG), :] = k[pl.ds(starts[j], SEG), :]
        vp[pl.ds(j * SEG, SEG), :] = v[pl.ds(starts[j], SEG), :]
    tile = pl.ds(pl.multiple_of(lax.rem(depth, 4) * SEG, SEG), SEG)
    hots = spread()
    g_wide = nn(g[...], hots).astype(BF)
    o_wide = nn(o[...], hots)
    scale = HEAD_DIM**-0.5
    outs = []
    for h in range(HEADS_DEV):
        head = slice(h * WIDE, (h + 1) * WIDE)
        mine, grad = q[:, head], g_wide[:, head]
        soft = p[0, h]
        inner = jnp.sum(grad.astype(F32) * o_wide[:, head], axis=1, keepdims=True)
        ds = soft.astype(F32) * (nt(grad, vp[:, head]) - inner)
        low = ds.astype(BF)
        outs.append((nn(low, kp[:, head]) * scale).astype(BF))
        mine_t = (mine.astype(F32).T[:HEAD_DIM] * scale).astype(BF)
        grad_t = grad.astype(F32).T[:HEAD_DIM].astype(BF)
        dk_part = nn(mine_t, low)
        dv_part = nn(grad_t, soft)
        for j in range(PATH):
            cols = slice(j * SEG, (j + 1) * SEG)
            dk[h, :, pl.ds(starts[j], SEG)] += dk_part[:, cols]
            dv[h, :, pl.ds(starts[j], SEG)] += dv_part[:, cols]
        down = low.astype(F32)
        dtab[h, tile, 0:256] += down[:, 0:256] + down[:, 512:768] + down[:, 1024:1280]
        dtab[h, tile, 256:512] += down[:, 256:512] + down[:, 768:1024]
    dq_out[...] = nt(jnp.concatenate(outs, axis=1), hots).astype(BF)

    @pl.when(a == 4)
    def _():
        for h in range(HEADS_DEV):
            dk_out[pl.ds(h * HEAD_DIM, HEAD_DIM), :] = dk[h].astype(BF)
            dv_out[pl.ds(h * HEAD_DIM, HEAD_DIM), :] = dv[h].astype(BF)
            tab_out[h] = dtab[h].astype(BF)


def attend_back(parents, q, k, v, o, g, p):
    shape = jax.ShapeDtypeStruct
    return pl.pallas_call(
        attend_back_kernel,
        grid=(5,),
        out_shape=(
            shape((CTX_ROWS, QK), BF),
            shape((QK, TREE), BF),
            shape((QK, TREE), BF),
            shape((HEADS_DEV, DEPTHS, DEPTHS), BF),
        ),
        in_specs=[
            SM,
            pl.BlockSpec((SEG, QKW), lambda a: (a, 0)),
            whole((TREE, QKW)),
            whole((TREE, QKW)),
            pl.BlockSpec((SEG, QK), lambda a: (a, 0)),
            pl.BlockSpec((SEG, QK), lambda a: (a, 0)),
            pl.BlockSpec((1, HEADS_DEV, SEG, KEYS), lambda a: (a, 0, 0, 0)),
        ],
        out_specs=(
            pl.BlockSpec((SEG, QK), lambda a: (a, 0)),
            whole((QK, TREE)),
            whole((QK, TREE)),
            whole((HEADS_DEV, DEPTHS, DEPTHS)),
        ),
        scratch_shapes=[
            pltpu.SMEM((PATH,), jnp.int32),
            pltpu.VMEM((KEYS, QKW), BF),
            pltpu.VMEM((KEYS, QKW), BF),
            pltpu.VMEM((HEADS_DEV, HEAD_DIM, TREE), F32),
            pltpu.VMEM((HEADS_DEV, HEAD_DIM, TREE), F32),
            pltpu.VMEM((HEADS_DEV, DEPTHS, DEPTHS), F32),
        ],
        compiler_params=pltpu.CompilerParams(vmem_limit_bytes=56 * MIB),
        cost_estimate=pl.CostEstimate(
            flops=5 * 2 * 15 * SEG * KEYS * WIDE, bytes_accessed=20 * MIB, transcendentals=0
        ),
        name="attend_back",
    )(parents, q, k, v, o, g, p)


def tn(a, b):
    return lax.dot_general(a, b, (((0,), (0,)), ((), ())), preferred_element_type=F32)


def unit(n):
    rows = lax.broadcasted_iota(jnp.int32, (n, n), 0)
    cols = lax.broadcasted_iota(jnp.int32, (n, n), 1)
    return (rows == cols).astype(BF)


def y_peers(at):
    spots = []
    for k in (1, 2, 3):
        y = around(at["yh"] * 2 + at["yl"], k)
        spots.append((lax.div(y, 2), lax.rem(y, 2)))
    return spots


def normed(values):
    centre = jnp.mean(values, axis=1, keepdims=True)
    off = values - centre
    inverse = lax.rsqrt(jnp.mean(off * off, axis=1, keepdims=True) + 1e-5)
    return off * inverse, inverse


def normed_back(grad, gain, n, inverse):
    e = grad * gain
    return inverse * (e - jnp.mean(e, axis=1, keepdims=True) - n * jnp.mean(e * n, axis=1, keepdims=True))


def total(values):
    return jnp.sum(values, axis=0, keepdims=True)


def middle_kernel(
    o,
    tok,
    cot,
    wo,
    wi,
    wout,
    bo,
    g1,
    s1,
    bi,
    bout,
    g2,
    s2,
    result,
    dh1_out,
    g_out,
    grads,
    grads_o,
    vec,
    w,
    wt,
    o2,
    bias,
    part,
    got,
    rows,
    act,
    slope,
    du,
    y1s,
    n1s,
    dh2s,
    leave,
    send,
    recv,
):
    at = place()
    x, yl, z, yh, core = at["x"], at["yl"], at["z"], at["yh"], at["core"]
    sib = ident(at, core=1 - core)
    far = ident(at, yh=1 - yh)
    xp = [ident(at, x=around(x, k)) for k in (1, 2, 3)]
    zp = [ident(at, z=around(z, k)) for k in (1, 2, 3)]
    yp = [ident(at, yh=a, yl=b) for a, b in y_peers(at)]
    yz = [
        ident(at, yh=a, yl=b, z=around(z, k)) for a, b in y_peers(at) for k in (1, 2, 3)
    ]
    w[yh, yl, z, :, 0:D] = wi[...]
    w[yh, yl, z, :, D : 2 * D] = nt(unit(96), wout[...]).astype(BF)
    wt[yh, yl, z] = nt(unit(96), wo[...]).astype(BF)
    bias[yh] = bi[...]
    o2[yh] = o[pl.ds(yh * 320, 320), :]
    greet([sib, *xp, *zp, *yp, *yz])
    mail = Mail(send, recv)

    def pass_on(src, device):
        return mail.post(src, src, device)

    def waits(copies):
        for copy in copies:
            copy.wait_recv()

    q = pl.multiple_of(x * 128, 128)
    q1, q2 = pl.ds(512 + q, 128), pl.ds(1024 + q, 128)
    all_o = [mail.post(o.at[pl.ds((1 - yh) * 320, 320)], o2.at[yh], far)]
    all_o += [pass_on(wt.at[yh, yl, z], d) for d in yp + zp + yz]
    one_z = [pass_on(w.at[yh, yl, z, :, q1], d) for d in zp]
    two_y = [pass_on(w.at[yh, yl, z, :, q2], d) for d in yp]
    zero_y = [pass_on(w.at[yh, yl, z, :, pl.ds(0, 512)], d) for d in yp]
    bias_far = pass_on(bias.at[yh], far)
    waits(one_z)
    one_x = [pass_on(w.at[yh, yl, :, :, q1], d) for d in xp]
    waits(two_y)
    two_z = [pass_on(w.at[:, :, z, :, q2], d) for d in zp]
    waits(zero_y)
    zero_z = [pass_on(w.at[:, :, z, :, pl.ds(0, 512)], d) for d in zp]
    waits(two_z)
    two_x = [pass_on(w.at[:, :, :, :, q2], d) for d in xp]
    waits(one_x)
    one_y = [pass_on(w.at[yh, yl, :, :, pl.ds(512, 512)], d) for d in yp]
    waits(all_o)

    mine, other = pl.ds(core * ROWS, ROWS), pl.ds((1 - core) * ROWS, ROWS)

    def trade_sum(slot):
        mail.done(mail.post(part.at[other], got.at[slot], sib))
        return part[mine, :] + got[slot]

    def trade_rows(slot, values):
        rows[slot, mine, :] = values
        copy = pass_on(rows.at[slot, mine], sib)
        copy.wait_recv()

    for half in range(2):
        cols = slice(half * 384, (half + 1) * 384)
        part[:, cols] = nt(o2[0], wt[0, half].reshape(384, QK)) + nt(
            o2[1], wt[1, half].reshape(384, QK)
        )
    n1, inv1 = normed(tok[...].astype(F32) + trade_sum(0) + bo[...])
    n1s[...] = n1
    y1 = n1 * g1[...] + s1[...]
    y1s[...] = y1
    trade_rows(0, y1.astype(BF))
    waits([bias_far, *zero_z, *one_y, *two_x])

    @pl.loop(0, 6)
    def _(i):
        which, col = lax.div(i, 3), pl.multiple_of(lax.rem(i, 3) * 256, 256)
        weight = w[which, :, :, :, pl.ds(col, 256)].reshape(D, 256)
        u = nn(rows[0], weight) + bias[which, :, pl.ds(col, 256)]
        phi = 0.5 * (1.0 + lax.erf(u * 0.7071067811865476))
        act[which, :, pl.ds(col, 256)] = (u * phi).astype(BF)
        slope[which, :, pl.ds(col, 256)] = phi + u * (jnp.exp(-0.5 * u * u) * 0.3989422804014327)

    for half in range(2):
        cols = slice(half * 384, (half + 1) * 384)
        part[:, cols] = nt(act[0], w[0, half, :, :, D:].reshape(384, D)) + nt(
            act[1], w[1, half, :, :, D:].reshape(384, D)
        )
    n2, inv2 = normed(y1s[...] + trade_sum(1) + bout[...])
    result[...] = (n2 * g2[...] + s2[...]).astype(BF)
    c = cot[...].astype(F32)
    vec[4:5, :] = total(c * n2)
    vec[5:6, :] = total(c)
    dh2 = normed_back(c, g2[...], n2, inv2)
    dh2s[...] = dh2
    df = dh2.astype(BF)
    vec[1:2, :] = total(df.astype(F32))
    trade_rows(1, df)

    @pl.loop(0, 6)
    def _(i):
        which, col = lax.div(i, 3), pl.multiple_of(lax.rem(i, 3) * 256, 256)
        later = pl.multiple_of(col + D, 256)
        weight = w[which, :, :, :, pl.ds(later, 256)].reshape(D, 256)
        low = (nn(rows[1], weight) * slope[which, :, pl.ds(col, 256)]).astype(BF)
        du[which, :, pl.ds(col, 256)] = low
        vec[pl.ds(6 + which, 1), pl.ds(col, 256)] = total(low.astype(F32))

    for half in range(2):
        cols = slice(half * 384, (half + 1) * 384)
        part[:, cols] = nt(du[0], w[0, half, :, :, :D].reshape(384, D)) + nt(
            du[1], w[1, half, :, :, :D].reshape(384, D)
        )
    dy1 = trade_sum(2) + dh2s[...]
    n1 = n1s[...]
    vec[2:3, :] = total(dy1 * n1)
    vec[3:4, :] = total(dy1)
    dh1 = normed_back(dy1, g1[...], n1, inv1)
    dh1_out[...] = dh1
    da = dh1.astype(BF)
    vec[0:1, :] = total(da.astype(F32))
    trade_rows(2, da)
    to_far = nn(rows[2], wt[1 - yh].reshape(D, QK))
    leave[...] = to_far.astype(BF)
    back = mail.post(leave, g_out.at[pl.ds(yh * 320, 320)], far)
    g_out[pl.ds(yh * 320, 320), :] = nn(rows[2], wt[yh].reshape(D, QK)).astype(BF)
    for which in range(2):
        grads_o[which] = tn(rows[2], o2[which]).astype(BF).reshape(2, 4, 96, QK)

    @pl.loop(0, 6)
    def _(i):
        which, col = lax.div(i, 3), pl.multiple_of(lax.rem(i, 3) * 256, 256)
        later = pl.multiple_of(col + D, 256)
        first = tn(rows[0], du[which, :, pl.ds(col, 256)]).astype(BF)
        grads[which, :, :, :, pl.ds(col, 256)] = first.reshape(2, 4, 96, 256)
        last = tn(rows[1], act[which, :, pl.ds(col, 256)]).astype(BF)
        grads[which, :, :, :, pl.ds(later, 256)] = last.reshape(2, 4, 96, 256)

    back.wait_recv()
    mail.close()


def middle(o, tok, cot, wo, wi, wout, bo, g1, s1, bi, bout, g2, s2):
    shape = jax.ShapeDtypeStruct
    posts = 1 + 15 + 1 + 3 * 8 + 3 + 3 + 1
    line = lambda v: v.reshape(1, D)
    return pl.pallas_call(
        middle_kernel,
        out_shape=(
            shape((ROWS, D), BF),
            shape((ROWS, D), F32),
            shape((CTX_ROWS, QK), BF),
            shape((2, 2, 4, 96, 2 * D), BF),
            shape((2, 2, 4, 96, QK), BF),
            shape((8, D), F32),
        ),
        in_specs=[VM] * 13,
        out_specs=[VM] * 6,
        scratch_shapes=[
            pltpu.VMEM((2, 2, 4, 96, 2 * D), BF),
            pltpu.VMEM((2, 2, 4, 96, QK), BF),
            pltpu.VMEM((2, 320, QK), BF),
            pltpu.VMEM((2, 1, D), F32),
            pltpu.VMEM((320, D), F32),
            pltpu.VMEM((3, ROWS, D), F32),
            pltpu.VMEM((3, 320, D), BF),
            pltpu.VMEM((2, 320, D), BF),
            pltpu.VMEM((2, 320, D), F32),
            pltpu.VMEM((2, 320, D), BF),
            pltpu.VMEM((ROWS, D), F32),
            pltpu.VMEM((ROWS, D), F32),
            pltpu.VMEM((ROWS, D), F32),
            pltpu.VMEM((320, QK), BF),
            pltpu.SemaphoreType.DMA((posts,)),
            pltpu.SemaphoreType.DMA((posts,)),
        ],
        compiler_params=pltpu.CompilerParams(
            collective_id=2, has_side_effects=True, vmem_limit_bytes=56 * MIB
        ),
        name="middle",
    )(o, tok, cot, wo, wi, wout, *map(line, (bo, g1, s1, bi, bout, g2, s2)))


def collect_kernel(
    dq,
    dk_t,
    dv_t,
    dtab,
    g,
    go,
    x_rows,
    ws,
    dh1,
    vec,
    f,
    fo,
    fq,
    ft,
    tg_out,
    vsum,
    r_dk,
    r_dv,
    r0z,
    s0z,
    r0y,
    s0y,
    r0x,
    r1y,
    s1y,
    r1x,
    s1x,
    r1z,
    r2x,
    s2x,
    r2z,
    s2z,
    r2y,
    t0z,
    u0z,
    t0y,
    u0y,
    t0x,
    t1y,
    u1y,
    t1x,
    u1x,
    t1z,
    t2x,
    u2x,
    t2z,
    u2z,
    t2y,
    roz,
    soz,
    roy,
    rox,
    gq,
    rqz,
    sqz,
    rqy,
    rqx,
    tgp,
    r_sib,
    s_far,
    r_far,
    v_own,
    vx,
    vz,
    vy,
    vc,
    send,
    recv,
):
    at = place()
    x, yl, z, yh, core = at["x"], at["yl"], at["z"], at["yh"], at["core"]
    y = yh * 2 + yl
    sib = ident(at, core=1 - core)
    far = ident(at, yh=1 - yh)
    low = ident(at, yl=1 - yl)
    steps = (1, 2, 3)
    xp = [ident(at, x=around(x, k)) for k in steps]
    zp = [ident(at, z=around(z, k)) for k in steps]
    ys = y_peers(at)
    yp = [ident(at, yh=a, yl=b) for a, b in ys]
    greet([sib, *xp, *zp, *yp])
    mail = Mail(send, recv)

    def lanes(base, k):
        return pl.ds(pl.multiple_of(base + around(x, k) * 128, 128), 128)

    def scatter(view, landing, peers):
        return [mail.post(view(k), landing.at[k - 1], peers[k - 1]) for k in steps]

    def gathered(copies, own, landing):
        for copy in copies:
            copy.wait_recv()
        return own.astype(F32) + landing[0].astype(F32) + landing[1].astype(F32) + landing[2].astype(F32)

    def paired(copy, own, landing):
        copy.wait_recv()
        return own.astype(F32) + landing[...].astype(F32)

    def share(slots, me, peers):
        return [mail.post(slots.at[me], slots.at[me], d) for d in peers]

    def summed(copies, slots):
        for copy in copies:
            copy.wait_recv()
        return (
            slots[0].astype(F32) + slots[1].astype(F32) + slots[2].astype(F32) + slots[3].astype(F32)
        )

    def tree_cols(k):
        return pl.ds(pl.multiple_of(around(x, k) * CTX_ROWS, 128), CTX_ROWS)

    c_dk = scatter(lambda k: dk_t.at[:, tree_cols(k)], r_dk, xp)
    c_dv = scatter(lambda k: dv_t.at[:, tree_cols(k)], r_dv, xp)
    c0z = scatter(lambda k: g.at[:, :, around(z, k), :, pl.ds(0, 512)], r0z, zp)
    c1y = scatter(lambda k: g.at[ys[k - 1][0], ys[k - 1][1], :, :, pl.ds(512, 512)], r1y, yp)
    c2x = scatter(lambda k: g.at[:, :, :, :, lanes(1024, k)], r2x, xp)
    d0z = scatter(lambda k: dtab.at[0, :, around(z, k)], t0z, zp)
    d1y = mail.post(dtab.at[1, 1 - yl], t1y, low)
    d2x = scatter(lambda k: dtab.at[2, :, :, :, lanes(0, k)], t2x, xp)
    coz = scatter(lambda k: go.at[:, :, around(z, k)], roz, zp)

    def project_grad(j, values):
        gq[j] = tn(x_rows[...], values).astype(BF).reshape(2, 4, 96, QK)
        return scatter(lambda k: gq.at[j, :, around(z, k)], rqz.at[j], zp)

    def weight(j):
        return ws[:, j].reshape(D, QK)

    q_low = dq[...]
    cqz = [project_grad(0, q_low)]
    tgp[...] = nt(q_low, weight(0))
    v_own[...] = jnp.zeros_like(v_own)
    v_own[0:8, :] = vec[...]
    v_own[pl.ds(8 + yh, 1), 0:QK] = total(q_low.astype(F32))
    k_low = gathered(c_dk, dk_t[:, tree_cols(0)], r_dk).T.astype(BF)
    v_low = gathered(c_dv, dv_t[:, tree_cols(0)], r_dv).T.astype(BF)
    v_own[pl.ds(10 + yh, 1), 0:QK] = total(v_low.astype(F32))
    vx[x] = v_own[...]
    c_vx = share(vx, x, xp)
    tgp[...] += nt(k_low, weight(1)) + nt(v_low, weight(2))

    def block(a, b):
        return pl.ds((a * 2 + b) * ROWS, ROWS)

    c_sib = [mail.post(tgp.at[block(a, 1 - core)], r_sib.at[a], sib) for a in range(2)]
    cqz.append(project_grad(1, k_low))
    cqz.append(project_grad(2, v_low))
    for copy in c_sib:
        copy.wait_recv()
    s_far[...] = (tgp[block(1 - yh, core), :] + r_sib[1 - yh]).astype(BF)
    c_far = mail.post(s_far, r_far, far)

    u0z[...] = gathered(d0z, dtab[0, :, z], t0z).astype(BF)
    d0y = mail.post(u0z.at[1 - yl], t0y, low)
    u1y[...] = paired(d1y, dtab[1, yl], t1y).astype(BF)
    d1x = scatter(lambda k: u1y.at[:, :, lanes(0, k)], t1x, xp)
    soz[...] = gathered(coz, go[:, :, z], roz).astype(BF)
    coy = scatter(lambda k: soz.at[ys[k - 1][0], ys[k - 1][1]], roy, yp)
    s0z[...] = gathered(c0z, g[:, :, z, :, 0:512], r0z).astype(BF)
    c0y = scatter(lambda k: s0z.at[ys[k - 1][0], ys[k - 1][1]], r0y, yp)
    s1y[...] = gathered(c1y, g[yh, yl, :, :, 512:1024], r1y).astype(BF)
    c1x = scatter(lambda k: s1y.at[:, :, lanes(0, k)], r1x, xp)
    s2x[...] = gathered(c2x, g[:, :, :, :, lanes(1024, 0)], r2x).astype(BF)
    c2z = scatter(lambda k: s2x.at[:, :, around(z, k)], r2z, zp)
    u2x[...] = gathered(d2x, dtab[2, :, :, :, lanes(0, 0)], t2x).astype(BF)
    d2z = scatter(lambda k: u2x.at[:, around(z, k)], t2z, zp)
    cqy = []
    for j in range(3):
        sqz[j] = gathered(cqz[j], gq[j, :, z], rqz.at[j]).astype(BF)
        cqy.append(mail.post(sqz.at[j, 1 - yl], rqy.at[j], low))
    vz[z] = summed(c_vx, vx)
    c_vz = share(vz, z, zp)

    c_far.wait_recv()
    tg_out[...] = tgp[block(yh, core), :] + r_sib[yh] + r_far[...].astype(F32) + dh1[...]
    u0y[...] = paired(d0y, u0z[yl], t0y).astype(BF)
    d0x = scatter(lambda k: u0y.at[:, lanes(0, k)], t0x, xp)
    rox[x] = gathered(coy, soz[yh, yl], roy).astype(BF)
    cox = share(rox, x, xp)
    s0y[...] = gathered(c0y, s0z[yh, yl], r0y).astype(BF)
    c0x = scatter(lambda k: s0y.at[:, lanes(0, k)], r0x, xp)
    s1x[...] = gathered(c1x, s1y[:, :, lanes(0, 0)], r1x).astype(BF)
    c1z = scatter(lambda k: s1x.at[around(z, k)], r1z, zp)
    s2z[...] = gathered(c2z, s2x[:, :, z], r2z).astype(BF)
    c2y = scatter(lambda k: s2z.at[ys[k - 1][0], ys[k - 1][1]], r2y, yp)
    u1x[...] = gathered(d1x, u1y[:, :, lanes(0, 0)], t1x).astype(BF)
    d1z = scatter(lambda k: u1x.at[around(z, k)], t1z, zp)
    u2z[...] = gathered(d2z, u2x[:, z], t2z).astype(BF)
    d2y = mail.post(u2z.at[1 - yl], t2y, low)
    cqx = []
    for j in range(3):
        rqx[j, x] = paired(cqy[j], sqz[j, yl], rqy.at[j]).astype(BF)
        cqx.append(share(rqx.at[j], x, xp))
    vy[y] = summed(c_vz, vz)
    c_vy = share(vy, y, yp)

    late = []

    def settle(ref, base, values):
        ref[:, lanes(base, 0)] = values.astype(BF)
        view = ref.at[:, lanes(base, 0)]
        late.extend(mail.post(view, view, d) for d in xp)

    settle(f, 0, gathered(c0x, s0y[:, lanes(0, 0)], r0x))
    settle(f, 512, gathered(c1z, s1x[z], r1z))
    settle(f, 1024, gathered(c2y, s2z[yh, yl], r2y))
    settle(ft.at[0], 0, gathered(d0x, u0y[:, lanes(0, 0)], t0x))
    settle(ft.at[1], 0, gathered(d1z, u1x[z], t1z))
    settle(ft.at[2], 0, paired(d2y, u2z[yl], t2y))
    vc[0] = summed(c_vy, vy)
    c_vc = mail.post(vc.at[0], vc.at[1], sib)
    fo[...] = summed(cox, rox)
    for j in range(3):
        fq[j] = summed(cqx[j], rqx.at[j])
    c_vc.wait_recv()
    vsum[...] = vc[0]
    vsum[0:6, :] = vc[0, 0:6, :] + vc[1, 0:6, :]
    for copy in late:
        copy.wait_recv()
    mail.close()


def collect(dq, dk_t, dv_t, dtab, g, go, x_rows, ws, dh1, vec):
    shape = jax.ShapeDtypeStruct
    posts = 6 + 9 + 3 + 1 + 3 + 3 + 9 + 3 + 2 + 1 + 1 + 3 + 3 + 3 + 3 + 3 + 3 + 3 + 3 + 3
    posts += 3 + 3 + 3 + 3 + 3 + 1 + 9 + 3 + 18 + 1 + 8
    buf = lambda *dims: pltpu.VMEM(dims, BF)
    buf32 = lambda *dims: pltpu.VMEM(dims, F32)
    return pl.pallas_call(
        collect_kernel,
        out_shape=(
            shape((96, 2 * D), BF),
            shape((96, QK), F32),
            shape((3, 96, QK), F32),
            shape((HEADS_DEV, 64, DEPTHS), BF),
            shape((ROWS, D), F32),
            shape((16, D), F32),
        ),
        in_specs=[VM] * 10,
        out_specs=[VM] * 6,
        scratch_shapes=[
            buf(3, QK, CTX_ROWS),
            buf(3, QK, CTX_ROWS),
            buf(3, 2, 2, 96, 512),
            buf(2, 2, 96, 512),
            buf(3, 96, 512),
            buf(96, 512),
            buf(3, 96, 128),
            buf(3, 4, 96, 512),
            buf(4, 96, 512),
            buf(3, 4, 96, 128),
            buf(4, 96, 128),
            buf(3, 96, 128),
            buf(3, 2, 2, 4, 96, 128),
            buf(2, 2, 4, 96, 128),
            buf(3, 2, 2, 96, 128),
            buf(2, 2, 96, 128),
            buf(3, 96, 128),
            buf(3, 2, 64, 512),
            buf(2, 64, 512),
            buf(64, 512),
            buf(64, 512),
            buf(3, 64, 128),
            buf(4, 64, 512),
            buf(4, 64, 512),
            buf(3, 4, 64, 128),
            buf(4, 64, 128),
            buf(3, 64, 128),
            buf(3, 2, 4, 64, 128),
            buf(2, 4, 64, 128),
            buf(3, 2, 64, 128),
            buf(2, 64, 128),
            buf(64, 128),
            buf(3, 2, 2, 96, QK),
            buf(2, 2, 96, QK),
            buf(3, 96, QK),
            buf(4, 96, QK),
            buf(3, 2, 4, 96, QK),
            buf(3, 3, 2, 96, QK),
            buf(3, 2, 96, QK),
            buf(3, 96, QK),
            buf(3, 4, 96, QK),
            buf32(CTX_ROWS, D),
            buf32(2, ROWS, D),
            buf(ROWS, D),
            buf(ROWS, D),
            buf32(16, D),
            buf32(4, 16, D),
            buf32(4, 16, D),
            buf32(4, 16, D),
            buf32(2, 16, D),
            pltpu.SemaphoreType.DMA((posts,)),
            pltpu.SemaphoreType.DMA((posts,)),
        ],
        compiler_params=pltpu.CompilerParams(
            collective_id=3, has_side_effects=True, vmem_limit_bytes=56 * MIB
        ),
        name="collect",
    )(dq, dk_t, dv_t, dtab, g, go, x_rows, ws, dh1, vec)


def finish_kernel(
    f,
    fo,
    fq,
    ft,
    tg,
    vsum,
    res,
    logits,
    noise,
    res_out,
    tg_out,
    gwq,
    gwk,
    gwv,
    gwo,
    gwi,
    gwout,
    mask,
    lines,
    narrow,
):
    res_out[...] = res[...]
    tg_out[...] = tg[...]
    gwq[...], gwk[...], gwv[...] = fq[0], fq[1], fq[2]
    gwo[...] = fo[...].T
    gwi[...] = f[:, :D].astype(F32)
    gwout[...] = f[:, D:].astype(F32).T
    mask[...] = ft[...].astype(F32) * jax.nn.sigmoid(-(logits[...] + noise[...]))
    yh = lax.div(lax.axis_index("tp"), 2)
    lines[...] = vsum[...]
    lines[6:7, :] = vsum[pl.ds(6 + yh, 1), :]
    narrow[0:1, :] = vsum[pl.ds(8 + yh, 1), 0:QK]
    narrow[1:2, :] = vsum[pl.ds(10 + yh, 1), 0:QK]


def finish(f, fo, fq, ft, tg, vsum, res, logits, noise):
    shape = jax.ShapeDtypeStruct
    return pl.pallas_call(
        finish_kernel,
        out_shape=(
            shape((ROWS, D), BF),
            shape((ROWS, D), F32),
            shape((96, QK), F32),
            shape((96, QK), F32),
            shape((96, QK), F32),
            shape((QK, 96), F32),
            shape((96, D), F32),
            shape((D, 96), F32),
            shape((HEADS_DEV, 64, DEPTHS), F32),
            shape((16, D), F32),
            shape((8, QK), F32),
        ),
        in_specs=[VM] * 9,
        out_specs=[VM] * 11,
        compiler_params=pltpu.CompilerParams(vmem_limit_bytes=56 * MIB),
        name="finish",
    )(f, fo, fq, ft, tg, vsum, res, logits, noise)


def shards(
    tokens,
    parents,
    query_weight,
    query_bias,
    key_weight,
    value_weight,
    value_bias,
    output_weight,
    output_bias,
    first_gain,
    first_shift,
    inner_weight,
    inner_bias,
    outer_weight,
    outer_bias,
    second_gain,
    second_shift,
    mask_logits,
    mask_noise,
    cotangent,
):
    q, k, v, rows, table, ws = project(
        tokens,
        query_weight,
        key_weight,
        value_weight,
        query_bias,
        value_bias,
        mask_logits,
        mask_noise,
    )
    table = table.reshape(HEADS_DEV, DEPTHS, DEPTHS)
    o, soft = attend(parents, q, k, v, table)
    result, dh1, dout, grads, grads_o, vec = middle(
        o,
        tokens,
        cotangent,
        output_weight,
        inner_weight,
        outer_weight,
        output_bias,
        first_gain,
        first_shift,
        inner_bias,
        outer_bias,
        second_gain,
        second_shift,
    )
    dq, dk_t, dv_t, dtab = attend_back(parents, q, k, v, o, dout, soft)
    dtab = dtab.reshape(HEADS_DEV, 2, 4, 64, DEPTHS)
    out = collect(dq, dk_t, dv_t, dtab, grads, grads_o, rows, ws, dh1, vec)
    result, tg, gwq, gwk, gwv, gwo, gwi, gwout, mask, lines, narrow = finish(
        *out, result, mask_logits, mask_noise
    )
    return (
        result,
        tg,
        gwq,
        narrow[0],
        gwk,
        gwv,
        narrow[1],
        gwo,
        lines[0],
        lines[2],
        lines[3],
        gwi,
        lines[6],
        gwout,
        lines[1],
        lines[4],
        lines[5],
        mask,
    )


def solution(mesh):
    in_specs = (
        P(("shard", "ctx", "tp"), None),
        P("shard", None),
        P("shard", "tp"),
        P("tp"),
        P("shard", "tp"),
        P("shard", "tp"),
        P("tp"),
        P("tp", "shard"),
        P(),
        P(),
        P(),
        P("shard", "tp"),
        P("tp"),
        P("tp", "shard"),
        P(),
        P(),
        P(),
        P("tp", "shard", None),
        P("tp", "shard", None),
        P(("shard", "ctx", "tp"), None),
    )
    out_specs = (
        P(("shard", "ctx", "tp"), None),
        P(("shard", "ctx", "tp"), None),
        P("shard", "tp"),
        P("tp"),
        P("shard", "tp"),
        P("shard", "tp"),
        P("tp"),
        P("tp", "shard"),
        P(),
        P(),
        P(),
        P("shard", "tp"),
        P("tp"),
        P("tp", "shard"),
        P(),
        P(),
        P(),
        P("tp", "shard", None),
    )
    return jax.shard_map(shards, mesh=mesh, in_specs=in_specs, out_specs=out_specs, check_vma=False)
```

```python
import jax
import jax.numpy as jnp
from jax import lax
from jax.experimental import pallas as pl
from jax.experimental.pallas import tpu as pltpu
from jax.sharding import PartitionSpec as P

MESH = pl.DeviceIdType.MESH
BF = jnp.bfloat16
F32 = jnp.float32
HEADS_DEV = 3
HEAD_DIM = 64
WIDE = 128
SEG = 128
SEGS = 20
OWN_SEGS = 5
PATH = 10
KEYS = PATH * SEG
D = 768
QK = 192
QKP = 256
QKW = 384
ROWS = 160
PAIR = 320
CTX_ROWS = 640
TREE = 2560
DEPTHS = 512
MIB = 2**20
SCALE = HEAD_DIM**-0.5
STEPS = (1, 2, 3)


def place():
    shard = lax.axis_index("shard")
    tp = lax.axis_index("tp")
    return {
        "x": lax.axis_index("ctx"),
        "yl": lax.div(shard, 4),
        "z": lax.rem(shard, 4),
        "yh": lax.div(tp, 2),
        "core": lax.rem(tp, 2),
    }


def ident(at, **moved):
    to = {**at, **moved}
    return {"shard": to["yl"] * 4 + to["z"], "ctx": to["x"], "tp": to["yh"] * 2 + to["core"]}


def around(value, step):
    return lax.rem(value + step, 4)


def greet(devices):
    barrier = pltpu.get_barrier_semaphore()
    for device in devices:
        pl.semaphore_signal(barrier, inc=1, device_id=device, device_id_type=MESH)
    pl.semaphore_wait(barrier, len(devices))


class Mail:
    def __init__(self, send, recv):
        self.send, self.recv, self.used, self.sent = send, recv, 0, []

    def post(self, src, dst, device):
        copy = pltpu.make_async_remote_copy(
            src_ref=src,
            dst_ref=dst,
            send_sem=self.send.at[self.used],
            recv_sem=self.recv.at[self.used],
            device_id=device,
            device_id_type=MESH,
        )
        self.used += 1
        copy.start()
        self.sent.append(copy)
        return copy

    def same(self, ref, devices):
        return [self.post(ref, ref, device) for device in devices]

    def spread(self, view, landing, devices):
        return [self.post(view(k), landing.at[k - 1], devices[k - 1]) for k in STEPS]

    def ring(self, view, ahead, behind):
        return [self.post(view(0), view(0), ahead), self.post(view(0), view(0), behind)]

    def ring_on(self, view, first, ahead, behind):
        arrived(first[:1])
        onward = [self.post(view(3, 0), view(3, 0), ahead)]
        arrived(first[1:])
        return onward + [self.post(view(1, 1), view(1, 1), behind)]

    def fold(self, view, landing, ahead, behind):
        return [
            self.post(view(2, 0), landing.at[0], ahead),
            self.post(view(2, 1), landing.at[1], behind),
            self.post(view(1, 1), landing.at[3], ahead),
            self.post(view(3, 0), landing.at[4], behind),
        ]

    def fold_on(self, view, landing, first, ahead, behind):
        out = first[2:]
        for half, k, slot, device in ((0, 1, 2, ahead), (1, 3, 5, behind)):
            arrived(first[half : half + 1])
            term = view(k, half)
            term[...] = (term[...].astype(F32) + landing[half].astype(F32)).astype(BF)
            out.append(self.post(term, landing.at[slot], device))
        return out

    def done(self, copy):
        copy.wait()
        self.sent = [kept for kept in self.sent if kept is not copy]

    def flush(self):
        for copy in self.sent:
            copy.wait_send()
        self.sent = []


def arrived(copies):
    for copy in copies:
        copy.wait_recv()


def nn(a, b):
    return jnp.dot(a, b, preferred_element_type=F32)


def nt(a, b):
    return lax.dot_general(a, b, (((1,), (1,)), ((), ())), preferred_element_type=F32)


def tn(a, b):
    return lax.dot_general(a, b, (((0,), (0,)), ((), ())), preferred_element_type=F32)


def spread_heads(kind=BF):
    rows = lax.broadcasted_iota(jnp.int32, (QK, QKW), 0)
    cols = lax.broadcasted_iota(jnp.int32, (QK, QKW), 1)
    head, lane = cols // WIDE, cols % WIDE
    return ((head * HEAD_DIM + lane == rows) & (lane < HEAD_DIM)).astype(kind)


def unit(rows_count, cols_count):
    rows = lax.broadcasted_iota(jnp.int32, (rows_count, cols_count), 0)
    cols = lax.broadcasted_iota(jnp.int32, (rows_count, cols_count), 1)
    return (rows == cols).astype(BF)


def line(ref):
    return jnp.concatenate([ref[i : i + 1, :] for i in range(6)], axis=1)


def normed(values):
    centre = jnp.mean(values, axis=1, keepdims=True)
    off = values - centre
    inverse = lax.rsqrt(jnp.mean(off * off, axis=1, keepdims=True) + 1e-5)
    return off * inverse, inverse


def normed_back(grad, gain, n, inverse):
    e = grad * gain
    return inverse * (e - jnp.mean(e, axis=1, keepdims=True) - n * jnp.mean(e * n, axis=1, keepdims=True))


def total(values):
    return jnp.sum(values, axis=0, keepdims=True)


def added(own, landing, count=3):
    out = own.astype(F32)
    for i in range(count):
        out = out + landing[i].astype(F32)
    return out


def folded(view, landing, half):
    near = landing[2 + half].astype(F32) + landing[4 + half].astype(F32)
    return view(0, half)[...].astype(F32) + near


def slots_total(slots):
    return slots[0].astype(F32) + slots[1].astype(F32) + slots[2].astype(F32) + slots[3].astype(F32)


INPUTS = (
    "parents",
    "tok",
    "cot",
    "wq",
    "wk",
    "wv",
    "qb",
    "vb",
    "logits",
    "noise",
    "wo",
    "wi",
    "wout_t",
    "bo",
    "g1",
    "s1",
    "bi",
    "bout",
    "g2",
    "s2",
)
OUTPUTS = {
    "res": ((ROWS, D), BF),
    "tg": ((ROWS, D), F32),
    "f": ((96, 2 * D), BF),
    "fo": ((96, QKP), F32),
    "fq": ((3, 96, QKP), F32),
    "ft": ((HEADS_DEV, 64, DEPTHS), BF),
    "vsum": ((16, D), F32),
}
SCRATCH = {
    "cots": ((ROWS, D), BF),
    "lines": ((7, 6, 128), F32),
    "qvb": ((2, 1, QK), F32),
    "wos": ((QK, 96), BF),
    "masks": ((2, HEADS_DEV, 64, DEPTHS), F32),
    "xs": ((4, 4, ROWS, D), BF),
    "ws": ((8, 3, 96, QK), BF),
    "wide": ((2, 4, 96, 3 * QKW), BF),
    "q": ((CTX_ROWS, QKW), BF),
    "k": ((SEGS, SEG, QKW), BF),
    "v": ((SEGS, SEG, QKW), BF),
    "tab": ((HEADS_DEV, 2, 4, 64, DEPTHS), BF),
    "kp": ((KEYS, QKW), BF),
    "vp": ((KEYS, QKW), BF),
    "p": ((OWN_SEGS, HEADS_DEV, SEG, KEYS), BF),
    "o_wide": ((CTX_ROWS, QKW), BF),
    "o": ((CTX_ROWS, QK), BF),
    "w": ((2, 2, 4, 96, 2 * D), BF),
    "wt": ((2, 2, 4, 96, QKP), BF),
    "o2": ((2, PAIR, QK), BF),
    "bias": ((2, 1, D), F32),
    "part": ((PAIR, D), F32),
    "got": ((3, ROWS, D), F32),
    "rows": ((3, PAIR, D), BF),
    "act": ((2, PAIR, D), BF),
    "slope": ((CTX_ROWS, D), F32),
    "du": ((2, PAIR, D), BF),
    "y1s": ((ROWS, D), F32),
    "n1s": ((ROWS, D), F32),
    "dh2s": ((ROWS, D), F32),
    "dh1s": ((ROWS, D), F32),
    "dout": ((CTX_ROWS, QK), BF),
    "parts": ((2, PATH, HEAD_DIM, SEG), F32),
    "dtab": ((HEADS_DEV, DEPTHS, DEPTHS), F32),
    "dq_wide": ((CTX_ROWS, QKW), BF),
    "tgp": ((CTX_ROWS, D), F32),
    "r_dkv": ((6, HEADS_DEV, 64, CTX_ROWS), BF),
    "r0z": ((6, 1, 2, 96, 512), BF),
    "s0z": ((2, 2, 96, 512), BF),
    "r0y": ((3, 96, 512), BF),
    "s0y": ((96, 512), BF),
    "r0x": ((3, 96, 128), BF),
    "r1y": ((6, 2, 96, 512), BF),
    "s1y": ((4, 96, 512), BF),
    "r1x": ((3, 4, 96, 128), BF),
    "s1x": ((4, 96, 128), BF),
    "r1z": ((3, 96, 128), BF),
    "r2x": ((6, 1, 2, 4, 96, 128), BF),
    "s2x": ((2, 2, 4, 96, 128), BF),
    "r2z": ((3, 2, 2, 96, 128), BF),
    "s2z": ((2, 2, 96, 128), BF),
    "r2y": ((3, 96, 128), BF),
    "t0z": ((3, 2, 64, 512), BF),
    "u0z": ((2, 64, 512), BF),
    "t0y": ((64, 512), BF),
    "u0y": ((64, 512), BF),
    "t0x": ((3, 64, 128), BF),
    "t1y": ((4, 64, 512), BF),
    "u1y": ((4, 64, 512), BF),
    "t1x": ((3, 4, 64, 128), BF),
    "u1x": ((4, 64, 128), BF),
    "t1z": ((3, 64, 128), BF),
    "t2y": ((4, 64, 512), BF),
    "u2y": ((4, 64, 512), BF),
    "t2z": ((3, 64, 512), BF),
    "u2z": ((64, 512), BF),
    "t2x": ((3, 64, 128), BF),
    "roz": ((3, 2, 2, 96, QKP), BF),
    "soz": ((2, 2, 96, QKP), BF),
    "roy": ((3, 96, QKP), BF),
    "rox": ((4, 96, QKP), BF),
    "rqz": ((3, 3, 2, 96, QKP), BF),
    "sqz": ((3, 2, 96, QKP), BF),
    "rqy": ((3, 96, QKP), BF),
    "rqx": ((3, 4, 96, QKP), BF),
    "r_far": ((ROWS, D), BF),
    "v_own": ((16, D), F32),
    "vx": ((4, 16, D), F32),
    "vz": ((4, 16, D), F32),
    "vy": ((4, 16, D), F32),
    "vc": ((2, 16, D), F32),
}
POSTS = 260


class Names:
    pass


def layer_kernel(*refs):
    r = Names()
    names = [*INPUTS, *OUTPUTS, *SCRATCH, "trail", "depths", "fetch", "send", "recv"]
    for name, ref in zip(names, refs, strict=True):
        setattr(r, name, ref)
    at = place()
    x, yl, z, yh, core = at["x"], at["yl"], at["z"], at["yh"], at["core"]
    shard, tp, y = yl * 4 + z, yh * 2 + core, yh * 2 + yl
    sib = ident(at, core=1 - core)
    far = ident(at, yh=1 - yh)
    low = ident(at, yl=1 - yl)
    xp = [ident(at, x=around(x, k)) for k in STEPS]
    zp = [ident(at, z=around(z, k)) for k in STEPS]
    ys = [(lax.div(around(y, k), 2), lax.rem(around(y, k), 2)) for k in (0, 1, 2, 3)]
    yp = [ident(at, yh=a, yl=b) for a, b in ys[1:]]
    x_ring, y_ring, z_ring = (xp[0], xp[2]), (yp[0], yp[2]), (zp[0], zp[2])
    mail = Mail(r.send, r.recv)

    def lanes(base, k):
        return pl.ds(pl.multiple_of(base + around(x, k) * 128, 128), 128)

    def halves(size, half):
        return pl.ds(0, size) if half is None else pl.ds(half * size // 2, size // 2)

    def tok_own(k, half=None):
        return r.xs.at[around(x, k), tp, halves(ROWS, half)]

    def tok_far(k, half=None):
        return r.xs.at[around(x, k), (1 - yh) * 2 + core, halves(ROWS, half)]

    def ws_of(side):
        return lambda k, half=None: r.ws.at[side * 4 + around(z, k), :, halves(96, half)]

    def tab_of(side):
        return lambda k, half=None: r.tab.at[halves(2, half), side, around(z, k)]

    def tab_last(k, half=None):
        return r.tab.at[2, yl, around(z, k), halves(64, half)]

    def w0(k, half=None):
        return r.w.at[halves(2, half), :, around(z, k), :, pl.ds(0, 512)]

    def w1(k, half=None):
        return r.w.at[ys[k][0], ys[k][1], halves(4, half), :, pl.ds(512, 512)]

    def w2(k, half=None):
        return r.w.at[halves(2, half), :, :, :, lanes(1024, k)]

    def bring(n, src, dst):
        copy = pltpu.make_async_copy(src, dst, r.fetch.at[n])
        copy.start()
        return copy

    def brought(copies):
        for copy in copies:
            copy.wait()

    get_tok = [bring(0, r.tok, tok_own(0))]
    get_ws = [bring(1 + j, w, r.ws.at[shard, j]) for j, w in enumerate((r.wq, r.wk, r.wv))]
    get_masks = [bring(4 + j, m, r.masks.at[j]) for j, m in enumerate((r.logits, r.noise))]
    get_w = [
        bring(6, r.wout_t, r.w.at[yh, yl, z, :, pl.ds(0, D)]),
        bring(7, r.wi, r.w.at[yh, yl, z, :, pl.ds(D, D)]),
        bring(8, r.wo, r.wos),
    ]
    vectors = (r.bo, r.g1, r.s1, r.bi, r.bout, r.g2, r.s2)
    get_rest = [bring(9 + j, v, r.lines.at[j]) for j, v in enumerate(vectors)]
    get_rest += [bring(16, r.cot, r.cots), bring(17, r.qb, r.qvb.at[0]), bring(18, r.vb, r.qvb.at[1])]
    bo, g1, s1, bi, bout, g2, s2 = [r.lines.at[j] for j in range(7)]
    greet([sib, *xp, *zp, *yp])
    brought(get_tok)
    first_far = mail.same(tok_own(0), [far])
    own_x = mail.ring(tok_own, *x_ring)
    to_sib = mail.same(tok_own(0), [sib])
    brought(get_ws)
    own_low = mail.same(r.ws.at[shard], [low])
    own_z = mail.ring(ws_of(yl), *z_ring)
    brought(get_masks)
    r.tab[:, yl, z] = jax.nn.log_sigmoid(r.masks[0] + r.masks[1]).astype(BF)
    tab_low = mail.same(tab_of(yl)(0), [low])
    to_low = mail.same(tab_last(0), [low])
    tab_z = mail.ring(tab_of(yl), *z_ring)
    last_z = mail.ring(tab_last, *z_ring)
    brought(get_w + get_rest)
    r.wt[yh, yl, z] = jnp.concatenate(
        [nt(unit(96, 96), r.wos[...]).astype(BF), jnp.zeros((96, QKP - QK), BF)], axis=1
    )
    r.bias[yh] = line(bi)
    one_z = mail.same(r.w.at[yh, yl, z, :, lanes(512, 0)], zp)
    o_z = mail.same(r.wt.at[yh, yl, z], zp)
    two_y = mail.same(r.w.at[yh, yl, z, :, lanes(1024, 0)], yp)
    zero_y = mail.same(r.w.at[yh, yl, z, :, pl.ds(0, 512)], yp)
    bias_far = mail.same(r.bias.at[yh], [far])
    arrived(first_far)
    far_x = mail.ring(tok_far, *x_ring)
    to_sib += mail.same(tok_far(0), [sib])
    arrived(own_low)
    low_z = mail.ring(ws_of(1 - yl), *z_ring)
    own_z2 = mail.ring_on(ws_of(yl), own_z, *z_ring)
    own_x2 = mail.ring_on(tok_own, own_x, *x_ring)
    to_sib += mail.same(tok_own(1), [sib]) + mail.same(tok_own(3), [sib])
    arrived(tab_low)
    low_tab = mail.ring(tab_of(1 - yl), *z_ring)
    low_z2 = mail.ring_on(ws_of(1 - yl), low_z, *z_ring)
    far_x2 = mail.ring_on(tok_far, far_x, *x_ring)
    to_sib += mail.same(tok_far(1), [sib]) + mail.same(tok_far(3), [sib])
    arrived(own_x2)
    to_sib += mail.same(tok_own(2), [sib])
    tab_z2 = mail.ring_on(tab_of(yl), tab_z, *z_ring)
    last_z2 = mail.ring_on(tab_last, last_z, *z_ring)
    to_low += mail.same(tab_last(1), [low]) + mail.same(tab_last(3), [low])
    arrived(two_y)
    two_z = mail.same(r.w.at[:, :, z, :, lanes(1024, 0)], zp)
    arrived(o_z)
    o_y = mail.same(r.wt.at[yh, yl], yp)
    arrived(far_x2)
    to_sib += mail.same(tok_far(2), [sib])
    arrived(one_z)
    one_x = mail.same(r.w.at[yh, yl, :, :, lanes(512, 0)], xp)
    arrived(own_z2 + low_z2)
    low_tab2 = mail.ring_on(tab_of(1 - yl), low_tab, *z_ring)
    arrived(last_z2)
    to_low += mail.same(tab_last(2), [low])
    arrived(zero_y)
    zero_z = mail.ring(w0, *z_ring)

    hots = spread_heads()
    hots32 = spread_heads(F32)
    for j in range(3):
        full = r.ws[:, j].reshape(D, QK)
        r.wide[:, :, :, j * QKW : (j + 1) * QKW] = nn(full, hots).astype(BF).reshape(2, 4, 96, QKW)
    q_add = jnp.dot(r.qvb[0], hots32, precision=lax.Precision.HIGHEST)
    v_add = jnp.dot(r.qvb[1], hots32, precision=lax.Precision.HIGHEST)
    arrived(to_sib)

    @pl.loop(0, 4)
    def _(i):
        both = nn(r.xs[i].reshape(CTX_ROWS, D), r.wide[:, :, :, QKW:].reshape(D, 2 * QKW))
        mine = pl.ds(i * OWN_SEGS, OWN_SEGS)
        r.k[mine] = both[:, :QKW].astype(BF).reshape(OWN_SEGS, SEG, QKW)
        r.v[mine] = (both[:, QKW:] + v_add).astype(BF).reshape(OWN_SEGS, SEG, QKW)

    @pl.loop(0, 4)
    def _(i):
        wide_q = r.wide[:, :, :, :QKW].reshape(D, QKW)
        r.q[pl.ds(i * ROWS, ROWS), :] = (nn(r.xs[x, i], wide_q) + q_add).astype(BF)

    arrived(one_x)
    one_y = mail.ring(w1, *y_ring)
    arrived(two_z)
    two_x = mail.ring(w2, *x_ring)

    def climb(seg):
        r.trail[0] = seg
        depth = jnp.int32(0)
        here = seg
        for i in range(1, PATH):
            up = r.parents[0, here]
            found = up >= 0
            here = jnp.where(found, up, here)
            r.trail[i] = here
            depth = depth + found.astype(jnp.int32)
        return depth

    def on_path(depth, j):
        return r.trail[jnp.maximum(depth - j, 0)]

    def fetch_path(depth):
        for j in range(PATH):
            above = on_path(depth, j)
            r.kp[pl.ds(j * SEG, SEG), :] = r.k[above]
            r.vp[pl.ds(j * SEG, SEG), :] = r.v[above]

    arrived(tab_z2 + low_tab2 + to_low)

    def attend(a):
        depth = climb(x * OWN_SEGS + a)
        fetch_path(depth)
        mine = pl.ds(pl.multiple_of(a * SEG, SEG), SEG)
        tile = lax.rem(depth, 4) * 2
        for h in range(HEADS_DEV):
            head = slice(h * WIDE, (h + 1) * WIDE)
            low_q = r.q[mine, head] * jnp.asarray(SCALE, BF)
            flat = r.tab.at[h]
            pieces = [
                flat[lax.div(tile + i, 4), lax.rem(tile + i, 4)].astype(F32) for i in range(2)
            ]
            table = jnp.concatenate(pieces, axis=0)
            scores = nt(low_q, r.kp[:, head])
            parts = []
            for j in range(PATH):
                cols = slice((j % 4) * SEG, (j % 4 + 1) * SEG)
                score = scores[:, j * SEG : (j + 1) * SEG] + table[:, cols]
                parts.append(jnp.where(j <= depth, score, -1e30))
            scores = jnp.concatenate(parts, axis=1)
            peak = jnp.max(scores, axis=1, keepdims=True)
            raised = jnp.exp(scores - peak)
            whole = jnp.sum(raised, axis=1, keepdims=True)
            soft = (raised * (1.0 / whole)).astype(BF)
            r.p[a, h] = soft
            r.o_wide[mine, head] = nn(soft, r.vp[:, head]).astype(BF)

    pl.loop(0, 2)(attend)
    zero_z2 = mail.ring_on(w0, zero_z, *z_ring)
    pl.loop(2, 4)(attend)
    one_y2 = mail.ring_on(w1, one_y, *y_ring)
    two_x2 = mail.ring_on(w2, two_x, *x_ring)
    pl.loop(4, 5)(attend)
    r.o[...] = nt(r.o_wide[...], hots).astype(BF)
    o_far = [mail.post(r.o.at[pl.ds((1 - yh) * PAIR, PAIR)], r.o2.at[yh], far)]
    r.o2[yh] = r.o[pl.ds(yh * PAIR, PAIR), :]

    own, other = pl.ds(core * ROWS, ROWS), pl.ds((1 - core) * ROWS, ROWS)

    def trade_sum(slot):
        mail.done(mail.post(r.part.at[other], r.got.at[slot], sib))
        return r.part[own, :] + r.got[slot]

    def trade_rows(slot, values):
        r.rows[slot, own, :] = values
        arrived(mail.same(r.rows.at[slot, own], [sib]))

    def both_halves(left0, left1, weights):
        for half in range(2):
            cols = slice(half * 384, (half + 1) * 384)
            r.part[:, cols] = nt(left0, weights(0, half)) + nt(left1, weights(1, half))

    def tiles():
        return [(which, n) for which in range(2) for n in range(3)]

    def outer(which, half):
        return r.w[which, half, :, :, :D].reshape(384, D)

    def inner(which, half):
        return r.w[which, half, :, :, D:].reshape(384, D)

    arrived(o_y + o_far)
    both_halves(r.o2[0], r.o2[1], lambda a, b: r.wt[a, b, :, :, :QK].reshape(384, QK))
    n1, inv1 = normed(r.xs[x, tp].astype(F32) + trade_sum(0) + line(bo))
    r.n1s[...] = n1
    y1 = n1 * line(g1) + line(s1)
    r.y1s[...] = y1
    trade_rows(0, y1.astype(BF))
    arrived([*bias_far, *zero_z2, *one_y2, *two_x2])

    @pl.loop(0, 6)
    def _(i):
        which, col = lax.div(i, 3), pl.multiple_of(lax.rem(i, 3) * 256, 256)
        later = pl.multiple_of(col + D, 256)
        weight = r.w[which, :, :, :, pl.ds(later, 256)].reshape(D, 256)
        u = nn(r.rows[0], weight) + r.bias[which, :, pl.ds(col, 256)]
        phi = 0.5 * (1.0 + lax.erf(u * 0.7071067811865476))
        r.act[which, :, pl.ds(col, 256)] = (u * phi).astype(BF)
        slope = phi + u * (jnp.exp(-0.5 * u * u) * 0.3989422804014327)
        r.slope[pl.ds(pl.multiple_of(which * PAIR, PAIR), PAIR), pl.ds(col, 256)] = slope

    both_halves(r.act[0], r.act[1], outer)
    n2, inv2 = normed(r.y1s[...] + trade_sum(1) + line(bout))
    gain2 = line(g2)
    r.res[...] = (n2 * gain2 + line(s2)).astype(BF)
    c = r.cots[...].astype(F32)
    r.v_own[...] = jnp.zeros_like(r.v_own)
    r.v_own[4:5, :] = total(c * n2)
    r.v_own[5:6, :] = total(c)
    dh2 = normed_back(c, gain2, n2, inv2)
    r.dh2s[...] = dh2
    df = dh2.astype(BF)
    r.v_own[1:2, :] = total(df.astype(F32))
    trade_rows(1, df)

    @pl.loop(0, 6)
    def _(i):
        which, col = lax.div(i, 3), pl.multiple_of(lax.rem(i, 3) * 256, 256)
        weight = r.w[which, :, :, :, pl.ds(col, 256)].reshape(D, 256)
        slope = r.slope[pl.ds(pl.multiple_of(which * PAIR, PAIR), PAIR), pl.ds(col, 256)]
        grad = (nn(r.rows[1], weight) * slope).astype(BF)
        r.du[which, :, pl.ds(col, 256)] = grad
        r.v_own[pl.ds(6 + which, 1), pl.ds(col, 256)] = total(grad.astype(F32))

    mail.flush()
    both_halves(r.du[0], r.du[1], inner)
    c_dy = [mail.post(r.part.at[other], r.got.at[2], sib)]

    @pl.loop(0, 6)
    def _(i):
        which, col = lax.div(i, 3), pl.multiple_of(lax.rem(i, 3) * 256, 256)
        later = pl.multiple_of(col + D, 256)
        grad = tn(r.rows[1], r.act[which, :, pl.ds(col, 256)]).astype(BF)
        r.w[which, :, :, :, pl.ds(col, 256)] = grad.reshape(2, 4, 96, 256)
        grad = tn(r.rows[0], r.du[which, :, pl.ds(col, 256)]).astype(BF)
        r.w[which, :, :, :, pl.ds(later, 256)] = grad.reshape(2, 4, 96, 256)

    c0z = mail.fold(w0, r.r0z, *z_ring)
    c2x = mail.fold(w2, r.r2x, *x_ring)
    arrived(c_dy)
    dy1 = r.part[own, :] + r.got[2] + r.dh2s[...]
    n1 = r.n1s[...]
    r.v_own[2:3, :] = total(dy1 * n1)
    r.v_own[3:4, :] = total(dy1)
    dh1 = normed_back(dy1, line(g1), n1, inv1)
    r.dh1s[...] = dh1
    da = dh1.astype(BF)
    r.v_own[0:1, :] = total(da.astype(F32))
    trade_rows(2, da)
    leave = r.o.at[pl.ds(0, PAIR)]
    leave[...] = nn(r.rows[2], r.wt[1 - yh, :, :, :, :QK].reshape(D, QK)).astype(BF)
    back = [mail.post(leave, r.dout.at[pl.ds(yh * PAIR, PAIR)], far)]
    r.dout[pl.ds(yh * PAIR, PAIR), :] = nn(r.rows[2], r.wt[yh, :, :, :, :QK].reshape(D, QK)).astype(BF)
    for which in range(2):
        grad = tn(r.rows[2], r.o2[which]).astype(BF)
        r.wt[which, :, :, :, :QK] = grad.reshape(2, 4, 96, QK)
    r.slope[...] = jnp.zeros_like(r.slope)
    r.tgp[...] = jnp.zeros_like(r.tgp)
    r.dtab[...] = jnp.zeros_like(r.dtab)
    for b in range(SEGS):
        r.depths[b] = climb(jnp.int32(b))
    arrived(back)
    c1y = mail.fold(w1, r.r1y, *y_ring)
    coz = mail.spread(lambda k: r.wt.at[:, :, around(z, k)], r.roz, zp)

    def spot(h, b):
        n = h * SEGS + b
        return slice(n // 6 * 64, n // 6 * 64 + 64), slice(n % 6 * 128, n % 6 * 128 + 128)

    def attend_back(a):
        depth = climb(x * OWN_SEGS + a)
        fetch_path(depth)
        mine = pl.ds(pl.multiple_of(a * SEG, SEG), SEG)
        tile = lax.rem(depth, 4)
        grads = nn(r.dout[mine, :], hots).astype(BF)
        for h in range(HEADS_DEV):
            head = slice(h * WIDE, (h + 1) * WIDE)
            low_q, grad = r.q[mine, head], grads[:, head]
            soft = r.p[a, h]
            inside = grad.astype(F32) * r.o_wide[mine, head].astype(F32)
            ds = soft.astype(F32) * (
                nt(grad, r.vp[:, head]) - jnp.sum(inside, axis=1, keepdims=True)
            )
            ds_low = ds.astype(BF)
            r.dq_wide[mine, head] = (nn(ds_low, r.kp[:, head]) * SCALE).astype(BF)
            q_t = (low_q.astype(F32).T[:HEAD_DIM] * SCALE).astype(BF)
            grad_t = grad.astype(F32).T[:HEAD_DIM].astype(BF)
            dk_part, dv_part = nn(q_t, ds_low), nn(grad_t, soft)
            for j in range(PATH):
                r.parts[0, j] = dk_part[:, j * SEG : (j + 1) * SEG]
                r.parts[1, j] = dv_part[:, j * SEG : (j + 1) * SEG]
            for b in range(SEGS):
                down = r.depths[b]
                held = (down <= depth) & (on_path(depth, down) == b)
                rows, cols = spot(h, b)
                r.slope[rows, cols] += jnp.where(held, r.parts[0, down], 0.0)
                r.tgp[rows, cols] += jnp.where(held, r.parts[1, down], 0.0)
            fall = ds_low.astype(F32)
            left = fall[:, 0:256] + fall[:, 512:768] + fall[:, 1024:1280]
            right = fall[:, 256:512] + fall[:, 768:1024]
            for t in range(4):
                span = slice(t * SEG, (t + 1) * SEG)
                r.dtab[h, span, 0:256] += jnp.where(tile == t, left, 0.0)
                r.dtab[h, span, 256:512] += jnp.where(tile == t, right, 0.0)

    c0z = mail.fold_on(w0, r.r0z, c0z, *z_ring)
    c2x = mail.fold_on(w2, r.r2x, c2x, *x_ring)
    pl.loop(0, OWN_SEGS)(attend_back)
    c1y = mail.fold_on(w1, r.r1y, c1y, *y_ring)
    for h in range(HEADS_DEV):
        for b in range(SEGS):
            rows, cols = spot(h, b)
            into = slice(b % 5 * SEG, (b % 5 + 1) * SEG)
            r.p[b // 5, h, 0:64, into] = r.slope[rows, cols].astype(BF)
            r.p[b // 5, h, 64:128, into] = r.tgp[rows, cols].astype(BF)

    def dkv(k, half):
        return r.p.at[around(x, k), :, pl.ds(half * 64, 64), pl.ds(0, CTX_ROWS)]

    c_dkv = mail.fold(dkv, r.r_dkv, *x_ring)
    for h in range(HEADS_DEV):
        r.tab[h] = r.dtab[h].astype(BF).reshape(2, 4, 64, DEPTHS)
    d0z = mail.spread(lambda k: r.tab.at[0, :, around(z, k)], r.t0z, zp)
    d1y = mail.post(r.tab.at[1, 1 - yl], r.t1y, low)
    d2y = mail.post(r.tab.at[2, 1 - yl], r.t2y, low)

    def project_grad(j, values):
        room = slice(j * QKW, j * QKW + QK)
        parts = [tn(r.xs[x, i], values[i * ROWS : (i + 1) * ROWS, :]) for i in range(4)]
        r.wide[:, :, :, room] = (parts[0] + parts[1] + parts[2] + parts[3]).astype(BF).reshape(2, 4, 96, QK)
        send = pl.ds(j * QKW, QKP)
        return mail.spread(lambda k: r.wide.at[:, around(z, k), :, send], r.rqz.at[j], zp)

    def weight_of(j):
        return r.ws[:, j].reshape(D, QK)

    q_low = nt(r.dq_wide[...], hots).astype(BF)
    cqz = [project_grad(0, q_low)]
    r.tgp[...] = nt(q_low, weight_of(0))
    r.v_own[pl.ds(8 + yh, 1), 0:QK] = total(q_low.astype(F32))
    c_dkv = mail.fold_on(dkv, r.r_dkv, c_dkv, *x_ring)
    arrived(c0z)
    for half in range(2):
        r.s0z[half : half + 1] = folded(w0, r.r0z, half).astype(BF)
    c0y = mail.spread(lambda k: r.s0z.at[ys[k][0], ys[k][1]], r.r0y, yp)
    arrived(c2x)
    for half in range(2):
        r.s2x[half : half + 1] = folded(w2, r.r2x, half).astype(BF)
    c2z = mail.spread(lambda k: r.s2x.at[:, :, around(z, k)], r.r2z, zp)
    arrived(coz)
    r.soz[...] = added(r.wt[:, :, z], r.roz).astype(BF)
    coy = mail.spread(lambda k: r.soz.at[ys[k][0], ys[k][1]], r.roy, yp)
    arrived(c1y)
    for half in range(2):
        r.s1y[half * 2 : half * 2 + 2] = folded(w1, r.r1y, half).astype(BF)
    c1x = mail.spread(lambda k: r.s1y.at[:, :, lanes(0, k)], r.r1x, xp)
    arrived(d0z)
    r.u0z[...] = added(r.tab[0, :, z], r.t0z).astype(BF)
    d0y = mail.post(r.u0z.at[1 - yl], r.t0y, low)
    arrived([d1y])
    r.u1y[...] = (r.tab[1, yl].astype(F32) + r.t1y[...].astype(F32)).astype(BF)
    d1x = mail.spread(lambda k: r.u1y.at[:, :, lanes(0, k)], r.t1x, xp)
    arrived([d2y])
    r.u2y[...] = (r.tab[2, yl].astype(F32) + r.t2y[...].astype(F32)).astype(BF)
    d2z = mail.spread(lambda k: r.u2y.at[around(z, k)], r.t2z, zp)

    arrived(c_dkv)
    k_low = folded(dkv, r.r_dkv, 0).reshape(QK, CTX_ROWS).T.astype(BF)
    v_low = folded(dkv, r.r_dkv, 1).reshape(QK, CTX_ROWS).T.astype(BF)
    r.v_own[pl.ds(10 + yh, 1), 0:QK] = total(v_low.astype(F32))
    r.vx[x] = r.v_own[...]
    c_vx = mail.same(r.vx.at[x], xp)
    r.tgp[...] += nt(k_low, weight_of(1)) + nt(v_low, weight_of(2))

    def quarter(a, b):
        return pl.ds((a * 2 + b) * ROWS, ROWS)

    c_sib = [mail.post(r.tgp.at[quarter(a, 1 - core)], r.got.at[a], sib) for a in range(2)]
    cqz.append(project_grad(1, k_low))
    cqz.append(project_grad(2, v_low))
    arrived(c_sib)
    s_far = r.rows.at[0, pl.ds(0, ROWS)]
    s_far[...] = (r.tgp[quarter(1 - yh, core), :] + r.got[1 - yh]).astype(BF)
    c_far = [mail.post(s_far, r.r_far, far)]

    arrived(c0y)
    r.s0y[...] = added(r.s0z[yh, yl], r.r0y).astype(BF)
    c0x = mail.spread(lambda k: r.s0y.at[:, lanes(0, k)], r.r0x, xp)
    arrived(coy)
    r.rox[x] = added(r.soz[yh, yl], r.roy).astype(BF)
    cox = mail.same(r.rox.at[x], xp)
    arrived(c1x)
    r.s1x[...] = added(r.s1y[:, :, lanes(0, 0)], r.r1x).astype(BF)
    c1z = mail.spread(lambda k: r.s1x.at[around(z, k)], r.r1z, zp)
    arrived([d0y])
    r.u0y[...] = (r.u0z[yl].astype(F32) + r.t0y[...].astype(F32)).astype(BF)
    d0x = mail.spread(lambda k: r.u0y.at[:, lanes(0, k)], r.t0x, xp)
    arrived(d1x)
    r.u1x[...] = added(r.u1y[:, :, lanes(0, 0)], r.t1x).astype(BF)
    d1z = mail.spread(lambda k: r.u1x.at[around(z, k)], r.t1z, zp)
    cqy = []
    for j in range(3):
        arrived(cqz[j])
        r.sqz[j] = added(r.wide[:, z, :, j * QKW : j * QKW + QKP], r.rqz.at[j]).astype(BF)
        cqy.append(mail.post(r.sqz.at[j, 1 - yl], r.rqy.at[j], low))
    arrived(c_vx)
    r.vz[z] = slots_total(r.vx)
    c_vz = mail.same(r.vz.at[z], zp)
    arrived(d2z)
    r.u2z[...] = added(r.u2y[z], r.t2z).astype(BF)
    d2x = mail.spread(lambda k: r.u2z.at[:, lanes(0, k)], r.t2x, xp)
    arrived(c_far)
    r.tg[...] = r.tgp[quarter(yh, core), :] + r.got[yh] + r.r_far[...].astype(F32) + r.dh1s[...]
    cqx = []
    for j in range(3):
        arrived([cqy[j]])
        r.rqx[j, x] = (r.sqz[j, yl].astype(F32) + r.rqy[j].astype(F32)).astype(BF)
        cqx.append(mail.same(r.rqx.at[j, x], xp))

    late = []

    def settle(ref, base, values):
        ref[:, lanes(base, 0)] = values.astype(BF)
        late.extend(mail.same(ref.at[:, lanes(base, 0)], xp))

    arrived(c0x)
    settle(r.f, 0, added(r.s0y[:, lanes(0, 0)], r.r0x))
    arrived(c1z)
    settle(r.f, 512, added(r.s1x[z], r.r1z))
    arrived(d0x)
    settle(r.ft.at[0], 0, added(r.u0y[:, lanes(0, 0)], r.t0x))
    arrived(d1z)
    settle(r.ft.at[1], 0, added(r.u1x[z], r.t1z))
    arrived(c_vz)
    r.vy[y] = slots_total(r.vz)
    c_vy = mail.same(r.vy.at[y], yp)
    arrived(c2z)
    r.s2z[...] = added(r.s2x[:, :, z], r.r2z).astype(BF)
    c2y = mail.spread(lambda k: r.s2z.at[ys[k][0], ys[k][1]], r.r2y, yp)
    arrived(d2x)
    settle(r.ft.at[2], 0, added(r.u2z[:, lanes(0, 0)], r.t2x))
    arrived(c_vy)
    r.vc[0] = slots_total(r.vy)
    c_vc = mail.post(r.vc.at[0], r.vc.at[1], sib)
    arrived(c2y)
    settle(r.f, 1024, added(r.s2z[yh, yl], r.r2y))
    arrived(cox)
    r.fo[...] = slots_total(r.rox)
    for j in range(3):
        arrived(cqx[j])
        r.fq[j] = slots_total(r.rqx.at[j])
    arrived([c_vc])
    r.vsum[...] = r.vc[0]
    r.vsum[0:6, :] = r.vc[0, 0:6, :] + r.vc[1, 0:6, :]
    arrived(late)
    mail.flush()
    assert mail.used <= POSTS


def layer(*arrays):
    vm = pl.BlockSpec(memory_space=pltpu.VMEM)
    hbm = pl.BlockSpec(memory_space=pltpu.HBM)
    return pl.pallas_call(
        layer_kernel,
        out_shape=tuple(jax.ShapeDtypeStruct(*entry) for entry in OUTPUTS.values()),
        in_specs=[pl.BlockSpec(memory_space=pltpu.SMEM)] + [hbm] * (len(INPUTS) - 1),
        out_specs=[vm] * len(OUTPUTS),
        scratch_shapes=[
            *(pltpu.VMEM(*entry) for entry in SCRATCH.values()),
            pltpu.SMEM((PATH,), jnp.int32),
            pltpu.SMEM((SEGS,), jnp.int32),
            pltpu.SemaphoreType.DMA((20,)),
            pltpu.SemaphoreType.DMA((POSTS,)),
            pltpu.SemaphoreType.DMA((POSTS,)),
        ],
        compiler_params=pltpu.CompilerParams(
            collective_id=1, has_side_effects=True, vmem_limit_bytes=60 * MIB
        ),
        name="layer",
    )(*arrays)


def finish_kernel(*refs):
    f_in, fo_in, fq_in, ft_in, tg, vsum_in, res, logits_in, noise_in = refs[:9]
    res_out, tg_out, gwq, gwk, gwv, gwo, gwi, gwout_t, mask, gbq, gbv, *lines = refs[9:-8]
    f, fo, fq, ft, vsum, logits, noise, sem = refs[-8:]
    pairs = [
        (res, res_out),
        (tg, tg_out),
        (f_in, f),
        (fo_in, fo),
        (fq_in, fq),
        (ft_in, ft),
        (vsum_in, vsum),
        (logits_in, logits),
        (noise_in, noise),
    ]
    copies = [pltpu.make_async_copy(src, dst, sem.at[n]) for n, (src, dst) in enumerate(pairs)]
    for copy in copies:
        copy.start()
    for copy in copies[2:]:
        copy.wait()
    gwq[...], gwk[...], gwv[...] = fq[0, :, :QK], fq[1, :, :QK], fq[2, :, :QK]
    gwo[...] = fo[...].T[:QK]
    gwout_t[...] = f[:, :D].astype(F32)
    gwi[...] = f[:, D:].astype(F32)
    mask[...] = ft[...].astype(F32) * jax.nn.sigmoid(-(logits[...] + noise[...]))
    yh = lax.div(lax.axis_index("tp"), 2)
    gbq[...] = vsum[pl.ds(8 + yh, 1), 0:QK]
    gbv[...] = vsum[pl.ds(10 + yh, 1), 0:QK]
    for n, out in enumerate(lines):
        row = vsum[pl.ds(6 + yh, 1), :] if n == 6 else vsum[n : n + 1, :]
        for i in range(6):
            out[i : i + 1, :] = row[:, i * 128 : (i + 1) * 128]
    for copy in copies[:2]:
        copy.wait()


def finish(f, fo, fq, ft, tg, vsum, res, logits, noise):
    shape = jax.ShapeDtypeStruct
    vm = pl.BlockSpec(memory_space=pltpu.VMEM)
    hbm = pl.BlockSpec(memory_space=pltpu.HBM)
    outs = (
        shape((ROWS, D), BF),
        shape((ROWS, D), F32),
        shape((96, QK), F32),
        shape((96, QK), F32),
        shape((96, QK), F32),
        shape((QK, 96), F32),
        shape((96, D), F32),
        shape((96, D), F32),
        shape((HEADS_DEV, 64, DEPTHS), F32),
        shape((1, QK), F32),
        shape((1, QK), F32),
        *[shape((6, 128), F32)] * 7,
    )
    held = (f, fo, fq, ft, vsum, logits, noise)
    return pl.pallas_call(
        finish_kernel,
        out_shape=outs,
        in_specs=[hbm] * 9,
        out_specs=[hbm] * 2 + [vm] * (len(outs) - 2),
        scratch_shapes=[
            *(pltpu.VMEM(entry.shape, entry.dtype) for entry in held),
            pltpu.SemaphoreType.DMA((9,)),
        ],
        compiler_params=pltpu.CompilerParams(vmem_limit_bytes=60 * MIB),
        name="finish",
    )(f, fo, fq, ft, tg, vsum, res, logits, noise)


def shards(
    tokens,
    parents,
    query_weight,
    query_bias,
    key_weight,
    value_weight,
    value_bias,
    output_weight,
    output_bias,
    first_gain,
    first_shift,
    inner_weight,
    inner_bias,
    outer_weight,
    outer_bias,
    second_gain,
    second_shift,
    mask_logits,
    mask_noise,
    cotangent,
):
    def lined(vector):
        return vector.reshape(6, 128)

    res, tg, f, fo, fq, ft, vsum = layer(
        parents,
        tokens,
        cotangent,
        query_weight,
        key_weight,
        value_weight,
        query_bias.reshape(1, QK),
        value_bias.reshape(1, QK),
        mask_logits,
        mask_noise,
        output_weight,
        inner_weight,
        outer_weight.T,
        lined(output_bias),
        lined(first_gain),
        lined(first_shift),
        lined(inner_bias),
        lined(outer_bias),
        lined(second_gain),
        lined(second_shift),
    )
    result, tg, gwq, gwk, gwv, gwo, gwi, gwout_t, mask, gbq, gbv, *lines = finish(
        f, fo, fq, ft, tg, vsum, res, mask_logits, mask_noise
    )
    bo, bout, g1, s1, g2, s2, bi = [entry.reshape(D) for entry in lines]
    return (
        result,
        tg,
        gwq,
        gbq.reshape(QK),
        gwk,
        gwv,
        gbv.reshape(QK),
        gwo,
        bo,
        g1,
        s1,
        gwi,
        bi,
        gwout_t.T,
        bout,
        g2,
        s2,
        mask,
    )


def solution(mesh):
    in_specs = (
        P(("shard", "ctx", "tp"), None),
        P("shard", None),
        P("shard", "tp"),
        P("tp"),
        P("shard", "tp"),
        P("shard", "tp"),
        P("tp"),
        P("tp", "shard"),
        P(),
        P(),
        P(),
        P("shard", "tp"),
        P("tp"),
        P("tp", "shard"),
        P(),
        P(),
        P(),
        P("tp", "shard", None),
        P("tp", "shard", None),
        P(("shard", "ctx", "tp"), None),
    )
    out_specs = (
        P(("shard", "ctx", "tp"), None),
        P(("shard", "ctx", "tp"), None),
        P("shard", "tp"),
        P("tp"),
        P("shard", "tp"),
        P("shard", "tp"),
        P("tp"),
        P("tp", "shard"),
        P(),
        P(),
        P(),
        P("shard", "tp"),
        P("tp"),
        P("tp", "shard"),
        P(),
        P(),
        P(),
        P("tp", "shard", None),
    )
    return jax.shard_map(shards, mesh=mesh, in_specs=in_specs, out_specs=out_specs, check_vma=False)
```

```python
import jax
import jax.numpy as jnp
from jax import lax
from jax.experimental import pallas as pl
from jax.experimental.pallas import tpu as pltpu
from jax.sharding import PartitionSpec as P

MESH = pl.DeviceIdType.MESH
BF = jnp.bfloat16
F32 = jnp.float32
HEADS_DEV = 3
HEAD_DIM = 64
WIDE = 128
SEG = 128
SEGS = 20
OWN_SEGS = 5
PATH = 10
KEYS = PATH * SEG
D = 768
QK = 192
QKP = 256
QKW = 384
QKV = QKP + QKW
ROWS = 160
PAIR = 320
CTX_ROWS = 640
TREE = 2560
DEPTHS = 512
MIB = 2**20
SCALE = HEAD_DIM**-0.5
STEPS = (1, 2, 3)


def place():
    shard = lax.axis_index("shard")
    tp = lax.axis_index("tp")
    return {
        "x": lax.axis_index("ctx"),
        "yl": lax.div(shard, 4),
        "z": lax.rem(shard, 4),
        "yh": lax.div(tp, 2),
        "core": lax.rem(tp, 2),
    }


def ident(at, **moved):
    to = {**at, **moved}
    return {"shard": to["yl"] * 4 + to["z"], "ctx": to["x"], "tp": to["yh"] * 2 + to["core"]}


def around(value, step):
    return lax.rem(value + step, 4)


def greet(devices):
    barrier = pltpu.get_barrier_semaphore()
    for device in devices:
        pl.semaphore_signal(barrier, inc=1, device_id=device, device_id_type=MESH)
    pl.semaphore_wait(barrier, len(devices))


class Mail:
    def __init__(self, send, recv):
        self.send, self.recv, self.used, self.sent = send, recv, 0, []

    def post(self, src, dst, device):
        copy = pltpu.make_async_remote_copy(
            src_ref=src,
            dst_ref=dst,
            send_sem=self.send.at[self.used],
            recv_sem=self.recv.at[self.used],
            device_id=device,
            device_id_type=MESH,
        )
        self.used += 1
        copy.start()
        self.sent.append(copy)
        return copy

    def same(self, ref, devices):
        return [self.post(ref, ref, device) for device in devices]

    def spread(self, view, landing, devices):
        return [self.post(view(k), landing.at[k - 1], devices[k - 1]) for k in STEPS]

    def ring(self, view, ahead, behind):
        return [self.post(view(0), view(0), ahead), self.post(view(0), view(0), behind)]

    def ring_on(self, view, first, ahead, behind):
        arrived(first[:1])
        onward = [self.post(view(3, 0), view(3, 0), ahead)]
        arrived(first[1:])
        return onward + [self.post(view(1, 1), view(1, 1), behind)]

    def fold(self, view, landing, ahead, behind):
        return [
            self.post(view(2, 0), landing.at[0], ahead),
            self.post(view(2, 1), landing.at[1], behind),
            self.post(view(1, 1), landing.at[3], ahead),
            self.post(view(3, 0), landing.at[4], behind),
        ]

    def fold_on(self, view, landing, first, ahead, behind):
        out = first[2:]
        for half, k, slot, device in ((0, 1, 2, ahead), (1, 3, 5, behind)):
            arrived(first[half : half + 1])
            term = view(k, half)
            term[...] = (term[...].astype(F32) + landing[half].astype(F32)).astype(BF)
            out.append(self.post(term, landing.at[slot], device))
        return out

    def done(self, copy):
        copy.wait()
        self.sent = [kept for kept in self.sent if kept is not copy]

    def flush(self):
        for copy in self.sent:
            copy.wait_send()
        self.sent = []


def arrived(copies):
    for copy in copies:
        copy.wait_recv()


def nn(a, b):
    return jnp.dot(a, b, preferred_element_type=F32)


def nt(a, b):
    return lax.dot_general(a, b, (((1,), (1,)), ((), ())), preferred_element_type=F32)


def tn(a, b):
    return lax.dot_general(a, b, (((0,), (0,)), ((), ())), preferred_element_type=F32)


def spread_heads(kind=BF):
    rows = lax.broadcasted_iota(jnp.int32, (QK, QKW), 0)
    cols = lax.broadcasted_iota(jnp.int32, (QK, QKW), 1)
    head, lane = cols // WIDE, cols % WIDE
    return ((head * HEAD_DIM + lane == rows) & (lane < HEAD_DIM)).astype(kind)


def unit(rows_count, cols_count):
    rows = lax.broadcasted_iota(jnp.int32, (rows_count, cols_count), 0)
    cols = lax.broadcasted_iota(jnp.int32, (rows_count, cols_count), 1)
    return (rows == cols).astype(BF)


def line(ref):
    return jnp.concatenate([ref[i : i + 1, :] for i in range(6)], axis=1)


def normed(values):
    centre = jnp.mean(values, axis=1, keepdims=True)
    off = values - centre
    inverse = lax.rsqrt(jnp.mean(off * off, axis=1, keepdims=True) + 1e-5)
    return off * inverse, inverse


def normed_back(grad, gain, n, inverse):
    e = grad * gain
    return inverse * (e - jnp.mean(e, axis=1, keepdims=True) - n * jnp.mean(e * n, axis=1, keepdims=True))


def total(values):
    return jnp.sum(values, axis=0, keepdims=True)


def added(own, landing, count=3):
    out = own.astype(F32)
    for i in range(count):
        out = out + landing[i].astype(F32)
    return out


def folded(view, landing, half):
    near = landing[2 + half].astype(F32) + landing[4 + half].astype(F32)
    return view(0, half)[...].astype(F32) + near


def slots_total(slots):
    return slots[0].astype(F32) + slots[1].astype(F32) + slots[2].astype(F32) + slots[3].astype(F32)


INPUTS = (
    "parents",
    "tok",
    "cot",
    "wq",
    "wk",
    "wv",
    "qb",
    "vb",
    "logits",
    "noise",
    "wo",
    "wi",
    "wout_t",
    "bo",
    "g1",
    "s1",
    "bi",
    "bout",
    "g2",
    "s2",
)
OUTPUTS = {
    "res": ((ROWS, D), BF),
    "tg": ((ROWS, D), F32),
    "f": ((96, 2 * D), BF),
    "fo": ((96, QKP), F32),
    "fq": ((96, QKV), F32),
    "ft": ((HEADS_DEV, 64, DEPTHS), BF),
    "vsum": ((16, D), F32),
}
SCRATCH = {
    "cots": ((ROWS, D), BF),
    "lines": ((7, 6, 128), F32),
    "qvb": ((2, 1, QK), F32),
    "wos": ((QK, 96), BF),
    "masks": ((2, HEADS_DEV, 64, DEPTHS), F32),
    "xs": ((4, 4, ROWS, D), BF),
    "ws": ((8, 3, 96, QK), BF),
    "wide": ((2, 4, 96, 3 * QKW), BF),
    "q": ((CTX_ROWS, QKW), BF),
    "k": ((SEGS, SEG, QKW), BF),
    "v": ((SEGS, SEG, QKW), BF),
    "tab": ((HEADS_DEV, 2, 4, 64, DEPTHS), BF),
    "kp": ((KEYS, QKW), BF),
    "vp": ((KEYS, QKW), BF),
    "p": ((OWN_SEGS, HEADS_DEV, SEG, KEYS), BF),
    "o_wide": ((CTX_ROWS, QKW), BF),
    "o": ((CTX_ROWS, QK), BF),
    "w": ((2, 2, 4, 96, 2 * D), BF),
    "wt": ((2, 2, 4, 96, QKP), BF),
    "o2": ((2, PAIR, QK), BF),
    "bias": ((2, 1, D), F32),
    "part": ((PAIR, D), F32),
    "got": ((3, ROWS, D), F32),
    "rows": ((3, PAIR, D), BF),
    "act": ((2, PAIR, D), BF),
    "slope": ((CTX_ROWS, D), F32),
    "du": ((2, PAIR, D), BF),
    "y1s": ((ROWS, D), F32),
    "n1s": ((ROWS, D), F32),
    "dh2s": ((ROWS, D), F32),
    "dh1s": ((ROWS, D), F32),
    "dout": ((CTX_ROWS, QK), BF),
    "parts": ((2, PATH, HEAD_DIM, SEG), F32),
    "dtab": ((HEADS_DEV, DEPTHS, DEPTHS), F32),
    "dq_wide": ((CTX_ROWS, QKW), BF),
    "tgp": ((CTX_ROWS, D), F32),
    "r_dka": ((6, 2, 64, CTX_ROWS), BF),
    "r_dkb": ((6, 1, 64, CTX_ROWS), BF),
    "kv_t": ((2 * QK, D), F32),
    "r0z": ((6, 1, 2, 96, 512), BF),
    "s0z": ((2, 2, 96, 512), BF),
    "r0y": ((3, 96, 512), BF),
    "s0y": ((96, 512), BF),
    "r0x": ((3, 96, 128), BF),
    "r1y": ((6, 2, 96, 512), BF),
    "s1y": ((4, 96, 512), BF),
    "r1x": ((3, 4, 96, 128), BF),
    "s1x": ((4, 96, 128), BF),
    "r1z": ((3, 96, 128), BF),
    "r2x": ((6, 1, 2, 4, 96, 128), BF),
    "s2x": ((2, 2, 4, 96, 128), BF),
    "r2z": ((3, 2, 2, 96, 128), BF),
    "s2z": ((2, 2, 96, 128), BF),
    "r2y": ((3, 96, 128), BF),
    "t0z": ((3, 2, 64, 512), BF),
    "u0z": ((2, 64, 512), BF),
    "t0y": ((64, 512), BF),
    "u0y": ((64, 512), BF),
    "t0x": ((3, 64, 128), BF),
    "t1y": ((4, 64, 512), BF),
    "u1y": ((4, 64, 512), BF),
    "t1x": ((3, 4, 64, 128), BF),
    "u1x": ((4, 64, 128), BF),
    "t1z": ((3, 64, 128), BF),
    "t2y": ((4, 64, 512), BF),
    "u2y": ((4, 64, 512), BF),
    "t2z": ((3, 64, 512), BF),
    "u2z": ((64, 512), BF),
    "t2x": ((3, 64, 128), BF),
    "roz": ((3, 2, 2, 96, QKP), BF),
    "soz": ((2, 2, 96, QKP), BF),
    "roy": ((3, 96, QKP), BF),
    "rox": ((4, 96, QKP), BF),
    "rqz": ((3, 2, 96, QKV), BF),
    "sqz": ((2, 96, QKV), BF),
    "rqy": ((96, QKV), BF),
    "rqx": ((4, 96, QKV), BF),
    "r_far": ((ROWS, D), BF),
    "v_own": ((16, D), F32),
    "vx": ((4, 16, D), F32),
    "vz": ((4, 16, D), F32),
    "vy": ((4, 16, D), F32),
    "vc": ((2, 16, D), F32),
}
POSTS = 260


class Names:
    pass


def layer_kernel(*refs):
    r = Names()
    names = [*INPUTS, *OUTPUTS, *SCRATCH, "trail", "depths", "fetch", "send", "recv"]
    for name, ref in zip(names, refs, strict=True):
        setattr(r, name, ref)
    at = place()
    x, yl, z, yh, core = at["x"], at["yl"], at["z"], at["yh"], at["core"]
    shard, tp, y = yl * 4 + z, yh * 2 + core, yh * 2 + yl
    sib = ident(at, core=1 - core)
    far = ident(at, yh=1 - yh)
    low = ident(at, yl=1 - yl)
    xp = [ident(at, x=around(x, k)) for k in STEPS]
    zp = [ident(at, z=around(z, k)) for k in STEPS]
    ys = [(lax.div(around(y, k), 2), lax.rem(around(y, k), 2)) for k in (0, 1, 2, 3)]
    yp = [ident(at, yh=a, yl=b) for a, b in ys[1:]]
    x_ring, y_ring, z_ring = (xp[0], xp[2]), (yp[0], yp[2]), (zp[0], zp[2])
    mail = Mail(r.send, r.recv)

    def lanes(base, k):
        return pl.ds(pl.multiple_of(base + around(x, k) * 128, 128), 128)

    def halves(size, half):
        return pl.ds(0, size) if half is None else pl.ds(half * size // 2, size // 2)

    def tok_own(k, half=None):
        return r.xs.at[around(x, k), tp, halves(ROWS, half)]

    def tok_far(k, half=None):
        return r.xs.at[around(x, k), (1 - yh) * 2 + core, halves(ROWS, half)]

    def ws_of(side):
        return lambda k, half=None: r.ws.at[side * 4 + around(z, k), :, halves(96, half)]

    def tab_of(side):
        return lambda k, half=None: r.tab.at[halves(2, half), side, around(z, k)]

    def tab_last(k, half=None):
        return r.tab.at[2, yl, around(z, k), halves(64, half)]

    def w0(k, half=None):
        return r.w.at[halves(2, half), :, around(z, k), :, pl.ds(0, 512)]

    def w1(k, half=None):
        return r.w.at[ys[k][0], ys[k][1], halves(4, half), :, pl.ds(512, 512)]

    def w2(k, half=None):
        return r.w.at[halves(2, half), :, :, :, lanes(1024, k)]

    def bring(n, src, dst):
        copy = pltpu.make_async_copy(src, dst, r.fetch.at[n])
        copy.start()
        return copy

    def brought(copies):
        for copy in copies:
            copy.wait()

    get_tok = [bring(0, r.tok, tok_own(0))]
    get_ws = [bring(1 + j, w, r.ws.at[shard, j]) for j, w in enumerate((r.wq, r.wk, r.wv))]
    get_masks = [bring(4 + j, m, r.masks.at[j]) for j, m in enumerate((r.logits, r.noise))]
    get_w = [
        bring(6, r.wout_t, r.w.at[yh, yl, z, :, pl.ds(0, D)]),
        bring(7, r.wi, r.w.at[yh, yl, z, :, pl.ds(D, D)]),
        bring(8, r.wo, r.wos),
    ]
    vectors = (r.bo, r.g1, r.s1, r.bi, r.bout, r.g2, r.s2)
    get_rest = [bring(9 + j, v, r.lines.at[j]) for j, v in enumerate(vectors)]
    get_rest += [bring(16, r.cot, r.cots), bring(17, r.qb, r.qvb.at[0]), bring(18, r.vb, r.qvb.at[1])]
    bo, g1, s1, bi, bout, g2, s2 = [r.lines.at[j] for j in range(7)]
    greet([sib, *xp, *zp, *yp])
    brought(get_tok)
    first_far = mail.same(tok_own(0), [far])
    own_x = mail.ring(tok_own, *x_ring)
    to_sib = mail.same(tok_own(0), [sib])
    brought(get_ws)
    own_low = mail.same(r.ws.at[shard], [low])
    own_z = mail.ring(ws_of(yl), *z_ring)
    brought(get_masks)
    r.tab[:, yl, z] = jax.nn.log_sigmoid(r.masks[0] + r.masks[1]).astype(BF)
    tab_low = mail.same(tab_of(yl)(0), [low])
    to_low = mail.same(tab_last(0), [low])
    tab_z = mail.ring(tab_of(yl), *z_ring)
    last_z = mail.ring(tab_last, *z_ring)
    brought(get_w + get_rest)
    r.wt[yh, yl, z] = jnp.concatenate(
        [nt(unit(96, 96), r.wos[...]).astype(BF), jnp.zeros((96, QKP - QK), BF)], axis=1
    )
    r.bias[yh] = line(bi)
    one_z = mail.same(r.w.at[yh, yl, z, :, lanes(512, 0)], zp)
    o_z = mail.same(r.wt.at[yh, yl, z], zp)
    two_y = mail.same(r.w.at[yh, yl, z, :, lanes(1024, 0)], yp)
    zero_y = mail.same(r.w.at[yh, yl, z, :, pl.ds(0, 512)], yp)
    bias_far = mail.same(r.bias.at[yh], [far])
    arrived(first_far)
    far_x = mail.ring(tok_far, *x_ring)
    to_sib += mail.same(tok_far(0), [sib])
    arrived(own_low)
    low_z = mail.ring(ws_of(1 - yl), *z_ring)
    own_z2 = mail.ring_on(ws_of(yl), own_z, *z_ring)
    own_x2 = mail.ring_on(tok_own, own_x, *x_ring)
    to_sib += mail.same(tok_own(1), [sib]) + mail.same(tok_own(3), [sib])
    arrived(tab_low)
    low_tab = mail.ring(tab_of(1 - yl), *z_ring)
    low_z2 = mail.ring_on(ws_of(1 - yl), low_z, *z_ring)
    far_x2 = mail.ring_on(tok_far, far_x, *x_ring)
    to_sib += mail.same(tok_far(1), [sib]) + mail.same(tok_far(3), [sib])
    arrived(own_x2)
    to_sib += mail.same(tok_own(2), [sib])
    tab_z2 = mail.ring_on(tab_of(yl), tab_z, *z_ring)
    last_z2 = mail.ring_on(tab_last, last_z, *z_ring)
    to_low += mail.same(tab_last(1), [low]) + mail.same(tab_last(3), [low])
    arrived(two_y)
    two_z = mail.same(r.w.at[:, :, z, :, lanes(1024, 0)], zp)
    arrived(o_z)
    o_y = mail.same(r.wt.at[yh, yl], yp)
    arrived(far_x2)
    to_sib += mail.same(tok_far(2), [sib])
    arrived(one_z)
    one_x = mail.same(r.w.at[yh, yl, :, :, lanes(512, 0)], xp)
    arrived(own_z2 + low_z2)
    low_tab2 = mail.ring_on(tab_of(1 - yl), low_tab, *z_ring)
    arrived(last_z2)
    to_low += mail.same(tab_last(2), [low])
    arrived(zero_y)
    zero_z = mail.ring(w0, *z_ring)

    hots = spread_heads()
    hots32 = spread_heads(F32)
    for j in range(3):
        full = r.ws[:, j].reshape(D, QK)
        r.wide[:, :, :, j * QKW : (j + 1) * QKW] = nn(full, hots).astype(BF).reshape(2, 4, 96, QKW)
    q_add = jnp.dot(r.qvb[0], hots32, precision=lax.Precision.HIGHEST)
    v_add = jnp.dot(r.qvb[1], hots32, precision=lax.Precision.HIGHEST)
    arrived(to_sib)

    @pl.loop(0, 4)
    def _(i):
        both = nn(r.xs[i].reshape(CTX_ROWS, D), r.wide[:, :, :, QKW:].reshape(D, 2 * QKW))
        mine = pl.ds(i * OWN_SEGS, OWN_SEGS)
        r.k[mine] = both[:, :QKW].astype(BF).reshape(OWN_SEGS, SEG, QKW)
        r.v[mine] = (both[:, QKW:] + v_add).astype(BF).reshape(OWN_SEGS, SEG, QKW)

    @pl.loop(0, 4)
    def _(i):
        wide_q = r.wide[:, :, :, :QKW].reshape(D, QKW)
        r.q[pl.ds(i * ROWS, ROWS), :] = (nn(r.xs[x, i], wide_q) + q_add).astype(BF)

    arrived(one_x)
    one_y = mail.ring(w1, *y_ring)
    arrived(two_z)
    two_x = mail.ring(w2, *x_ring)

    def climb(seg):
        r.trail[0] = seg
        depth = jnp.int32(0)
        here = seg
        for i in range(1, PATH):
            up = r.parents[0, here]
            found = up >= 0
            here = jnp.where(found, up, here)
            r.trail[i] = here
            depth = depth + found.astype(jnp.int32)
        return depth

    def on_path(depth, j):
        return r.trail[jnp.maximum(depth - j, 0)]

    def fetch_path(depth):
        for j in range(PATH):
            above = on_path(depth, j)
            r.kp[pl.ds(j * SEG, SEG), :] = r.k[above]
            r.vp[pl.ds(j * SEG, SEG), :] = r.v[above]

    arrived(tab_z2 + low_tab2 + to_low)

    def attend(a):
        depth = climb(x * OWN_SEGS + a)
        fetch_path(depth)
        mine = pl.ds(pl.multiple_of(a * SEG, SEG), SEG)
        tile = lax.rem(depth, 4) * 2
        for h in range(HEADS_DEV):
            head = slice(h * WIDE, (h + 1) * WIDE)
            low_q = r.q[mine, head] * jnp.asarray(SCALE, BF)
            flat = r.tab.at[h]
            pieces = [
                flat[lax.div(tile + i, 4), lax.rem(tile + i, 4)].astype(F32) for i in range(2)
            ]
            table = jnp.concatenate(pieces, axis=0)
            scores = nt(low_q, r.kp[:, head])
            parts = []
            for j in range(PATH):
                cols = slice((j % 4) * SEG, (j % 4 + 1) * SEG)
                score = scores[:, j * SEG : (j + 1) * SEG] + table[:, cols]
                parts.append(jnp.where(j <= depth, score, -1e30))
            scores = jnp.concatenate(parts, axis=1)
            peak = jnp.max(scores, axis=1, keepdims=True)
            raised = jnp.exp(scores - peak)
            whole = jnp.sum(raised, axis=1, keepdims=True)
            soft = (raised * (1.0 / whole)).astype(BF)
            r.p[a, h] = soft
            r.o_wide[mine, head] = nn(soft, r.vp[:, head]).astype(BF)

    pl.loop(0, 2)(attend)
    zero_z2 = mail.ring_on(w0, zero_z, *z_ring)
    pl.loop(2, 4)(attend)
    one_y2 = mail.ring_on(w1, one_y, *y_ring)
    two_x2 = mail.ring_on(w2, two_x, *x_ring)
    pl.loop(4, 5)(attend)
    r.o[...] = nt(r.o_wide[...], hots).astype(BF)
    o_far = [mail.post(r.o.at[pl.ds((1 - yh) * PAIR, PAIR)], r.o2.at[yh], far)]
    r.o2[yh] = r.o[pl.ds(yh * PAIR, PAIR), :]

    own, other = pl.ds(core * ROWS, ROWS), pl.ds((1 - core) * ROWS, ROWS)

    def trade_sum(slot):
        mail.done(mail.post(r.part.at[other], r.got.at[slot], sib))
        return r.part[own, :] + r.got[slot]

    def trade_rows(slot, values):
        r.rows[slot, own, :] = values
        arrived(mail.same(r.rows.at[slot, own], [sib]))

    def both_halves(left0, left1, weights):
        for half in range(2):
            cols = slice(half * 384, (half + 1) * 384)
            r.part[:, cols] = nt(left0, weights(0, half)) + nt(left1, weights(1, half))

    def tiles():
        return [(which, n) for which in range(2) for n in range(3)]

    def outer(which, half):
        return r.w[which, half, :, :, :D].reshape(384, D)

    def inner(which, half):
        return r.w[which, half, :, :, D:].reshape(384, D)

    arrived(o_y + o_far)
    both_halves(r.o2[0], r.o2[1], lambda a, b: r.wt[a, b, :, :, :QK].reshape(384, QK))
    n1, inv1 = normed(r.xs[x, tp].astype(F32) + trade_sum(0) + line(bo))
    r.n1s[...] = n1
    y1 = n1 * line(g1) + line(s1)
    r.y1s[...] = y1
    trade_rows(0, y1.astype(BF))
    arrived([*bias_far, *zero_z2, *one_y2, *two_x2])

    @pl.loop(0, 6)
    def _(i):
        which, col = lax.div(i, 3), pl.multiple_of(lax.rem(i, 3) * 256, 256)
        later = pl.multiple_of(col + D, 256)
        weight = r.w[which, :, :, :, pl.ds(later, 256)].reshape(D, 256)
        u = nn(r.rows[0], weight) + r.bias[which, :, pl.ds(col, 256)]
        phi = 0.5 * (1.0 + lax.erf(u * 0.7071067811865476))
        r.act[which, :, pl.ds(col, 256)] = (u * phi).astype(BF)
        slope = phi + u * (jnp.exp(-0.5 * u * u) * 0.3989422804014327)
        r.slope[pl.ds(pl.multiple_of(which * PAIR, PAIR), PAIR), pl.ds(col, 256)] = slope

    both_halves(r.act[0], r.act[1], outer)
    n2, inv2 = normed(r.y1s[...] + trade_sum(1) + line(bout))
    gain2 = line(g2)
    r.res[...] = (n2 * gain2 + line(s2)).astype(BF)
    c = r.cots[...].astype(F32)
    r.v_own[...] = jnp.zeros_like(r.v_own)
    r.v_own[4:5, :] = total(c * n2)
    r.v_own[5:6, :] = total(c)
    dh2 = normed_back(c, gain2, n2, inv2)
    r.dh2s[...] = dh2
    df = dh2.astype(BF)
    r.v_own[1:2, :] = total(df.astype(F32))
    trade_rows(1, df)

    @pl.loop(0, 6)
    def _(i):
        which, col = lax.div(i, 3), pl.multiple_of(lax.rem(i, 3) * 256, 256)
        weight = r.w[which, :, :, :, pl.ds(col, 256)].reshape(D, 256)
        slope = r.slope[pl.ds(pl.multiple_of(which * PAIR, PAIR), PAIR), pl.ds(col, 256)]
        grad = (nn(r.rows[1], weight) * slope).astype(BF)
        r.du[which, :, pl.ds(col, 256)] = grad
        r.v_own[pl.ds(6 + which, 1), pl.ds(col, 256)] = total(grad.astype(F32))

    mail.flush()
    both_halves(r.du[0], r.du[1], inner)
    c_dy = [mail.post(r.part.at[other], r.got.at[2], sib)]

    @pl.loop(0, 6)
    def _(i):
        which, col = lax.div(i, 3), pl.multiple_of(lax.rem(i, 3) * 256, 256)
        later = pl.multiple_of(col + D, 256)
        grad = tn(r.rows[1], r.act[which, :, pl.ds(col, 256)]).astype(BF)
        r.w[which, :, :, :, pl.ds(col, 256)] = grad.reshape(2, 4, 96, 256)
        grad = tn(r.rows[0], r.du[which, :, pl.ds(col, 256)]).astype(BF)
        r.w[which, :, :, :, pl.ds(later, 256)] = grad.reshape(2, 4, 96, 256)

    c0z = mail.fold(w0, r.r0z, *z_ring)
    c2x = mail.fold(w2, r.r2x, *x_ring)
    arrived(c_dy)
    dy1 = r.part[own, :] + r.got[2] + r.dh2s[...]
    n1 = r.n1s[...]
    r.v_own[2:3, :] = total(dy1 * n1)
    r.v_own[3:4, :] = total(dy1)
    dh1 = normed_back(dy1, line(g1), n1, inv1)
    r.dh1s[...] = dh1
    da = dh1.astype(BF)
    r.v_own[0:1, :] = total(da.astype(F32))
    trade_rows(2, da)
    leave = r.o.at[pl.ds(0, PAIR)]
    leave[...] = nn(r.rows[2], r.wt[1 - yh, :, :, :, :QK].reshape(D, QK)).astype(BF)
    back = [mail.post(leave, r.dout.at[pl.ds(yh * PAIR, PAIR)], far)]
    c1y = mail.fold(w1, r.r1y, *y_ring)
    r.dout[pl.ds(yh * PAIR, PAIR), :] = nn(r.rows[2], r.wt[yh, :, :, :, :QK].reshape(D, QK)).astype(BF)
    for which in range(2):
        grad = tn(r.rows[2], r.o2[which]).astype(BF)
        r.wt[which, :, :, :, :QK] = grad.reshape(2, 4, 96, QK)
    r.slope[...] = jnp.zeros_like(r.slope)
    r.tgp[...] = jnp.zeros_like(r.tgp)
    r.dtab[...] = jnp.zeros_like(r.dtab)
    for b in range(SEGS):
        r.depths[b] = climb(jnp.int32(b))
    arrived(back)
    coz = mail.spread(lambda k: r.wt.at[:, :, around(z, k)], r.roz, zp)

    def spot(h, b):
        n = h * SEGS + b
        return slice(n // 6 * 64, n // 6 * 64 + 64), slice(n % 6 * 128, n % 6 * 128 + 128)

    def attend_back(a, heads):
        depth = climb(x * OWN_SEGS + a)
        fetch_path(depth)
        mine = pl.ds(pl.multiple_of(a * SEG, SEG), SEG)
        tile = lax.rem(depth, 4)
        grads = nn(r.dout[mine, :], hots).astype(BF)
        for h in heads:
            head = slice(h * WIDE, (h + 1) * WIDE)
            low_q, grad = r.q[mine, head], grads[:, head]
            soft = r.p[a, h]
            inside = grad.astype(F32) * r.o_wide[mine, head].astype(F32)
            ds = soft.astype(F32) * (
                nt(grad, r.vp[:, head]) - jnp.sum(inside, axis=1, keepdims=True)
            )
            ds_low = ds.astype(BF)
            r.dq_wide[mine, head] = (nn(ds_low, r.kp[:, head]) * SCALE).astype(BF)
            q_t = (low_q.astype(F32).T[:HEAD_DIM] * SCALE).astype(BF)
            grad_t = grad.astype(F32).T[:HEAD_DIM].astype(BF)
            dk_part, dv_part = nn(q_t, ds_low), nn(grad_t, soft)
            for j in range(PATH):
                r.parts[0, j] = dk_part[:, j * SEG : (j + 1) * SEG]
                r.parts[1, j] = dv_part[:, j * SEG : (j + 1) * SEG]
            for b in range(SEGS):
                down = r.depths[b]
                held = (down <= depth) & (on_path(depth, down) == b)
                rows, cols = spot(h, b)
                r.slope[rows, cols] += jnp.where(held, r.parts[0, down], 0.0)
                r.tgp[rows, cols] += jnp.where(held, r.parts[1, down], 0.0)
            fall = ds_low.astype(F32)
            left = fall[:, 0:256] + fall[:, 512:768] + fall[:, 1024:1280]
            right = fall[:, 256:512] + fall[:, 768:1024]
            for t in range(4):
                span = slice(t * SEG, (t + 1) * SEG)
                r.dtab[h, span, 0:256] += jnp.where(tile == t, left, 0.0)
                r.dtab[h, span, 256:512] += jnp.where(tile == t, right, 0.0)

    def settle_heads(heads):
        for h in heads:
            for b in range(SEGS):
                rows, cols = spot(h, b)
                into = slice(b % 5 * SEG, (b % 5 + 1) * SEG)
                r.p[b // 5, h, 0:64, into] = r.slope[rows, cols].astype(BF)
                r.p[b // 5, h, 64:128, into] = r.tgp[rows, cols].astype(BF)
            r.tab[h] = r.dtab[h].astype(BF).reshape(2, 4, 64, DEPTHS)

    def dkv(first, count):
        def view(k, half):
            span = (pl.ds(half * 64, 64), pl.ds(0, CTX_ROWS))
            return r.p.at[around(x, k), pl.ds(first, count), *span]

        return view

    c0z = mail.fold_on(w0, r.r0z, c0z, *z_ring)
    c2x = mail.fold_on(w2, r.r2x, c2x, *x_ring)
    pl.loop(0, OWN_SEGS)(lambda a: attend_back(a, (0, 1)))
    settle_heads((0, 1))
    c_dka = mail.fold(dkv(0, 2), r.r_dka, *x_ring)
    d0z = mail.spread(lambda k: r.tab.at[0, :, around(z, k)], r.t0z, zp)
    d1y = mail.post(r.tab.at[1, 1 - yl], r.t1y, low)
    pl.loop(0, OWN_SEGS)(lambda a: attend_back(a, (2,)))
    settle_heads((2,))
    c_dkb = mail.fold(dkv(2, 1), r.r_dkb, *x_ring)
    d2y = mail.post(r.tab.at[2, 1 - yl], r.t2y, low)

    def weight_of(j):
        return r.ws[:, j].reshape(D, QK)

    def quarter(a, b):
        return pl.ds((a * 2 + b) * ROWS, ROWS)

    late = []

    def settle(ref, base, values):
        ref[:, lanes(base, 0)] = values.astype(BF)
        late.extend(mail.same(ref.at[:, lanes(base, 0)], xp))

    q_low = nt(r.dq_wide[...], hots).astype(BF)
    grad = tn(r.xs[x].reshape(CTX_ROWS, D), q_low).astype(BF)
    r.wide[:, :, :, 0:QK] = grad.reshape(2, 4, 96, QK)
    for i in range(4):
        both = r.p[i, :, :, 0:CTX_ROWS].reshape(2 * QK, CTX_ROWS)
        term = nn(both, r.xs[i].reshape(CTX_ROWS, D))
        r.kv_t[...] = term if i == 0 else r.kv_t[...] + term
    r.wide[:, :, :, QKP : QKP + QKW] = r.kv_t[...].T.astype(BF).reshape(2, 4, 96, QKW)
    cqz = mail.spread(lambda k: r.wide.at[:, around(z, k), :, pl.ds(0, QKV)], r.rqz, zp)
    r.v_own[pl.ds(8 + yh, 1), 0:QK] = total(q_low.astype(F32))
    ones = jnp.ones((8, CTX_ROWS), BF)
    sums = [nt(ones, r.p[i, :, 64:128, 0:CTX_ROWS].reshape(QK, CTX_ROWS)) for i in range(4)]
    r.v_own[pl.ds(10 + yh, 1), 0:QK] = (sums[0] + sums[1] + sums[2] + sums[3])[0:1]
    c_dka = mail.fold_on(dkv(0, 2), r.r_dka, c_dka, *x_ring)
    r.vx[x] = r.v_own[...]
    c_vx = mail.same(r.vx.at[x], xp)
    c1y = mail.fold_on(w1, r.r1y, c1y, *y_ring)
    arrived(c0z)
    for half in range(2):
        r.s0z[half : half + 1] = folded(w0, r.r0z, half).astype(BF)
    c0y = mail.spread(lambda k: r.s0z.at[ys[k][0], ys[k][1]], r.r0y, yp)
    arrived(c2x)
    for half in range(2):
        r.s2x[half : half + 1] = folded(w2, r.r2x, half).astype(BF)
    c2z = mail.spread(lambda k: r.s2x.at[:, :, around(z, k)], r.r2z, zp)
    arrived(coz)
    r.soz[...] = added(r.wt[:, :, z], r.roz).astype(BF)
    coy = mail.spread(lambda k: r.soz.at[ys[k][0], ys[k][1]], r.roy, yp)
    arrived(d0z)
    r.u0z[...] = added(r.tab[0, :, z], r.t0z).astype(BF)
    d0y = mail.post(r.u0z.at[1 - yl], r.t0y, low)
    arrived([d1y])
    r.u1y[...] = (r.tab[1, yl].astype(F32) + r.t1y[...].astype(F32)).astype(BF)
    d1x = mail.spread(lambda k: r.u1y.at[:, :, lanes(0, k)], r.t1x, xp)
    r.tgp[...] = nt(q_low, weight_of(0))
    c_dkb = mail.fold_on(dkv(2, 1), r.r_dkb, c_dkb, *x_ring)
    arrived(c_vx)
    r.vz[z] = slots_total(r.vx)
    c_vz = mail.same(r.vz.at[z], zp)
    arrived([d2y])
    r.u2y[...] = (r.tab[2, yl].astype(F32) + r.t2y[...].astype(F32)).astype(BF)
    d2z = mail.spread(lambda k: r.u2y.at[around(z, k)], r.t2z, zp)
    arrived(c1y)
    for half in range(2):
        r.s1y[half * 2 : half * 2 + 2] = folded(w1, r.r1y, half).astype(BF)
    c1x = mail.spread(lambda k: r.s1y.at[:, :, lanes(0, k)], r.r1x, xp)

    arrived(c_dka + c_dkb)
    k_low, v_low = (
        jnp.concatenate(
            [
                folded(dkv(0, 2), r.r_dka, half).reshape(2 * 64, CTX_ROWS),
                folded(dkv(2, 1), r.r_dkb, half).reshape(64, CTX_ROWS),
            ],
            axis=0,
        ).T.astype(BF)
        for half in range(2)
    )
    r.tgp[...] += nt(k_low, weight_of(1)) + nt(v_low, weight_of(2))
    c_sib = [mail.post(r.tgp.at[quarter(a, 1 - core)], r.got.at[a], sib) for a in range(2)]
    arrived(coy)
    r.rox[x] = added(r.soz[yh, yl], r.roy).astype(BF)
    cox = mail.same(r.rox.at[x], xp)
    arrived(c0y)
    r.s0y[...] = added(r.s0z[yh, yl], r.r0y).astype(BF)
    c0x = mail.spread(lambda k: r.s0y.at[:, lanes(0, k)], r.r0x, xp)
    arrived([d0y])
    r.u0y[...] = (r.u0z[yl].astype(F32) + r.t0y[...].astype(F32)).astype(BF)
    d0x = mail.spread(lambda k: r.u0y.at[:, lanes(0, k)], r.t0x, xp)
    arrived(c_sib)
    s_far = r.rows.at[0, pl.ds(0, ROWS)]
    s_far[...] = (r.tgp[quarter(1 - yh, core), :] + r.got[1 - yh]).astype(BF)
    c_far = [mail.post(s_far, r.r_far, far)]

    arrived(cqz)
    r.sqz[...] = added(r.wide[:, z, :, 0:QKV], r.rqz).astype(BF)
    cqy = mail.post(r.sqz.at[1 - yl], r.rqy, low)
    arrived(d1x)
    r.u1x[...] = added(r.u1y[:, :, lanes(0, 0)], r.t1x).astype(BF)
    d1z = mail.spread(lambda k: r.u1x.at[around(z, k)], r.t1z, zp)
    arrived(c2z)
    r.s2z[...] = added(r.s2x[:, :, z], r.r2z).astype(BF)
    c2y = mail.spread(lambda k: r.s2z.at[ys[k][0], ys[k][1]], r.r2y, yp)
    arrived(c_vz)
    r.vy[y] = slots_total(r.vz)
    c_vy = mail.same(r.vy.at[y], yp)
    arrived(c1x)
    r.s1x[...] = added(r.s1y[:, :, lanes(0, 0)], r.r1x).astype(BF)
    c1z = mail.spread(lambda k: r.s1x.at[around(z, k)], r.r1z, zp)
    arrived(d2z)
    r.u2z[...] = added(r.u2y[z], r.t2z).astype(BF)
    d2x = mail.spread(lambda k: r.u2z.at[:, lanes(0, k)], r.t2x, xp)
    arrived(c0x)
    settle(r.f, 0, added(r.s0y[:, lanes(0, 0)], r.r0x))
    arrived(d0x)
    settle(r.ft.at[0], 0, added(r.u0y[:, lanes(0, 0)], r.t0x))
    arrived([cqy])
    r.rqx[x] = (r.sqz[yl].astype(F32) + r.rqy[...].astype(F32)).astype(BF)
    cqx = mail.same(r.rqx.at[x], xp)

    arrived(d1z)
    settle(r.ft.at[1], 0, added(r.u1x[z], r.t1z))
    arrived(c2y)
    settle(r.f, 1024, added(r.s2z[yh, yl], r.r2y))
    arrived(c1z)
    settle(r.f, 512, added(r.s1x[z], r.r1z))
    arrived(d2x)
    settle(r.ft.at[2], 0, added(r.u2z[:, lanes(0, 0)], r.t2x))
    arrived(c_vy)
    r.vc[0] = slots_total(r.vy)
    c_vc = mail.post(r.vc.at[0], r.vc.at[1], sib)
    arrived(cox)
    r.fo[...] = slots_total(r.rox)
    arrived(c_far)
    r.tg[...] = r.tgp[quarter(yh, core), :] + r.got[yh] + r.r_far[...].astype(F32) + r.dh1s[...]
    arrived(cqx)
    r.fq[...] = slots_total(r.rqx)
    arrived([c_vc])
    r.vsum[...] = r.vc[0]
    r.vsum[0:6, :] = r.vc[0, 0:6, :] + r.vc[1, 0:6, :]
    arrived(late)
    mail.flush()
    assert mail.used <= POSTS


def layer(*arrays):
    vm = pl.BlockSpec(memory_space=pltpu.VMEM)
    hbm = pl.BlockSpec(memory_space=pltpu.HBM)
    return pl.pallas_call(
        layer_kernel,
        out_shape=tuple(jax.ShapeDtypeStruct(*entry) for entry in OUTPUTS.values()),
        in_specs=[pl.BlockSpec(memory_space=pltpu.SMEM)] + [hbm] * (len(INPUTS) - 1),
        out_specs=[vm] * len(OUTPUTS),
        scratch_shapes=[
            *(pltpu.VMEM(*entry) for entry in SCRATCH.values()),
            pltpu.SMEM((PATH,), jnp.int32),
            pltpu.SMEM((SEGS,), jnp.int32),
            pltpu.SemaphoreType.DMA((20,)),
            pltpu.SemaphoreType.DMA((POSTS,)),
            pltpu.SemaphoreType.DMA((POSTS,)),
        ],
        compiler_params=pltpu.CompilerParams(
            collective_id=1, has_side_effects=True, vmem_limit_bytes=60 * MIB
        ),
        name="layer",
    )(*arrays)


def finish_kernel(*refs):
    f_in, fo_in, fq_in, ft_in, tg, vsum_in, res, logits_in, noise_in = refs[:9]
    res_out, tg_out, gwq, gwk, gwv, gwo, gwi, gwout_t, mask, gbq, gbv, *lines = refs[9:-8]
    f, fo, fq, ft, vsum, logits, noise, sem = refs[-8:]
    pairs = [
        (res, res_out),
        (tg, tg_out),
        (f_in, f),
        (fo_in, fo),
        (fq_in, fq),
        (ft_in, ft),
        (vsum_in, vsum),
        (logits_in, logits),
        (noise_in, noise),
    ]
    copies = [pltpu.make_async_copy(src, dst, sem.at[n]) for n, (src, dst) in enumerate(pairs)]
    for copy in copies:
        copy.start()
    for copy in copies[2:]:
        copy.wait()
    gwq[...] = fq[:, :QK]
    rows = lax.broadcasted_iota(jnp.int32, (QKW, QK), 0)
    cols = lax.broadcasted_iota(jnp.int32, (QKW, QK), 1)
    wanted = cols // HEAD_DIM * WIDE + cols % HEAD_DIM
    for out, shift in ((gwk, 0), (gwv, HEAD_DIM)):
        pick = (rows == wanted + shift).astype(F32)
        out[...] = jnp.dot(fq[:, QKP:], pick, precision=lax.Precision.HIGHEST)
    gwo[...] = fo[...].T[:QK]
    gwout_t[...] = f[:, :D].astype(F32)
    gwi[...] = f[:, D:].astype(F32)
    mask[...] = ft[...].astype(F32) * jax.nn.sigmoid(-(logits[...] + noise[...]))
    yh = lax.div(lax.axis_index("tp"), 2)
    gbq[...] = vsum[pl.ds(8 + yh, 1), 0:QK]
    gbv[...] = vsum[pl.ds(10 + yh, 1), 0:QK]
    for n, out in enumerate(lines):
        row = vsum[pl.ds(6 + yh, 1), :] if n == 6 else vsum[n : n + 1, :]
        for i in range(6):
            out[i : i + 1, :] = row[:, i * 128 : (i + 1) * 128]
    for copy in copies[:2]:
        copy.wait()


def finish(f, fo, fq, ft, tg, vsum, res, logits, noise):
    shape = jax.ShapeDtypeStruct
    vm = pl.BlockSpec(memory_space=pltpu.VMEM)
    hbm = pl.BlockSpec(memory_space=pltpu.HBM)
    outs = (
        shape((ROWS, D), BF),
        shape((ROWS, D), F32),
        shape((96, QK), F32),
        shape((96, QK), F32),
        shape((96, QK), F32),
        shape((QK, 96), F32),
        shape((96, D), F32),
        shape((96, D), F32),
        shape((HEADS_DEV, 64, DEPTHS), F32),
        shape((1, QK), F32),
        shape((1, QK), F32),
        *[shape((6, 128), F32)] * 7,
    )
    held = (f, fo, fq, ft, vsum, logits, noise)
    return pl.pallas_call(
        finish_kernel,
        out_shape=outs,
        in_specs=[hbm] * 9,
        out_specs=[vm] * len(outs),
        scratch_shapes=[
            *(pltpu.VMEM(entry.shape, entry.dtype) for entry in held),
            pltpu.SemaphoreType.DMA((9,)),
        ],
        compiler_params=pltpu.CompilerParams(vmem_limit_bytes=60 * MIB),
        name="finish",
    )(f, fo, fq, ft, tg, vsum, res, logits, noise)


def shards(
    tokens,
    parents,
    query_weight,
    query_bias,
    key_weight,
    value_weight,
    value_bias,
    output_weight,
    output_bias,
    first_gain,
    first_shift,
    inner_weight,
    inner_bias,
    outer_weight,
    outer_bias,
    second_gain,
    second_shift,
    mask_logits,
    mask_noise,
    cotangent,
):
    def lined(vector):
        return vector.reshape(6, 128)

    res, tg, f, fo, fq, ft, vsum = layer(
        parents,
        tokens,
        cotangent,
        query_weight,
        key_weight,
        value_weight,
        query_bias.reshape(1, QK),
        value_bias.reshape(1, QK),
        mask_logits,
        mask_noise,
        output_weight,
        inner_weight,
        outer_weight.T,
        lined(output_bias),
        lined(first_gain),
        lined(first_shift),
        lined(inner_bias),
        lined(outer_bias),
        lined(second_gain),
        lined(second_shift),
    )
    result, tg, gwq, gwk, gwv, gwo, gwi, gwout_t, mask, gbq, gbv, *lines = finish(
        f, fo, fq, ft, tg, vsum, res, mask_logits, mask_noise
    )
    bo, bout, g1, s1, g2, s2, bi = [entry.reshape(D) for entry in lines]
    return (
        result,
        tg,
        gwq,
        gbq.reshape(QK),
        gwk,
        gwv,
        gbv.reshape(QK),
        gwo,
        bo,
        g1,
        s1,
        gwi,
        bi,
        gwout_t.T,
        bout,
        g2,
        s2,
        mask,
    )


def solution(mesh):
    in_specs = (
        P(("shard", "ctx", "tp"), None),
        P("shard", None),
        P("shard", "tp"),
        P("tp"),
        P("shard", "tp"),
        P("shard", "tp"),
        P("tp"),
        P("tp", "shard"),
        P(),
        P(),
        P(),
        P("shard", "tp"),
        P("tp"),
        P("tp", "shard"),
        P(),
        P(),
        P(),
        P("tp", "shard", None),
        P("tp", "shard", None),
        P(("shard", "ctx", "tp"), None),
    )
    out_specs = (
        P(("shard", "ctx", "tp"), None),
        P(("shard", "ctx", "tp"), None),
        P("shard", "tp"),
        P("tp"),
        P("shard", "tp"),
        P("shard", "tp"),
        P("tp"),
        P("tp", "shard"),
        P(),
        P(),
        P(),
        P("shard", "tp"),
        P("tp"),
        P("tp", "shard"),
        P(),
        P(),
        P(),
        P("tp", "shard", None),
    )
    return jax.shard_map(shards, mesh=mesh, in_specs=in_specs, out_specs=out_specs, check_vma=False)
```

```python
import jax
import jax.numpy as jnp
from jax import lax
from jax.experimental import pallas as pl
from jax.experimental.pallas import tpu as pltpu
from jax.sharding import PartitionSpec as P

MESH = pl.DeviceIdType.MESH
BF = jnp.bfloat16
F32 = jnp.float32
HEADS_DEV = 3
HEAD_DIM = 64
WIDE = 128
SEG = 128
SEGS = 20
OWN_SEGS = 5
PATH = 10
KEYS = PATH * SEG
D = 768
QK = 192
QKP = 256
QKW = 384
QKV = QKP + QKW
ROWS = 160
PAIR = 320
CTX_ROWS = 640
TREE = 2560
DEPTHS = 512
MIB = 2**20
SCALE = HEAD_DIM**-0.5
STEPS = (1, 2, 3)


def place():
    shard = lax.axis_index("shard")
    tp = lax.axis_index("tp")
    return {
        "x": lax.axis_index("ctx"),
        "yl": lax.div(shard, 4),
        "z": lax.rem(shard, 4),
        "yh": lax.div(tp, 2),
        "core": lax.rem(tp, 2),
    }


def ident(at, **moved):
    to = {**at, **moved}
    return {"shard": to["yl"] * 4 + to["z"], "ctx": to["x"], "tp": to["yh"] * 2 + to["core"]}


def around(value, step):
    return lax.rem(value + step, 4)


def greet(devices):
    barrier = pltpu.get_barrier_semaphore()
    for device in devices:
        pl.semaphore_signal(barrier, inc=1, device_id=device, device_id_type=MESH)
    pl.semaphore_wait(barrier, len(devices))


class Mail:
    def __init__(self, send, recv):
        self.send, self.recv, self.used, self.sent = send, recv, 0, []

    def post(self, src, dst, device):
        copy = pltpu.make_async_remote_copy(
            src_ref=src,
            dst_ref=dst,
            send_sem=self.send.at[self.used],
            recv_sem=self.recv.at[self.used],
            device_id=device,
            device_id_type=MESH,
        )
        self.used += 1
        copy.start()
        self.sent.append(copy)
        return copy

    def same(self, ref, devices):
        return [self.post(ref, ref, device) for device in devices]

    def spread(self, view, landing, devices):
        return [self.post(view(k), landing.at[k - 1], devices[k - 1]) for k in STEPS]

    def ring(self, view, ahead, behind):
        return [self.post(view(0), view(0), ahead), self.post(view(0), view(0), behind)]

    def ring_on(self, view, first, ahead, behind):
        arrived(first[:1])
        onward = [self.post(view(3, 0), view(3, 0), ahead)]
        arrived(first[1:])
        return onward + [self.post(view(1, 1), view(1, 1), behind)]

    def fold(self, view, landing, ahead, behind):
        return [
            self.post(view(2, 0), landing.at[0], ahead),
            self.post(view(2, 1), landing.at[1], behind),
            self.post(view(1, 1), landing.at[3], ahead),
            self.post(view(3, 0), landing.at[4], behind),
        ]

    def fold_on(self, view, landing, first, ahead, behind):
        out = first[2:]
        for half, k, slot, device in ((0, 1, 2, ahead), (1, 3, 5, behind)):
            arrived(first[half : half + 1])
            term = view(k, half)
            term[...] = (term[...].astype(F32) + landing[half].astype(F32)).astype(BF)
            out.append(self.post(term, landing.at[slot], device))
        return out

    def done(self, copy):
        copy.wait()
        self.sent = [kept for kept in self.sent if kept is not copy]

    def flush(self):
        for copy in self.sent:
            copy.wait_send()
        self.sent = []


def arrived(copies):
    for copy in copies:
        copy.wait_recv()


def nn(a, b):
    return jnp.dot(a, b, preferred_element_type=F32)


def nt(a, b):
    return lax.dot_general(a, b, (((1,), (1,)), ((), ())), preferred_element_type=F32)


def tn(a, b):
    return lax.dot_general(a, b, (((0,), (0,)), ((), ())), preferred_element_type=F32)


def spread_heads(kind=BF):
    rows = lax.broadcasted_iota(jnp.int32, (QK, QKW), 0)
    cols = lax.broadcasted_iota(jnp.int32, (QK, QKW), 1)
    head, lane = cols // WIDE, cols % WIDE
    return ((head * HEAD_DIM + lane == rows) & (lane < HEAD_DIM)).astype(kind)


def unit(rows_count, cols_count):
    rows = lax.broadcasted_iota(jnp.int32, (rows_count, cols_count), 0)
    cols = lax.broadcasted_iota(jnp.int32, (rows_count, cols_count), 1)
    return (rows == cols).astype(BF)


def line(ref):
    return jnp.concatenate([ref[i : i + 1, :] for i in range(6)], axis=1)


def normed(values):
    centre = jnp.mean(values, axis=1, keepdims=True)
    off = values - centre
    inverse = lax.rsqrt(jnp.mean(off * off, axis=1, keepdims=True) + 1e-5)
    return off * inverse, inverse


def normed_back(grad, gain, n, inverse):
    e = grad * gain
    return inverse * (e - jnp.mean(e, axis=1, keepdims=True) - n * jnp.mean(e * n, axis=1, keepdims=True))


def total(values):
    return jnp.sum(values, axis=0, keepdims=True)


def added(own, landing, count=3):
    out = own.astype(F32)
    for i in range(count):
        out = out + landing[i].astype(F32)
    return out


def folded(view, landing, half):
    near = landing[2 + half].astype(F32) + landing[4 + half].astype(F32)
    return view(0, half)[...].astype(F32) + near


def slots_total(slots):
    return slots[0].astype(F32) + slots[1].astype(F32) + slots[2].astype(F32) + slots[3].astype(F32)


INPUTS = (
    "parents",
    "tok",
    "cot",
    "wq",
    "wk",
    "wv",
    "qb",
    "vb",
    "logits",
    "noise",
    "wo",
    "wi",
    "wout_t",
    "bo",
    "g1",
    "s1",
    "bi",
    "bout",
    "g2",
    "s2",
)
OUTPUTS = {
    "res": ((ROWS, D), BF),
    "tg": ((ROWS, D), F32),
    "f": ((96, 2 * D), BF),
    "fo": ((96, QKP), F32),
    "fq": ((96, QKV), F32),
    "ft": ((HEADS_DEV, 64, DEPTHS), BF),
    "vsum": ((16, D), F32),
}
SCRATCH = {
    "cots": ((ROWS, D), BF),
    "lines": ((7, 6, 128), F32),
    "qvb": ((2, 1, QK), F32),
    "wos": ((QK, 96), BF),
    "masks": ((2, HEADS_DEV, 64, DEPTHS), F32),
    "xs": ((4, 4, ROWS, D), BF),
    "ws": ((8, 3, 96, QK), BF),
    "wide": ((2, 4, 96, 3 * QKW), BF),
    "q": ((CTX_ROWS, QKW), BF),
    "k": ((SEGS, SEG, QKW), BF),
    "v": ((SEGS, SEG, QKW), BF),
    "tab": ((HEADS_DEV, 2, 4, 64, DEPTHS), BF),
    "kp": ((KEYS, QKW), BF),
    "vp": ((KEYS, QKW), BF),
    "p": ((OWN_SEGS, HEADS_DEV, SEG, KEYS), BF),
    "o_wide": ((CTX_ROWS, QKW), BF),
    "o": ((CTX_ROWS, QK), BF),
    "w": ((2, 2, 4, 96, 2 * D), BF),
    "wt": ((2, 2, 4, 96, QKP), BF),
    "o2": ((2, PAIR, QK), BF),
    "bias": ((2, 1, D), F32),
    "part": ((PAIR, D), F32),
    "got": ((3, ROWS, D), F32),
    "rows": ((3, PAIR, D), BF),
    "act": ((2, PAIR, D), BF),
    "slope": ((CTX_ROWS, D), F32),
    "du": ((2, PAIR, D), BF),
    "y1s": ((ROWS, D), F32),
    "n1s": ((ROWS, D), F32),
    "dh2s": ((ROWS, D), F32),
    "dh1s": ((ROWS, D), F32),
    "dout": ((CTX_ROWS, QK), BF),
    "parts": ((2, PATH, HEAD_DIM, SEG), F32),
    "dtab": ((HEADS_DEV, DEPTHS, DEPTHS), F32),
    "dq_wide": ((CTX_ROWS, QKW), BF),
    "tgp": ((CTX_ROWS, D), F32),
    "r_dka": ((6, 2, 64, CTX_ROWS), BF),
    "r_dkb": ((6, 1, 64, CTX_ROWS), BF),
    "kv_t": ((2 * QK, D), F32),
    "r0z": ((6, 1, 2, 96, 512), BF),
    "s0z": ((2, 2, 96, 512), BF),
    "r0y": ((3, 96, 512), BF),
    "s0y": ((96, 512), BF),
    "r0x": ((3, 96, 128), BF),
    "r1y": ((6, 2, 96, 512), BF),
    "s1y": ((4, 96, 512), BF),
    "r1x": ((3, 4, 96, 128), BF),
    "s1x": ((4, 96, 128), BF),
    "r1z": ((3, 96, 128), BF),
    "r2x": ((6, 1, 2, 4, 96, 128), BF),
    "s2x": ((2, 2, 4, 96, 128), BF),
    "r2z": ((3, 2, 2, 96, 128), BF),
    "s2z": ((2, 2, 96, 128), BF),
    "r2y": ((3, 96, 128), BF),
    "t0z": ((3, 2, 64, 512), BF),
    "u0z": ((2, 64, 512), BF),
    "t0y": ((64, 512), BF),
    "u0y": ((64, 512), BF),
    "t0x": ((3, 64, 128), BF),
    "t1y": ((4, 64, 512), BF),
    "u1y": ((4, 64, 512), BF),
    "t1x": ((3, 4, 64, 128), BF),
    "u1x": ((4, 64, 128), BF),
    "t1z": ((3, 64, 128), BF),
    "t2y": ((4, 64, 512), BF),
    "u2y": ((4, 64, 512), BF),
    "t2z": ((3, 64, 512), BF),
    "u2z": ((64, 512), BF),
    "t2x": ((3, 64, 128), BF),
    "roz": ((3, 2, 2, 96, QKP), BF),
    "soz": ((2, 2, 96, QKP), BF),
    "roy": ((3, 96, QKP), BF),
    "rox": ((4, 96, QKP), BF),
    "rqz": ((3, 2, 96, QKV), BF),
    "sqz": ((2, 96, QKV), BF),
    "rqy": ((96, QKV), BF),
    "rqx": ((4, 96, QKV), BF),
    "r_far": ((ROWS, D), BF),
    "v_own": ((16, D), F32),
    "vx": ((4, 16, D), F32),
    "vz": ((4, 16, D), F32),
    "vy": ((4, 16, D), F32),
    "vc": ((2, 16, D), F32),
}
POSTS = 260


class Names:
    pass


def layer_kernel(*refs):
    r = Names()
    names = [*INPUTS, *OUTPUTS, *SCRATCH, "trail", "depths", "fetch", "send", "recv"]
    for name, ref in zip(names, refs, strict=True):
        setattr(r, name, ref)
    at = place()
    x, yl, z, yh, core = at["x"], at["yl"], at["z"], at["yh"], at["core"]
    shard, tp, y = yl * 4 + z, yh * 2 + core, yh * 2 + yl
    sib = ident(at, core=1 - core)
    far = ident(at, yh=1 - yh)
    low = ident(at, yl=1 - yl)
    xp = [ident(at, x=around(x, k)) for k in STEPS]
    zp = [ident(at, z=around(z, k)) for k in STEPS]
    ys = [(lax.div(around(y, k), 2), lax.rem(around(y, k), 2)) for k in (0, 1, 2, 3)]
    yp = [ident(at, yh=a, yl=b) for a, b in ys[1:]]
    x_ring, y_ring, z_ring = (xp[0], xp[2]), (yp[0], yp[2]), (zp[0], zp[2])
    mail = Mail(r.send, r.recv)

    def lanes(base, k):
        return pl.ds(pl.multiple_of(base + around(x, k) * 128, 128), 128)

    def halves(size, half):
        return pl.ds(0, size) if half is None else pl.ds(half * size // 2, size // 2)

    def tok_own(k, half=None):
        return r.xs.at[around(x, k), tp, halves(ROWS, half)]

    def tok_far(k, half=None):
        return r.xs.at[around(x, k), (1 - yh) * 2 + core, halves(ROWS, half)]

    def ws_of(side):
        return lambda k, half=None: r.ws.at[side * 4 + around(z, k), :, halves(96, half)]

    def tab_of(side):
        return lambda k, half=None: r.tab.at[halves(2, half), side, around(z, k)]

    def tab_last(k, half=None):
        return r.tab.at[2, yl, around(z, k), halves(64, half)]

    def w0(k, half=None):
        return r.w.at[halves(2, half), :, around(z, k), :, pl.ds(0, 512)]

    def w1(k, half=None):
        return r.w.at[ys[k][0], ys[k][1], halves(4, half), :, pl.ds(512, 512)]

    def w2(k, half=None):
        return r.w.at[halves(2, half), :, :, :, lanes(1024, k)]

    def bring(n, src, dst):
        copy = pltpu.make_async_copy(src, dst, r.fetch.at[n])
        copy.start()
        return copy

    def brought(copies):
        for copy in copies:
            copy.wait()

    get_tok = [bring(0, r.tok, tok_own(0))]
    get_ws = [bring(1 + j, w, r.ws.at[shard, j]) for j, w in enumerate((r.wq, r.wk, r.wv))]
    get_masks = [bring(4 + j, m, r.masks.at[j]) for j, m in enumerate((r.logits, r.noise))]
    get_w = [
        bring(6, r.wout_t, r.w.at[yh, yl, z, :, pl.ds(0, D)]),
        bring(7, r.wi, r.w.at[yh, yl, z, :, pl.ds(D, D)]),
        bring(8, r.wo, r.wos),
    ]
    vectors = (r.bo, r.g1, r.s1, r.bi, r.bout, r.g2, r.s2)
    get_rest = [bring(9 + j, v, r.lines.at[j]) for j, v in enumerate(vectors)]
    get_rest += [bring(16, r.cot, r.cots), bring(17, r.qb, r.qvb.at[0]), bring(18, r.vb, r.qvb.at[1])]
    bo, g1, s1, bi, bout, g2, s2 = [r.lines.at[j] for j in range(7)]
    greet([sib, *xp, *zp, *yp])
    brought(get_tok)
    first_far = mail.same(tok_own(0), [far])
    own_x = mail.ring(tok_own, *x_ring)
    to_sib = mail.same(tok_own(0), [sib])
    brought(get_ws)
    own_low = mail.same(r.ws.at[shard], [low])
    own_z = mail.ring(ws_of(yl), *z_ring)
    brought(get_masks)
    r.tab[:, yl, z] = jax.nn.log_sigmoid(r.masks[0] + r.masks[1]).astype(BF)
    tab_low = mail.same(tab_of(yl)(0), [low])
    to_low = mail.same(tab_last(0), [low])
    tab_z = mail.ring(tab_of(yl), *z_ring)
    last_z = mail.ring(tab_last, *z_ring)
    brought(get_w + get_rest)
    r.wt[yh, yl, z] = jnp.concatenate(
        [nt(unit(96, 96), r.wos[...]).astype(BF), jnp.zeros((96, QKP - QK), BF)], axis=1
    )
    r.bias[yh] = line(bi)
    one_z = mail.same(r.w.at[yh, yl, z, :, lanes(512, 0)], zp)
    o_z = mail.same(r.wt.at[yh, yl, z], zp)
    two_y = mail.same(r.w.at[yh, yl, z, :, lanes(1024, 0)], yp)
    zero_y = mail.same(r.w.at[yh, yl, z, :, pl.ds(0, 512)], yp)
    bias_far = mail.same(r.bias.at[yh], [far])
    arrived(first_far)
    far_x = mail.ring(tok_far, *x_ring)
    to_sib += mail.same(tok_far(0), [sib])
    arrived(own_low)
    low_z = mail.ring(ws_of(1 - yl), *z_ring)
    own_z2 = mail.ring_on(ws_of(yl), own_z, *z_ring)
    arrived(tab_low)
    low_tab = mail.ring(tab_of(1 - yl), *z_ring)
    own_x2 = mail.ring_on(tok_own, own_x, *x_ring)
    to_sib += mail.same(tok_own(1), [sib]) + mail.same(tok_own(3), [sib])
    low_z2 = mail.ring_on(ws_of(1 - yl), low_z, *z_ring)
    far_x2 = mail.ring_on(tok_far, far_x, *x_ring)
    to_sib += mail.same(tok_far(1), [sib]) + mail.same(tok_far(3), [sib])
    arrived(own_x2)
    to_sib += mail.same(tok_own(2), [sib])
    tab_z2 = mail.ring_on(tab_of(yl), tab_z, *z_ring)
    last_z2 = mail.ring_on(tab_last, last_z, *z_ring)
    to_low += mail.same(tab_last(1), [low]) + mail.same(tab_last(3), [low])
    arrived(two_y)
    two_z = mail.same(r.w.at[:, :, z, :, lanes(1024, 0)], zp)
    arrived(o_z)
    o_y = mail.same(r.wt.at[yh, yl], yp)
    arrived(far_x2)
    to_sib += mail.same(tok_far(2), [sib])
    arrived(one_z)
    one_x = mail.same(r.w.at[yh, yl, :, :, lanes(512, 0)], xp)
    arrived(own_z2 + low_z2)
    low_tab2 = mail.ring_on(tab_of(1 - yl), low_tab, *z_ring)
    arrived(last_z2)
    to_low += mail.same(tab_last(2), [low])
    arrived(zero_y)
    zero_z = mail.ring(w0, *z_ring)

    hots = spread_heads()
    hots32 = spread_heads(F32)
    for j in range(3):
        full = r.ws[:, j].reshape(D, QK)
        r.wide[:, :, :, j * QKW : (j + 1) * QKW] = nn(full, hots).astype(BF).reshape(2, 4, 96, QKW)
    q_add = jnp.dot(r.qvb[0], hots32, precision=lax.Precision.HIGHEST)
    v_add = jnp.dot(r.qvb[1], hots32, precision=lax.Precision.HIGHEST)
    arrived(to_sib)

    @pl.loop(0, 4)
    def _(i):
        both = nn(r.xs[i].reshape(CTX_ROWS, D), r.wide[:, :, :, QKW:].reshape(D, 2 * QKW))
        mine = pl.ds(i * OWN_SEGS, OWN_SEGS)
        r.k[mine] = both[:, :QKW].astype(BF).reshape(OWN_SEGS, SEG, QKW)
        r.v[mine] = (both[:, QKW:] + v_add).astype(BF).reshape(OWN_SEGS, SEG, QKW)

    @pl.loop(0, 4)
    def _(i):
        wide_q = r.wide[:, :, :, :QKW].reshape(D, QKW)
        r.q[pl.ds(i * ROWS, ROWS), :] = (nn(r.xs[x, i], wide_q) + q_add).astype(BF)

    arrived(one_x)
    one_y = mail.ring(w1, *y_ring)
    arrived(two_z)
    two_x = mail.ring(w2, *x_ring)

    def climb(seg):
        r.trail[0] = seg
        depth = jnp.int32(0)
        here = seg
        for i in range(1, PATH):
            up = r.parents[0, here]
            found = up >= 0
            here = jnp.where(found, up, here)
            r.trail[i] = here
            depth = depth + found.astype(jnp.int32)
        return depth

    def on_path(depth, j):
        return r.trail[jnp.maximum(depth - j, 0)]

    def fetch_path(depth):
        for j in range(PATH):
            above = on_path(depth, j)
            r.kp[pl.ds(j * SEG, SEG), :] = r.k[above]
            r.vp[pl.ds(j * SEG, SEG), :] = r.v[above]

    arrived(tab_z2 + low_tab2 + to_low)

    def attend(a):
        depth = climb(x * OWN_SEGS + a)
        fetch_path(depth)
        mine = pl.ds(pl.multiple_of(a * SEG, SEG), SEG)
        tile = lax.rem(depth, 4) * 2
        for h in range(HEADS_DEV):
            head = slice(h * WIDE, (h + 1) * WIDE)
            low_q = r.q[mine, head] * jnp.asarray(SCALE, BF)
            flat = r.tab.at[h]
            pieces = [
                flat[lax.div(tile + i, 4), lax.rem(tile + i, 4)].astype(F32) for i in range(2)
            ]
            table = jnp.concatenate(pieces, axis=0)
            scores = nt(low_q, r.kp[:, head])
            parts = []
            for j in range(PATH):
                cols = slice((j % 4) * SEG, (j % 4 + 1) * SEG)
                score = scores[:, j * SEG : (j + 1) * SEG] + table[:, cols]
                parts.append(jnp.where(j <= depth, score, -1e30))
            scores = jnp.concatenate(parts, axis=1)
            peak = jnp.max(scores, axis=1, keepdims=True)
            raised = jnp.exp(scores - peak)
            whole = jnp.sum(raised, axis=1, keepdims=True)
            soft = (raised * (1.0 / whole)).astype(BF)
            r.p[a, h] = soft
            r.o_wide[mine, head] = nn(soft, r.vp[:, head]).astype(BF)

    pl.loop(0, 2)(attend)
    zero_z2 = mail.ring_on(w0, zero_z, *z_ring)
    pl.loop(2, 4)(attend)
    one_y2 = mail.ring_on(w1, one_y, *y_ring)
    two_x2 = mail.ring_on(w2, two_x, *x_ring)
    pl.loop(4, 5)(attend)
    r.o[...] = nt(r.o_wide[...], hots).astype(BF)
    o_far = [mail.post(r.o.at[pl.ds((1 - yh) * PAIR, PAIR)], r.o2.at[yh], far)]
    r.o2[yh] = r.o[pl.ds(yh * PAIR, PAIR), :]

    own, other = pl.ds(core * ROWS, ROWS), pl.ds((1 - core) * ROWS, ROWS)

    def trade_sum(slot):
        mail.done(mail.post(r.part.at[other], r.got.at[slot], sib))
        return r.part[own, :] + r.got[slot]

    def trade_rows(slot, values):
        r.rows[slot, own, :] = values
        arrived(mail.same(r.rows.at[slot, own], [sib]))

    def both_halves(left0, left1, weights):
        for half in range(2):
            cols = slice(half * 384, (half + 1) * 384)
            r.part[:, cols] = nt(left0, weights(0, half)) + nt(left1, weights(1, half))

    def tiles():
        return [(which, n) for which in range(2) for n in range(3)]

    def outer(which, half):
        return r.w[which, half, :, :, :D].reshape(384, D)

    def inner(which, half):
        return r.w[which, half, :, :, D:].reshape(384, D)

    arrived(o_y + o_far)
    both_halves(r.o2[0], r.o2[1], lambda a, b: r.wt[a, b, :, :, :QK].reshape(384, QK))
    n1, inv1 = normed(r.xs[x, tp].astype(F32) + trade_sum(0) + line(bo))
    r.n1s[...] = n1
    y1 = n1 * line(g1) + line(s1)
    r.y1s[...] = y1
    trade_rows(0, y1.astype(BF))
    arrived([*bias_far, *zero_z2, *one_y2, *two_x2])

    @pl.loop(0, 6)
    def _(i):
        which, col = lax.div(i, 3), pl.multiple_of(lax.rem(i, 3) * 256, 256)
        later = pl.multiple_of(col + D, 256)
        weight = r.w[which, :, :, :, pl.ds(later, 256)].reshape(D, 256)
        u = nn(r.rows[0], weight) + r.bias[which, :, pl.ds(col, 256)]
        phi = 0.5 * (1.0 + lax.erf(u * 0.7071067811865476))
        r.act[which, :, pl.ds(col, 256)] = (u * phi).astype(BF)
        slope = phi + u * (jnp.exp(-0.5 * u * u) * 0.3989422804014327)
        r.slope[pl.ds(pl.multiple_of(which * PAIR, PAIR), PAIR), pl.ds(col, 256)] = slope

    both_halves(r.act[0], r.act[1], outer)
    n2, inv2 = normed(r.y1s[...] + trade_sum(1) + line(bout))
    gain2 = line(g2)
    r.res[...] = (n2 * gain2 + line(s2)).astype(BF)
    c = r.cots[...].astype(F32)
    r.v_own[...] = jnp.zeros_like(r.v_own)
    r.v_own[4:5, :] = total(c * n2)
    r.v_own[5:6, :] = total(c)
    dh2 = normed_back(c, gain2, n2, inv2)
    r.dh2s[...] = dh2
    df = dh2.astype(BF)
    r.v_own[1:2, :] = total(df.astype(F32))
    trade_rows(1, df)

    @pl.loop(0, 6)
    def _(i):
        which, col = lax.div(i, 3), pl.multiple_of(lax.rem(i, 3) * 256, 256)
        weight = r.w[which, :, :, :, pl.ds(col, 256)].reshape(D, 256)
        slope = r.slope[pl.ds(pl.multiple_of(which * PAIR, PAIR), PAIR), pl.ds(col, 256)]
        grad = (nn(r.rows[1], weight) * slope).astype(BF)
        r.du[which, :, pl.ds(col, 256)] = grad
        r.v_own[pl.ds(6 + which, 1), pl.ds(col, 256)] = total(grad.astype(F32))

    mail.flush()
    both_halves(r.du[0], r.du[1], inner)
    c_dy = [mail.post(r.part.at[other], r.got.at[2], sib)]

    @pl.loop(0, 6)
    def _(i):
        which, col = lax.div(i, 3), pl.multiple_of(lax.rem(i, 3) * 256, 256)
        later = pl.multiple_of(col + D, 256)
        grad = tn(r.rows[1], r.act[which, :, pl.ds(col, 256)]).astype(BF)
        r.w[which, :, :, :, pl.ds(col, 256)] = grad.reshape(2, 4, 96, 256)
        grad = tn(r.rows[0], r.du[which, :, pl.ds(col, 256)]).astype(BF)
        r.w[which, :, :, :, pl.ds(later, 256)] = grad.reshape(2, 4, 96, 256)

    c0z = mail.fold(w0, r.r0z, *z_ring)
    c2x = mail.fold(w2, r.r2x, *x_ring)
    arrived(c_dy)
    dy1 = r.part[own, :] + r.got[2] + r.dh2s[...]
    n1 = r.n1s[...]
    r.v_own[2:3, :] = total(dy1 * n1)
    r.v_own[3:4, :] = total(dy1)
    dh1 = normed_back(dy1, line(g1), n1, inv1)
    r.dh1s[...] = dh1
    da = dh1.astype(BF)
    r.v_own[0:1, :] = total(da.astype(F32))
    trade_rows(2, da)
    leave = r.o.at[pl.ds(0, PAIR)]
    leave[...] = nn(r.rows[2], r.wt[1 - yh, :, :, :, :QK].reshape(D, QK)).astype(BF)
    back = [mail.post(leave, r.dout.at[pl.ds(yh * PAIR, PAIR)], far)]
    c1y = mail.fold(w1, r.r1y, *y_ring)
    r.dout[pl.ds(yh * PAIR, PAIR), :] = nn(r.rows[2], r.wt[yh, :, :, :, :QK].reshape(D, QK)).astype(BF)
    for which in range(2):
        grad = tn(r.rows[2], r.o2[which]).astype(BF)
        r.wt[which, :, :, :, :QK] = grad.reshape(2, 4, 96, QK)
    r.slope[...] = jnp.zeros_like(r.slope)
    r.tgp[...] = jnp.zeros_like(r.tgp)
    r.dtab[...] = jnp.zeros_like(r.dtab)
    for b in range(SEGS):
        r.depths[b] = climb(jnp.int32(b))
    arrived(back)
    coz = mail.spread(lambda k: r.wt.at[:, :, around(z, k)], r.roz, zp)

    def spot(h, b):
        n = h * SEGS + b
        return slice(n // 6 * 64, n // 6 * 64 + 64), slice(n % 6 * 128, n % 6 * 128 + 128)

    def attend_back(a, heads):
        depth = climb(x * OWN_SEGS + a)
        fetch_path(depth)
        mine = pl.ds(pl.multiple_of(a * SEG, SEG), SEG)
        tile = lax.rem(depth, 4)
        grads = nn(r.dout[mine, :], hots).astype(BF)
        for h in heads:
            head = slice(h * WIDE, (h + 1) * WIDE)
            low_q, grad = r.q[mine, head], grads[:, head]
            soft = r.p[a, h]
            inside = grad.astype(F32) * r.o_wide[mine, head].astype(F32)
            ds = soft.astype(F32) * (
                nt(grad, r.vp[:, head]) - jnp.sum(inside, axis=1, keepdims=True)
            )
            ds_low = ds.astype(BF)
            r.dq_wide[mine, head] = (nn(ds_low, r.kp[:, head]) * SCALE).astype(BF)
            q_t = (low_q.astype(F32).T[:HEAD_DIM] * SCALE).astype(BF)
            grad_t = grad.astype(F32).T[:HEAD_DIM].astype(BF)
            dk_part, dv_part = nn(q_t, ds_low), nn(grad_t, soft)
            for j in range(PATH):
                r.parts[0, j] = dk_part[:, j * SEG : (j + 1) * SEG]
                r.parts[1, j] = dv_part[:, j * SEG : (j + 1) * SEG]
            for b in range(SEGS):
                down = r.depths[b]
                held = (down <= depth) & (on_path(depth, down) == b)
                rows, cols = spot(h, b)
                r.slope[rows, cols] += jnp.where(held, r.parts[0, down], 0.0)
                r.tgp[rows, cols] += jnp.where(held, r.parts[1, down], 0.0)
            fall = ds_low.astype(F32)
            left = fall[:, 0:256] + fall[:, 512:768] + fall[:, 1024:1280]
            right = fall[:, 256:512] + fall[:, 768:1024]
            for t in range(4):
                span = slice(t * SEG, (t + 1) * SEG)
                r.dtab[h, span, 0:256] += jnp.where(tile == t, left, 0.0)
                r.dtab[h, span, 256:512] += jnp.where(tile == t, right, 0.0)

    def settle_heads(heads):
        for h in heads:
            for b in range(SEGS):
                rows, cols = spot(h, b)
                into = slice(b % 5 * SEG, (b % 5 + 1) * SEG)
                r.p[b // 5, h, 0:64, into] = r.slope[rows, cols].astype(BF)
                r.p[b // 5, h, 64:128, into] = r.tgp[rows, cols].astype(BF)
            r.tab[h] = r.dtab[h].astype(BF).reshape(2, 4, 64, DEPTHS)

    def dkv(first, count):
        def view(k, half):
            span = (pl.ds(half * 64, 64), pl.ds(0, CTX_ROWS))
            return r.p.at[around(x, k), pl.ds(first, count), *span]

        return view

    c0z = mail.fold_on(w0, r.r0z, c0z, *z_ring)
    c2x = mail.fold_on(w2, r.r2x, c2x, *x_ring)
    pl.loop(0, OWN_SEGS)(lambda a: attend_back(a, (0, 1)))
    settle_heads((0, 1))
    c_dka = mail.fold(dkv(0, 2), r.r_dka, *x_ring)
    d0z = mail.spread(lambda k: r.tab.at[0, :, around(z, k)], r.t0z, zp)
    d1y = mail.post(r.tab.at[1, 1 - yl], r.t1y, low)
    pl.loop(0, OWN_SEGS)(lambda a: attend_back(a, (2,)))
    settle_heads((2,))
    c_dkb = mail.fold(dkv(2, 1), r.r_dkb, *x_ring)
    d2y = mail.post(r.tab.at[2, 1 - yl], r.t2y, low)

    def weight_of(j):
        return r.ws[:, j].reshape(D, QK)

    def quarter(a, b):
        return pl.ds((a * 2 + b) * ROWS, ROWS)

    late = []

    def settle(ref, base, values):
        ref[:, lanes(base, 0)] = values.astype(BF)
        late.extend(mail.same(ref.at[:, lanes(base, 0)], xp))

    q_low = nt(r.dq_wide[...], hots).astype(BF)
    grad = tn(r.xs[x].reshape(CTX_ROWS, D), q_low).astype(BF)
    r.wide[:, :, :, 0:QK] = grad.reshape(2, 4, 96, QK)
    for i in range(4):
        both = r.p[i, :, :, 0:CTX_ROWS].reshape(2 * QK, CTX_ROWS)
        term = nn(both, r.xs[i].reshape(CTX_ROWS, D))
        r.kv_t[...] = term if i == 0 else r.kv_t[...] + term
    r.wide[:, :, :, QKP : QKP + QKW] = r.kv_t[...].T.astype(BF).reshape(2, 4, 96, QKW)
    cqz = mail.spread(lambda k: r.wide.at[:, around(z, k), :, pl.ds(0, QKV)], r.rqz, zp)
    r.v_own[pl.ds(8 + yh, 1), 0:QK] = total(q_low.astype(F32))
    ones = jnp.ones((8, CTX_ROWS), BF)
    sums = [nt(ones, r.p[i, :, 64:128, 0:CTX_ROWS].reshape(QK, CTX_ROWS)) for i in range(4)]
    r.v_own[pl.ds(10 + yh, 1), 0:QK] = (sums[0] + sums[1] + sums[2] + sums[3])[0:1]
    c_dka = mail.fold_on(dkv(0, 2), r.r_dka, c_dka, *x_ring)
    r.vx[x] = r.v_own[...]
    c_vx = mail.same(r.vx.at[x], xp)
    c1y = mail.fold_on(w1, r.r1y, c1y, *y_ring)
    arrived(c0z)
    for half in range(2):
        r.s0z[half : half + 1] = folded(w0, r.r0z, half).astype(BF)
    c0y = mail.spread(lambda k: r.s0z.at[ys[k][0], ys[k][1]], r.r0y, yp)
    arrived(c2x)
    for half in range(2):
        r.s2x[half : half + 1] = folded(w2, r.r2x, half).astype(BF)
    c2z = mail.spread(lambda k: r.s2x.at[:, :, around(z, k)], r.r2z, zp)
    arrived(coz)
    r.soz[...] = added(r.wt[:, :, z], r.roz).astype(BF)
    coy = mail.spread(lambda k: r.soz.at[ys[k][0], ys[k][1]], r.roy, yp)
    arrived(d0z)
    r.u0z[...] = added(r.tab[0, :, z], r.t0z).astype(BF)
    d0y = mail.post(r.u0z.at[1 - yl], r.t0y, low)
    arrived([d1y])
    r.u1y[...] = (r.tab[1, yl].astype(F32) + r.t1y[...].astype(F32)).astype(BF)
    d1x = mail.spread(lambda k: r.u1y.at[:, :, lanes(0, k)], r.t1x, xp)
    r.tgp[...] = nt(q_low, weight_of(0))
    c_dkb = mail.fold_on(dkv(2, 1), r.r_dkb, c_dkb, *x_ring)
    arrived(c_vx)
    r.vz[z] = slots_total(r.vx)
    c_vz = mail.same(r.vz.at[z], zp)
    arrived([d2y])
    r.u2y[...] = (r.tab[2, yl].astype(F32) + r.t2y[...].astype(F32)).astype(BF)
    d2z = mail.spread(lambda k: r.u2y.at[around(z, k)], r.t2z, zp)
    arrived(c1y)
    for half in range(2):
        r.s1y[half * 2 : half * 2 + 2] = folded(w1, r.r1y, half).astype(BF)
    c1x = mail.spread(lambda k: r.s1y.at[:, :, lanes(0, k)], r.r1x, xp)

    arrived(c_dka + c_dkb)
    k_low, v_low = (
        jnp.concatenate(
            [
                folded(dkv(0, 2), r.r_dka, half).reshape(2 * 64, CTX_ROWS),
                folded(dkv(2, 1), r.r_dkb, half).reshape(64, CTX_ROWS),
            ],
            axis=0,
        ).T.astype(BF)
        for half in range(2)
    )
    r.tgp[...] += nt(k_low, weight_of(1)) + nt(v_low, weight_of(2))
    c_sib = [mail.post(r.tgp.at[quarter(a, 1 - core)], r.got.at[a], sib) for a in range(2)]
    arrived(coy)
    r.rox[x] = added(r.soz[yh, yl], r.roy).astype(BF)
    cox = mail.same(r.rox.at[x], xp)
    arrived(c0y)
    r.s0y[...] = added(r.s0z[yh, yl], r.r0y).astype(BF)
    c0x = mail.spread(lambda k: r.s0y.at[:, lanes(0, k)], r.r0x, xp)
    arrived([d0y])
    r.u0y[...] = (r.u0z[yl].astype(F32) + r.t0y[...].astype(F32)).astype(BF)
    d0x = mail.spread(lambda k: r.u0y.at[:, lanes(0, k)], r.t0x, xp)
    arrived(c_sib)
    s_far = r.rows.at[0, pl.ds(0, ROWS)]
    s_far[...] = (r.tgp[quarter(1 - yh, core), :] + r.got[1 - yh]).astype(BF)
    c_far = [mail.post(s_far, r.r_far, far)]

    arrived(cqz)
    r.sqz[...] = added(r.wide[:, z, :, 0:QKV], r.rqz).astype(BF)
    cqy = mail.post(r.sqz.at[1 - yl], r.rqy, low)
    arrived(d1x)
    r.u1x[...] = added(r.u1y[:, :, lanes(0, 0)], r.t1x).astype(BF)
    d1z = mail.spread(lambda k: r.u1x.at[around(z, k)], r.t1z, zp)
    arrived(c2z)
    r.s2z[...] = added(r.s2x[:, :, z], r.r2z).astype(BF)
    c2y = mail.spread(lambda k: r.s2z.at[ys[k][0], ys[k][1]], r.r2y, yp)
    arrived(c_vz)
    r.vy[y] = slots_total(r.vz)
    c_vy = mail.same(r.vy.at[y], yp)
    arrived(c1x)
    r.s1x[...] = added(r.s1y[:, :, lanes(0, 0)], r.r1x).astype(BF)
    c1z = mail.spread(lambda k: r.s1x.at[around(z, k)], r.r1z, zp)
    arrived(d2z)
    r.u2z[...] = added(r.u2y[z], r.t2z).astype(BF)
    d2x = mail.spread(lambda k: r.u2z.at[:, lanes(0, k)], r.t2x, xp)
    arrived(c0x)
    settle(r.f, 0, added(r.s0y[:, lanes(0, 0)], r.r0x))
    arrived(d0x)
    settle(r.ft.at[0], 0, added(r.u0y[:, lanes(0, 0)], r.t0x))
    arrived([cqy])
    r.rqx[x] = (r.sqz[yl].astype(F32) + r.rqy[...].astype(F32)).astype(BF)
    cqx = mail.same(r.rqx.at[x], xp)

    arrived(d1z)
    settle(r.ft.at[1], 0, added(r.u1x[z], r.t1z))
    arrived(c2y)
    settle(r.f, 1024, added(r.s2z[yh, yl], r.r2y))
    arrived(c1z)
    settle(r.f, 512, added(r.s1x[z], r.r1z))
    arrived(d2x)
    settle(r.ft.at[2], 0, added(r.u2z[:, lanes(0, 0)], r.t2x))
    arrived(c_vy)
    r.vc[0] = slots_total(r.vy)
    c_vc = mail.post(r.vc.at[0], r.vc.at[1], sib)
    arrived(cox)
    r.fo[...] = slots_total(r.rox)
    arrived(c_far)
    r.tg[...] = r.tgp[quarter(yh, core), :] + r.got[yh] + r.r_far[...].astype(F32) + r.dh1s[...]
    arrived(cqx)
    r.fq[...] = slots_total(r.rqx)
    arrived([c_vc])
    r.vsum[...] = r.vc[0]
    r.vsum[0:6, :] = r.vc[0, 0:6, :] + r.vc[1, 0:6, :]
    arrived(late)
    mail.flush()
    assert mail.used <= POSTS


def layer(*arrays):
    vm = pl.BlockSpec(memory_space=pltpu.VMEM)
    hbm = pl.BlockSpec(memory_space=pltpu.HBM)
    return pl.pallas_call(
        layer_kernel,
        out_shape=tuple(jax.ShapeDtypeStruct(*entry) for entry in OUTPUTS.values()),
        in_specs=[pl.BlockSpec(memory_space=pltpu.SMEM)] + [hbm] * (len(INPUTS) - 1),
        out_specs=[vm] * len(OUTPUTS),
        scratch_shapes=[
            *(pltpu.VMEM(*entry) for entry in SCRATCH.values()),
            pltpu.SMEM((PATH,), jnp.int32),
            pltpu.SMEM((SEGS,), jnp.int32),
            pltpu.SemaphoreType.DMA((20,)),
            pltpu.SemaphoreType.DMA((POSTS,)),
            pltpu.SemaphoreType.DMA((POSTS,)),
        ],
        compiler_params=pltpu.CompilerParams(
            collective_id=1, has_side_effects=True, vmem_limit_bytes=60 * MIB
        ),
        name="layer",
    )(*arrays)


def finish_kernel(*refs):
    f_in, fo_in, fq_in, ft_in, tg, vsum_in, res, logits_in, noise_in = refs[:9]
    res_out, tg_out, gwq, gwk, gwv, gwo, gwi, gwout_t, mask, gbq, gbv, *lines = refs[9:-8]
    f, fo, fq, ft, vsum, logits, noise, sem = refs[-8:]
    pairs = [
        (res, res_out),
        (tg, tg_out),
        (f_in, f),
        (fo_in, fo),
        (fq_in, fq),
        (ft_in, ft),
        (vsum_in, vsum),
        (logits_in, logits),
        (noise_in, noise),
    ]
    copies = [pltpu.make_async_copy(src, dst, sem.at[n]) for n, (src, dst) in enumerate(pairs)]
    for copy in copies:
        copy.start()
    for copy in copies[2:]:
        copy.wait()
    gwq[...] = fq[:, :QK]
    rows = lax.broadcasted_iota(jnp.int32, (QKW, QK), 0)
    cols = lax.broadcasted_iota(jnp.int32, (QKW, QK), 1)
    wanted = cols // HEAD_DIM * WIDE + cols % HEAD_DIM
    for out, shift in ((gwk, 0), (gwv, HEAD_DIM)):
        pick = (rows == wanted + shift).astype(F32)
        out[...] = jnp.dot(fq[:, QKP:], pick, precision=lax.Precision.HIGHEST)
    gwo[...] = fo[...].T[:QK]
    gwout_t[...] = f[:, :D].astype(F32)
    gwi[...] = f[:, D:].astype(F32)
    mask[...] = ft[...].astype(F32) * jax.nn.sigmoid(-(logits[...] + noise[...]))
    yh = lax.div(lax.axis_index("tp"), 2)
    gbq[...] = vsum[pl.ds(8 + yh, 1), 0:QK]
    gbv[...] = vsum[pl.ds(10 + yh, 1), 0:QK]
    for n, out in enumerate(lines):
        row = vsum[pl.ds(6 + yh, 1), :] if n == 6 else vsum[n : n + 1, :]
        for i in range(6):
            out[i : i + 1, :] = row[:, i * 128 : (i + 1) * 128]
    for copy in copies[:2]:
        copy.wait()


def finish(f, fo, fq, ft, tg, vsum, res, logits, noise):
    shape = jax.ShapeDtypeStruct
    vm = pl.BlockSpec(memory_space=pltpu.VMEM)
    hbm = pl.BlockSpec(memory_space=pltpu.HBM)
    outs = (
        shape((ROWS, D), BF),
        shape((ROWS, D), F32),
        shape((96, QK), F32),
        shape((96, QK), F32),
        shape((96, QK), F32),
        shape((QK, 96), F32),
        shape((96, D), F32),
        shape((96, D), F32),
        shape((HEADS_DEV, 64, DEPTHS), F32),
        shape((1, QK), F32),
        shape((1, QK), F32),
        *[shape((6, 128), F32)] * 7,
    )
    held = (f, fo, fq, ft, vsum, logits, noise)
    return pl.pallas_call(
        finish_kernel,
        out_shape=outs,
        in_specs=[hbm] * 9,
        out_specs=[vm] * len(outs),
        scratch_shapes=[
            *(pltpu.VMEM(entry.shape, entry.dtype) for entry in held),
            pltpu.SemaphoreType.DMA((9,)),
        ],
        compiler_params=pltpu.CompilerParams(vmem_limit_bytes=60 * MIB),
        name="finish",
    )(f, fo, fq, ft, tg, vsum, res, logits, noise)


def shards(
    tokens,
    parents,
    query_weight,
    query_bias,
    key_weight,
    value_weight,
    value_bias,
    output_weight,
    output_bias,
    first_gain,
    first_shift,
    inner_weight,
    inner_bias,
    outer_weight,
    outer_bias,
    second_gain,
    second_shift,
    mask_logits,
    mask_noise,
    cotangent,
):
    def lined(vector):
        return vector.reshape(6, 128)

    res, tg, f, fo, fq, ft, vsum = layer(
        parents,
        tokens,
        cotangent,
        query_weight,
        key_weight,
        value_weight,
        query_bias.reshape(1, QK),
        value_bias.reshape(1, QK),
        mask_logits,
        mask_noise,
        output_weight,
        inner_weight,
        outer_weight.T,
        lined(output_bias),
        lined(first_gain),
        lined(first_shift),
        lined(inner_bias),
        lined(outer_bias),
        lined(second_gain),
        lined(second_shift),
    )
    result, tg, gwq, gwk, gwv, gwo, gwi, gwout_t, mask, gbq, gbv, *lines = finish(
        f, fo, fq, ft, tg, vsum, res, mask_logits, mask_noise
    )
    bo, bout, g1, s1, g2, s2, bi = [entry.reshape(D) for entry in lines]
    return (
        result,
        tg,
        gwq,
        gbq.reshape(QK),
        gwk,
        gwv,
        gbv.reshape(QK),
        gwo,
        bo,
        g1,
        s1,
        gwi,
        bi,
        gwout_t.T,
        bout,
        g2,
        s2,
        mask,
    )


def solution(mesh):
    in_specs = (
        P(("shard", "ctx", "tp"), None),
        P("shard", None),
        P("shard", "tp"),
        P("tp"),
        P("shard", "tp"),
        P("shard", "tp"),
        P("tp"),
        P("tp", "shard"),
        P(),
        P(),
        P(),
        P("shard", "tp"),
        P("tp"),
        P("tp", "shard"),
        P(),
        P(),
        P(),
        P("tp", "shard", None),
        P("tp", "shard", None),
        P(("shard", "ctx", "tp"), None),
    )
    out_specs = (
        P(("shard", "ctx", "tp"), None),
        P(("shard", "ctx", "tp"), None),
        P("shard", "tp"),
        P("tp"),
        P("shard", "tp"),
        P("shard", "tp"),
        P("tp"),
        P("tp", "shard"),
        P(),
        P(),
        P(),
        P("shard", "tp"),
        P("tp"),
        P("tp", "shard"),
        P(),
        P(),
        P(),
        P("tp", "shard", None),
    )
    return jax.shard_map(shards, mesh=mesh, in_specs=in_specs, out_specs=out_specs, check_vma=False)
```
